256 devices in a mesh: segment: 8 (over x, core), slab: 32 (over y, z).
Axes of the slice: x: 4, y: 4, z: 8, core: 2. Of those that a mesh axis runs over, the one named last changes fastest.
Arguments:
- fwd_input: bfloat16 [8, 192, 64, 128], P('segment', None, 'slab'), may hold values from -90 to 90
- fwd_skip: bfloat16 [8, 192, 64, 128], P('segment', None, 'slab'), may hold values from -6 to 6
- bwd_input: bfloat16 [8, 192, 64, 128], P('segment', None, 'slab'), may hold values from -90 to 90
- bwd_skip: bfloat16 [8, 192, 64, 128], P('segment', None, 'slab'), may hold values from -6 to 6
- out_cot: bfloat16 [8, 192, 64, 128], P('segment', None, 'slab'), may hold values from -6 to 6
- skip_cot: bfloat16 [8, 192, 64, 128], P('segment', None, 'slab'), may hold values from -6 to 6
- kernel: bfloat16 [8, 192, 5184], P('segment'), may hold values from -0.078125 to 0.078125
- norm_gain: float32 [8, 192], P('segment'), may hold values from 0.1 to 1.9
- norm_shift: float32 [8, 192], P('segment'), may hold values from -0.5 to 0.5
- head_weight: bfloat16 [192, 105], replicated, may hold values from -2.8867513 to 2.8867513
- labels: int32 [64, 128], P('slab'), may hold values from 0 to 104
Outputs:
- next_input: bfloat16 [8, 192, 64, 128], P('segment', None, 'slab')
- next_cot: bfloat16 [8, 192, 64, 128], P('segment', None, 'slab')
- skip_store: bfloat16 [8, 192, 64, 128], P('segment', None, 'slab')
- kernel_grad: float32 [8, 192, 5184], P('segment', 'slab')
- gain_grad: float32 [8, 192], P('segment')
- shift_grad: float32 [8, 192], P('segment')
The draws below stay inside these ranges and needn't reach their ends.
All inputs are finite; a program needn't handle non-finite values.
Results may differ from the reference program's by a relative error of at most 0.038.
Values may be sent and summed in bfloat16 or wider, within the bound.
No kernel may reach another device: no remote copies, remote signals or barrier semaphores. Data moves between devices by JAX's collectives and lax.ppermute only.
A program may use at most 64 MiB of HBM per device.

```python
import math
import jax
import jax.numpy as jnp
import numpy as np
from jax import lax

C = 192
CLASSES = 105
ROWS = 8
COLS = 16
SECTIONS = 8
DEPTH = 64
AREA = 128


def shape_volume(key, noise_base, cell_low, cell_high):
    chan_key, cell_key, offset_key = jax.random.split(key, 3)
    offsets = jnp.clip(jax.random.normal(offset_key, (SECTIONS, C, 1, 1), jnp.float32), -2.5, 2.5)
    chan_scale = jnp.exp(jax.random.uniform(chan_key, (SECTIONS, C, 1, 1), jnp.float32, math.log(0.5), math.log(2.0)))
    cell_scale = jnp.exp(jax.random.uniform(cell_key, (SECTIONS, 1, DEPTH, AREA), jnp.float32, math.log(cell_low), math.log(cell_high)))
    depth_frac = jnp.arange(DEPTH, dtype=jnp.float32) / max(DEPTH - 1, 1)
    depth_ramp = (0.6 * (1.0 + 2.0 * depth_frac))[None, None, :, None]
    return ((noise_base + offsets) * chan_scale * cell_scale * depth_ramp).astype(jnp.bfloat16)


def draw_fwd_input(key, part):
    key = jax.random.fold_in(key, 11)
    noise_key, shape_key = jax.random.split(key)
    noise_base = jnp.clip(jax.random.normal(noise_key, (SECTIONS, C, DEPTH, AREA), jnp.float32), -5.0, 5.0)
    return shape_volume(shape_key, noise_base, 0.3, 3.0)


def draw_bwd_input(key, part):
    key = jax.random.fold_in(key, 13)
    noise_key, shape_key = jax.random.split(key)
    noise_base = jnp.clip(jax.random.normal(noise_key, (SECTIONS, C, DEPTH, AREA), jnp.float32), -5.0, 5.0)
    return shape_volume(shape_key, noise_base, 0.3, 3.0)


def draw_head_weight(key, part):
    key = jax.random.fold_in(key, 23)
    values = jnp.clip(jax.random.normal(key, (C, CLASSES), jnp.float32), -5.0, 5.0) * (3.0 / math.sqrt(C))
    return values.astype(jnp.bfloat16)


def touch_ends(entries, key, smallest, high):
    spot = [jax.random.randint(jax.random.fold_in(key, axis), (), 0, length) for axis, length in enumerate(entries.shape)]
    longest = entries.shape.index(max(entries.shape))
    neighbour = spot[:longest] + [(spot[longest] + 1) % entries.shape[longest]] + spot[longest + 1:]
    return entries.at[tuple(spot)].set(smallest).at[tuple(neighbour)].set(high)


def block_scale(stream_key, dims, cuts, smallest, largest):
    gain, own = 1.0, jax.random.fold_in(stream_key, 6)
    for axis_at, parts in cuts:
        draws = jnp.exp(jax.random.uniform(jax.random.fold_in(own, axis_at), (parts,), jnp.float32, smallest / len(cuts), largest / len(cuts)))
        gain = gain * jnp.repeat(draws, dims[axis_at] // parts).reshape([-1 if axis == axis_at else 1 for axis in range(len(dims))])
    return gain


def rank_bounds(number_of, skew):
    weights = [(1 << 20) // math.isqrt(standing ** skew) + 1 for standing in range(1, number_of + 1)]
    deviation = 1 + sum(weights) // (1 << 30)
    return np.cumsum(np.array([max(1, weight // deviation) for weight in weights]))


def ranked_ids(stream_key, extent, number_of, slope):
    listing = rank_bounds(number_of, slope)
    lot = jax.random.randint(jax.random.fold_in(stream_key, 1), extent, 0, int(listing[number_of - 1]))
    rank = jnp.searchsorted(jnp.asarray(listing, jnp.int32), lot, side="right")
    return jax.random.permutation(jax.random.fold_in(stream_key, 2), number_of)[rank].astype(jnp.int32)


def centred(rng, dims, scale, bound, cuts=(), kind=jnp.bfloat16):
    values = jax.random.normal(rng, dims, jnp.float32) * scale
    if len(cuts) > 0:
        values = block_scale(rng, dims, cuts, -0.22, 0.18) * values
    return jnp.clip(values, min=-bound, max=bound).astype(kind)


def setup_inputs(seed: int = 0) -> dict:
    key_list = jax.random.split(jax.random.key(seed), 12)
    return {
        "fwd_input": draw_fwd_input(jax.random.fold_in(key_list[11], 71), 0),
        "fwd_skip": centred(key_list[1], (SECTIONS, C, DEPTH, AREA), 1.0, 6.0, ((0, 8), (2, 32))),
        "bwd_input": draw_bwd_input(jax.random.fold_in(key_list[11], 71), 0),
        "bwd_skip": centred(key_list[3], (SECTIONS, C, DEPTH, AREA), 1.0, 6.0, ((0, 8), (2, 32))),
        "out_cot": centred(key_list[4], (SECTIONS, C, DEPTH, AREA), 1.0, 6.0, ((0, 8), (2, 32))),
        "skip_cot": centred(key_list[5], (SECTIONS, C, DEPTH, AREA), 1.0, 6.0, ((0, 8), (2, 32))),
        "kernel": centred(key_list[6], (SECTIONS, C, 27 * C), (27 * C) ** -0.5, 0.078125, ((0, 8),)),
        "norm_gain": jnp.clip(1.0 + 0.18 * jax.random.normal(key_list[7], (SECTIONS, C), jnp.float32), 0.1, 1.9),
        "norm_shift": jnp.clip(jax.random.uniform(key_list[8], (SECTIONS, C), jnp.float32, -0.5, 0.5) * block_scale(key_list[8], (SECTIONS, C), ((0, 8),), -0.4, 0.0), -0.5, 0.5),
        "head_weight": draw_head_weight(jax.random.fold_in(key_list[11], 71), 0),
        "labels": touch_ends(ranked_ids(key_list[10], (DEPTH, AREA), CLASSES, 2), jax.random.fold_in(key_list[10], 3), 0, CLASSES - 1).astype(jnp.int32),
    }


epsilon = 1e-05
leak_slope = 0.01

def rim_pad(volume):
    grid = volume.reshape(volume.shape[0], volume.shape[1], ROWS, COLS)
    return jnp.pad(grid, ((0, 0), (1, 1), (1, 1), (1, 1)))

def tap_views(padded, planes, mirror):
    tap_list = []
    for plane_off in range(3):
        for row_off in range(3):
            for col_off in range(3):
                if mirror:
                    offsets = (2 - plane_off, 2 - row_off, 2 - col_off)
                else:
                    offsets = (plane_off, row_off, col_off)
                window = padded[:, offsets[0]:offsets[0] + planes, offsets[1]:offsets[1] + ROWS, offsets[2]:offsets[2] + COLS]
                tap_list.append(window.reshape(padded.shape[0], planes * ROWS * COLS))
    return tap_list

def convolve(tap_list, kernel_mat):
    channels = kernel_mat.shape[0]
    summed = jnp.zeros((channels, tap_list[0].shape[1]), jnp.float32)
    for tap_index in range(27):
        weight = kernel_mat[:, tap_index * channels:(tap_index + 1) * channels]
        summed = summed + jnp.dot(weight.T, tap_list[tap_index], preferred_element_type=jnp.float32)
    return summed

def convolve_back(tap_list, kernel_mat):
    channels = kernel_mat.shape[0]
    summed = jnp.zeros((channels, tap_list[0].shape[1]), jnp.float32)
    for tap_index in range(27):
        weight = kernel_mat[:, tap_index * channels:(tap_index + 1) * channels]
        summed = summed + jnp.dot(weight, tap_list[tap_index], preferred_element_type=jnp.float32)
    return summed

def section_forward(joined, kernel_mat, gain_vec, shift_vec):
    tap_list = tap_views(rim_pad(joined), DEPTH, False)
    conv_out = convolve(tap_list, kernel_mat)
    center = lax.optimization_barrier(jnp.mean(conv_out, axis=1))
    spread = lax.optimization_barrier(jnp.mean(jnp.square(conv_out - center[:, None]), axis=1))
    inv_std = lax.rsqrt(spread + epsilon)
    normed = (conv_out - center[:, None]) * inv_std[:, None]
    scaled = normed * gain_vec[:, None] + shift_vec[:, None]
    activated = jnp.where(scaled > 0, scaled, leak_slope * scaled)
    output = (joined.reshape(conv_out.shape).astype(jnp.float32) + activated).astype(jnp.bfloat16)
    return (output, tap_list, normed, scaled, inv_std)

def one_segment(packed, head_weight, labels):
    segment_id, fwd_input, fwd_skip, bwd_input, bwd_skip, out_cot, skip_cot, kernel_mat, gain_vec, shift_vec = packed
    is_decoder = segment_id * 2 >= SECTIONS
    is_last = segment_id == SECTIONS - 1
    channels = kernel_mat.shape[0]
    joined_fwd = jnp.where(is_decoder, (fwd_input.astype(jnp.float32) + fwd_skip.astype(jnp.float32)).astype(jnp.bfloat16), fwd_input)
    joined_bwd = jnp.where(is_decoder, (bwd_input.astype(jnp.float32) + bwd_skip.astype(jnp.float32)).astype(jnp.bfloat16), bwd_input)
    fwd_out = section_forward(joined_fwd, kernel_mat, gain_vec, shift_vec)[0]
    bwd_out, tap_list, normed, scaled, inv_std = section_forward(joined_bwd, kernel_mat, gain_vec, shift_vec)
    logits = jnp.dot(head_weight.T, bwd_out, preferred_element_type=jnp.float32)
    class_prob = jax.nn.softmax(logits, axis=0)
    one_hot = (jnp.arange(head_weight.shape[1], dtype=jnp.int32)[:, None] == labels.reshape(1, -1)).astype(jnp.float32)
    head_delta = (class_prob - one_hot).astype(jnp.bfloat16)
    head_cot = jnp.dot(head_weight, head_delta, preferred_element_type=jnp.float32)
    cot_plain = out_cot.reshape(channels, -1).astype(jnp.float32)
    skip_plain = skip_cot.reshape(channels, -1).astype(jnp.float32)
    upstream = jnp.where(is_last, head_cot, cot_plain) + jnp.where(is_decoder, jnp.zeros_like(skip_plain), skip_plain)
    grad_act = upstream * jnp.where(scaled > 0, 1.0, leak_slope)
    sum_grad = lax.optimization_barrier(jnp.sum(grad_act, axis=1))
    sum_cross = lax.optimization_barrier(jnp.sum(grad_act * normed, axis=1))
    total_cells = float(DEPTH * AREA)
    grad_z = (gain_vec[:, None] * inv_std[:, None] * (grad_act - sum_grad[:, None] / total_cells - normed * sum_cross[:, None] / total_cells)).astype(jnp.bfloat16)
    blocks = []
    for tap_index in range(27):
        blocks.append(lax.dot_general(tap_list[tap_index], grad_z, (((1,), (1,)), ((), ())), preferred_element_type=jnp.float32))
    kernel_full = jnp.concatenate(blocks, axis=1)
    back_taps = tap_views(rim_pad(grad_z.reshape(channels, DEPTH, AREA)), DEPTH, True)
    grad_joined = (upstream + convolve_back(back_taps, kernel_mat)).astype(jnp.bfloat16)
    return (fwd_out, grad_joined, kernel_full, sum_cross, sum_grad)

def reference(fwd_input, fwd_skip, bwd_input, bwd_skip, out_cot, skip_cot, kernel, norm_gain, norm_shift, head_weight, labels):
    segment_ids = jnp.arange(SECTIONS, dtype=jnp.int32)

    def run_segment(packed):
        return one_segment(packed, head_weight, labels)
    fwd_out, grad_joined, kernel_full, sum_cross, sum_grad = lax.map(run_segment, (segment_ids, fwd_input, fwd_skip, bwd_input, bwd_skip, out_cot, skip_cot, kernel, norm_gain, norm_shift))
    scale_out = float(DEPTH * AREA) ** (-0.5)
    fwd_out = fwd_out.reshape(SECTIONS, C, DEPTH, AREA)
    grad_joined = grad_joined.reshape(SECTIONS, C, DEPTH, AREA)
    next_input = jnp.roll(fwd_out, 1, axis=0)
    next_cot = jnp.roll(grad_joined, -1, axis=0)
    decoder_mask = (segment_ids * 2 >= SECTIONS)[:, None, None, None]
    skip_store = jnp.where(decoder_mask, fwd_out[::-1], grad_joined[::-1])
    return (next_input, next_cot, skip_store, kernel_full * scale_out, sum_cross * scale_out, sum_grad * scale_out)
```

```python
import jax
import jax.numpy as jnp
from jax import lax
from jax.experimental import pallas as pl
from jax.experimental.pallas import tpu as pltpu
from jax.sharding import Mesh
from jax.sharding import PartitionSpec as P

ROWS = 8
COLS = 16
AREA = ROWS * COLS
TAPS = 27
SLABS = ("y", "z")

epsilon = 1e-05
leak_slope = 0.01

F32 = jnp.float32
BF16 = jnp.bfloat16
VMEM = pl.BlockSpec(memory_space=pltpu.VMEM)
SMEM = pl.BlockSpec(memory_space=pltpu.SMEM)


def call(body, outs, scratch, flops, moved, *args, smem=0):
    specs = [SMEM] * smem + [VMEM] * (len(args) - smem)
    shapes = [jax.ShapeDtypeStruct(shape, kind) for shape, kind in outs]
    return pl.pallas_call(
        body,
        out_shape=shapes,
        in_specs=specs,
        out_specs=[VMEM] * len(outs),
        scratch_shapes=[pltpu.VMEM(shape, kind) for shape, kind in scratch],
        compiler_params=pltpu.CompilerParams(vmem_limit_bytes=40 * 1024 * 1024),
        cost_estimate=pl.CostEstimate(flops=flops, bytes_accessed=moved, transcendentals=0),
        name=body.__name__,
    )(*args)


def tap_masks():
    cell = lax.broadcasted_iota(jnp.int32, (1, AREA), 1)
    row = cell // COLS
    col = cell % COLS
    masks = {}
    for b in range(3):
        for c in range(3):
            inside = None
            if b != 1:
                inside = row > 0 if b == 0 else row < ROWS - 1
            if c != 1:
                part = col > 0 if c == 0 else col < COLS - 1
                inside = part if inside is None else jnp.logical_and(inside, part)
            masks[(b, c)] = inside
    return masks


def shifted(plane, b, c, masks):
    step = (b - 1) * COLS + (c - 1)
    if step == 0:
        return plane
    moved = pltpu.roll(plane, (-step) % AREA, 1)
    return jnp.where(masks[(b, c)], moved, 0.0)


def columns(tile, row):
    square = jnp.concatenate([tile, jnp.zeros((AREA - 8, AREA), F32)], axis=0).T
    return jnp.concatenate([square[:, row : row + 1], square[:64, row + 1 : row + 2]], axis=0)


def packed_tile(cols):
    lane = lax.broadcasted_iota(jnp.int32, (AREA, AREA), 1)
    square = jnp.zeros((AREA, AREA), F32)
    for index, col in enumerate(cols):
        high = jnp.concatenate([col[128:], jnp.zeros((64, 1), F32)], axis=0)
        square = jnp.where(lane == 2 * index, col[:128], square)
        square = jnp.where(lane == 2 * index + 1, high, square)
    return square.T[:8]


def spread_sums(received, row, cells, peers):
    total = jnp.sum(received, axis=0)
    mean = total / peers
    apart = jnp.sum(jnp.square(received - mean[None]), axis=0)
    return columns(mean, row), columns(total, row + 2) + cells * columns(apart, row)


def local_stats(planes_out, cells):
    mean = sum(jnp.sum(p, axis=1, keepdims=True) for p in planes_out) / cells
    squares = sum(jnp.sum(jnp.square(p - mean), axis=1, keepdims=True) for p in planes_out)
    return mean, squares


def turn_weights(w_ref, out_ref):
    for pair in range(14):
        width = 384 if pair < 13 else 192
        block = w_ref[:, pair * 384 : pair * 384 + width].T
        if width == 384:
            block = jnp.concatenate([block[:192], block[192:]], axis=1)
        out_ref[:, pair * 384 : pair * 384 + width] = block


def fill_taps(planes, outputs, x_ref, masks, channels):
    for q, plane in enumerate(planes):
        wide = plane.astype(F32)
        for b in range(3):
            for c in range(3):
                view = shifted(wide, b, c, masks).astype(BF16)
                for a in range(3):
                    j = q - a
                    if 0 <= j < outputs:
                        tap = 9 * a + 3 * b + c
                        x_ref[
                            tap * channels : (tap + 1) * channels, j * AREA : (j + 1) * AREA
                        ] = view


def conv_bwd(own_ref, low_ref, high_ref, wt_ref, z_ref, send_ref, x_ref):
    masks = tap_masks()
    planes = [low_ref[0], low_ref[1], own_ref[0], own_ref[1], high_ref[0], high_ref[1]]
    fill_taps(planes, 4, x_ref, masks, 192)
    z = jnp.dot(wt_ref[...], x_ref[...], preferred_element_type=F32)
    for j in range(4):
        z_ref[j] = z[:, j * AREA : (j + 1) * AREA]
    mean, squares = local_stats([z[:, AREA : 2 * AREA], z[:, 2 * AREA : 3 * AREA]], 2.0 * AREA)
    tile = packed_tile([mean, squares])
    send_ref[...] = jnp.broadcast_to(tile[None], send_ref.shape)


def conv_fwd(own_ref, low_ref, high_ref, wt_ref, z_ref, tile_ref, x_ref):
    masks = tap_masks()
    planes = [low_ref[0], own_ref[0], own_ref[1], high_ref[0]]
    fill_taps(planes, 2, x_ref, masks, 192)
    z = jnp.dot(wt_ref[...], x_ref[...], preferred_element_type=F32)
    for j in range(2):
        z_ref[j] = z[:, j * AREA : (j + 1) * AREA]
    mean, squares = local_stats([z[:, :AREA], z[:, AREA:]], 2.0 * AREA)
    tile_ref[...] = packed_tile([jnp.zeros_like(mean), jnp.zeros_like(mean), mean, squares])


def row_taps(own_ref, a_ref, b_ref, c_ref, out_ref, wide_ref, turned_ref):
    masks = tap_masks()
    for peer, ref in enumerate((own_ref, a_ref, b_ref, c_ref)):
        for q in range(4):
            wide_ref[...] = ref[q].astype(F32)
            for r in range(6):
                turned_ref[8 * r : 8 * r + 8, :] = wide_ref[pl.ds(r, 8, stride=6), :]
            plane = turned_ref[...]
            for b in range(3):
                for c in range(3):
                    view = shifted(plane, b, c, masks).astype(BF16)
                    for a in range(3):
                        j = q - a
                        if 0 <= j < 2:
                            tap = 9 * a + 3 * b + c
                            lanes = (2 * peer + j) * AREA
                            out_ref[tap * 48 : (tap + 1) * 48, lanes : lanes + AREA] = view


def head_and_sums(
    flag_ref,
    z_ref,
    recv_ref,
    own_ref,
    low_ref,
    high_ref,
    out_cot_ref,
    skip_cot_ref,
    rim_low_ref,
    rim_high_ref,
    label_ref,
    affine_ref,
    head_ref,
    head_turned_ref,
    fwd_tile_ref,
    normed_ref,
    act_ref,
    up_ref,
    share_ref,
    scale_ref,
    send_ref,
):
    decoder = flag_ref[0] == 1
    last = flag_ref[1] == 1
    peers = recv_ref.shape[0]
    cells = 2.0 * AREA
    mean, squares = spread_sums(recv_ref[...], 0, cells, peers)
    inv_std = lax.rsqrt(squares / (cells * peers) + epsilon)
    gain = columns(affine_ref[...], 0)
    shift = columns(affine_ref[...], 2)
    scale_ref[...] = jnp.broadcast_to(gain * inv_std, scale_ref.shape)
    joined = [low_ref[1], own_ref[0], own_ref[1], high_ref[0]]
    out_cots = [rim_low_ref[192:384], out_cot_ref[0], out_cot_ref[1], rim_high_ref[192:384]]
    skip_cots = [rim_low_ref[384:576], skip_cot_ref[0], skip_cot_ref[1], rim_high_ref[384:576]]
    labels = [
        rim_low_ref[576:592].astype(F32)[:1],
        label_ref[0:1, :].astype(F32),
        label_ref[1:2, :].astype(F32),
        rim_high_ref[576:592].astype(F32)[:1],
    ]
    classes = head_ref.shape[1]
    class_id = lax.broadcasted_iota(jnp.int32, (classes, AREA), 0).astype(F32)
    sum_grad = jnp.zeros((192, 1), F32)
    sum_cross = jnp.zeros((192, 1), F32)
    for j in range(4):
        normed = (z_ref[j] - mean) * inv_std
        scaled = normed * gain + shift
        activated = jnp.where(scaled > 0, scaled, leak_slope * scaled)
        output = (joined[j].astype(F32) + activated).astype(BF16)
        logits = jnp.dot(head_turned_ref[...], output, preferred_element_type=F32)
        raised = jnp.exp(logits - jnp.max(logits, axis=0, keepdims=True))
        prob = raised / jnp.sum(raised, axis=0, keepdims=True)
        delta = (prob - jnp.where(class_id == labels[j], 1.0, 0.0)).astype(BF16)
        head_cot = jnp.dot(head_ref[...], delta, preferred_element_type=F32)
        upstream = jnp.where(last, head_cot, out_cots[j].astype(F32)) + jnp.where(
            decoder, 0.0, skip_cots[j].astype(F32)
        )
        grad_act = upstream * jnp.where(scaled > 0, 1.0, leak_slope)
        normed_ref[j] = normed
        act_ref[j] = grad_act
        if j in (1, 2):
            up_ref[j - 1] = upstream
            share_ref[j - 1] = grad_act.astype(BF16)
            share_ref[j + 1] = normed.astype(BF16)
            sum_grad = sum_grad + jnp.sum(grad_act, axis=1, keepdims=True)
            sum_cross = sum_cross + jnp.sum(grad_act * normed, axis=1, keepdims=True)
    tile = packed_tile([sum_grad, sum_cross]) + fwd_tile_ref[...]
    send_ref[...] = jnp.broadcast_to(tile[None], send_ref.shape)


def kernel_grads(
    recv_ref,
    own_ref,
    a_ref,
    b_ref,
    c_ref,
    scale_ref,
    taps_ref,
    out_ref,
    tot_ref,
    gz_ref,
    low_ref,
    rest_ref,
):
    total_cells = 2.0 * AREA * recv_ref.shape[0]
    total = jnp.sum(recv_ref[...], axis=0)
    tot_ref[...] = total * (total_cells ** (-0.5))
    sum_grad = columns(total, 0) / total_cells
    sum_cross = columns(total, 2) / total_cells
    scale = scale_ref[...]
    for peer, ref in enumerate((own_ref, a_ref, b_ref, c_ref)):
        for j in range(2):
            grad_z = scale * (ref[j].astype(F32) - sum_grad - ref[2 + j].astype(F32) * sum_cross)
            lanes = (2 * peer + j) * AREA
            gz_ref[:, lanes : lanes + AREA] = grad_z.astype(BF16)
    grads = lax.dot_general(
        taps_ref[...], gz_ref[...], (((1,), (1,)), ((), ())), preferred_element_type=F32
    )
    low_ref[...] = grads[:, :128]
    rest_ref[...] = jnp.concatenate([grads[:648, 128:], grads[648:, 128:]], axis=1)
    pad = jnp.zeros((15, 384), F32)
    for z in range(8):
        first = low_ref[pl.ds(z, 81, stride=8), :]
        second = low_ref[pl.ds(z + 648, 81, stride=8), :]
        third = rest_ref[pl.ds(z, 81, stride=8), :]
        both = jnp.concatenate([first, second, third], axis=1)
        out_ref[z] = jnp.concatenate([both, pad], axis=0).astype(BF16)


def input_grads(
    flag_ref,
    recv_ref,
    normed_ref,
    act_ref,
    up_ref,
    scale_ref,
    w_ref,
    fwd_z_ref,
    fwd_ref,
    affine_ref,
    gj_ref,
    fwd_out_ref,
    skip_ref,
    x_ref,
):
    decoder = flag_ref[0] == 1
    peers = recv_ref.shape[0]
    cells = 2.0 * AREA
    total_cells = cells * peers
    masks = tap_masks()
    total = jnp.sum(recv_ref[...], axis=0)
    sum_grad = columns(total, 0) / total_cells
    sum_cross = columns(total, 2) / total_cells
    scale = scale_ref[...]
    for q in range(4):
        grad_z = scale * (act_ref[q] - sum_grad - normed_ref[q] * sum_cross)
        if q == 0:
            grad_z = jnp.where(flag_ref[2] == 1, grad_z, 0.0)
        if q == 3:
            grad_z = jnp.where(flag_ref[3] == 1, grad_z, 0.0)
        for b in range(3):
            for c in range(3):
                view = shifted(grad_z, 2 - b, 2 - c, masks).astype(BF16)
                for a in range(3):
                    j = q + a - 2
                    if 0 <= j < 2:
                        tap = 9 * a + 3 * b + c
                        x_ref[tap * 192 : (tap + 1) * 192, j * AREA : (j + 1) * AREA] = view
    back = jnp.dot(w_ref[...], x_ref[...], preferred_element_type=F32)
    mean, squares = spread_sums(recv_ref[...], 4, cells, peers)
    inv_std = lax.rsqrt(squares / total_cells + epsilon)
    gain = columns(affine_ref[...], 0)
    shift = columns(affine_ref[...], 2)
    for j in range(2):
        grad = (up_ref[j] + back[:, j * AREA : (j + 1) * AREA]).astype(BF16)
        scaled = (fwd_z_ref[j] - mean) * inv_std * gain + shift
        activated = jnp.where(scaled > 0, scaled, leak_slope * scaled)
        output = (fwd_ref[j].astype(F32) + activated).astype(BF16)
        gj_ref[j] = grad
        fwd_out_ref[j] = output
        skip_ref[j] = jnp.where(decoder, grad.astype(F32), output.astype(F32)).astype(BF16)


def sum_rows(scale_out, recv_ref, out_ref):
    total = jnp.sum(recv_ref[...].astype(F32), axis=0) * scale_out
    for tap in range(TAPS):
        for r in range(6):
            flat = tap * 6 + r
            half, row = flat // 81, flat % 81
            low = total[row : row + 1, half * 128 : half * 128 + 128]
            rest = total[row : row + 1, 256 + half * 64 : 320 + half * 64]
            out_ref[0, r : r + 1, tap * 192 : (tap + 1) * 192] = jnp.concatenate(
                [low, rest], axis=1
            )


def pair_rows(values):
    padded = jnp.pad(values, ((0, 2), (0, 64)))
    return padded.reshape(8, AREA)


def moved(block, axis, distance, wrap=True):
    count = lax.axis_size(axis)
    route = [(i, (i + distance) % count) for i in range(count) if wrap or 0 <= i + distance < count]
    return lax.ppermute(block, axis, route)


def per_device(
    fwd_input,
    fwd_skip,
    bwd_input,
    bwd_skip,
    out_cot,
    skip_cot,
    kernel,
    norm_gain,
    norm_shift,
    head_weight,
    labels,
):
    segments = lax.axis_size("segment")
    slabs = lax.axis_size("y") * lax.axis_size("z")
    segment_id = lax.axis_index("segment")
    y_id = lax.axis_index("y")
    slab_id = y_id * lax.axis_size("z") + lax.axis_index("z")
    is_decoder = segment_id * 2 >= segments
    flags = jnp.stack(
        [is_decoder, segment_id == segments - 1, slab_id > 0, slab_id < slabs - 1]
    ).astype(jnp.int32)
    kernel_mat = kernel[0]
    affine = pair_rows(jnp.concatenate([norm_gain, norm_shift], axis=0))

    def by_plane(block):
        return jnp.swapaxes(block[0], 0, 1)

    def joined(block, skip):
        added = (block.astype(F32) + skip.astype(F32)).astype(BF16)
        return by_plane(jnp.where(is_decoder, added, block))

    bwd = joined(bwd_input, bwd_skip)
    bwd_low = moved(bwd, SLABS, 1, False)
    bwd_high = moved(bwd, SLABS, -1, False)
    fwd = joined(fwd_input, fwd_skip)
    out_cots = by_plane(out_cot)
    skip_cots = by_plane(skip_cot)

    def rim(p):
        names = jnp.broadcast_to(labels[p : p + 1].astype(BF16), (16, AREA))
        return jnp.concatenate([fwd[p], out_cots[p], skip_cots[p], names], axis=0)

    rim_low = moved(rim(1), SLABS, 1, False)
    rim_high = moved(rim(0), SLABS, -1, False)
    (turned,) = call(
        turn_weights, [((192, 5184), BF16)], [], 0, 4 * 192 * 5184, kernel_mat
    )
    z, stats_send = call(
        conv_bwd,
        [((4, 192, AREA), F32), ((slabs, 8, AREA), F32)],
        [((5184, 512), BF16)],
        2 * 5184 * 192 * 512,
        5000000,
        bwd,
        bwd_low,
        bwd_high,
        turned,
    )
    stats = lax.all_to_all(stats_send, SLABS, 0, 0, tiled=True)
    window = jnp.concatenate([bwd_low[1:], bwd, bwd_high[:1]], axis=0)

    def rows_for(distance):
        start = 48 * ((y_id + distance) % 4)
        return lax.dynamic_slice_in_dim(window, start, 48, axis=1)

    row_parts = [rows_for(0)] + [moved(rows_for(d), "y", d) for d in (1, 2, 3)]
    fwd_z, fwd_tile = call(
        conv_fwd,
        [((2, 192, AREA), F32), ((8, AREA), F32)],
        [((5184, 256), BF16)],
        2 * 5184 * 192 * 256,
        4000000,
        fwd,
        rim_low[None, :192],
        rim_high[None, :192],
        turned,
    )
    (taps,) = call(
        row_taps,
        [((1296, 1024), BF16)],
        [((48, AREA), F32), ((48, AREA), F32)],
        0,
        6000000,
        *row_parts,
    )
    normed, grad_act, upstream, share, scale, sums_send = call(
        head_and_sums,
        [
            ((4, 192, AREA), F32),
            ((4, 192, AREA), F32),
            ((2, 192, AREA), F32),
            ((4, 192, AREA), BF16),
            ((192, AREA), F32),
            ((slabs, 8, AREA), F32),
        ],
        [],
        4 * 192 * 105 * 512,
        4000000,
        flags,
        z,
        stats,
        bwd,
        bwd_low,
        bwd_high,
        out_cots,
        skip_cots,
        rim_low,
        rim_high,
        labels,
        affine,
        head_weight,
        head_weight.T,
        fwd_tile,
        smem=1,
    )
    sums = lax.all_to_all(sums_send, SLABS, 0, 0, tiled=True)
    shares = [share] + [moved(share, "y", d) for d in (1, 2, 3)]
    parts, totals = call(
        kernel_grads,
        [((8, 96, 384), BF16), ((8, AREA), F32)],
        [((192, 1024), BF16), ((1296, AREA), F32), ((648, AREA), F32)],
        2 * 1296 * 1024 * 192,
        5000000,
        sums,
        *shares,
        scale,
        taps,
    )
    summed = lax.all_to_all(parts, "z", 0, 0, tiled=True)
    grad_joined, fwd_out, outgoing = call(
        input_grads,
        [((2, 192, AREA), BF16)] * 3,
        [((5184, 256), BF16)],
        2 * 5184 * 192 * 256,
        4000000,
        flags,
        sums,
        normed,
        grad_act,
        upstream,
        scale,
        kernel_mat,
        fwd_z,
        fwd,
        affine,
        smem=1,
    )
    next_block = moved(fwd_out, "segment", 1)
    prev_block = moved(grad_joined, "segment", -1)
    mirrored = lax.ppermute(outgoing, "segment", [(i, segments - 1 - i) for i in range(segments)])
    total_cells = float(2 * slabs * AREA)
    (kernel_grad,) = pl.pallas_call(
        lambda recv, out: sum_rows(total_cells ** (-0.5), recv, out),
        out_shape=[jax.ShapeDtypeStruct((1, 6, 5184), F32)],
        in_specs=[VMEM],
        out_specs=[VMEM],
        name="sum_rows",
    )(summed)
    flat = totals.reshape(-1)

    def by_channel(block):
        return jnp.swapaxes(block, 0, 1)[None]

    return (
        by_channel(next_block),
        by_channel(prev_block),
        by_channel(mirrored),
        kernel_grad,
        flat[256:448][None],
        flat[:192][None],
    )


def solution(mesh):
    grid = Mesh(mesh.devices.reshape(mesh.devices.shape[0], 4, 8), ("segment", "y", "z"))
    field = P("segment", None, SLABS, None)
    in_specs = (field,) * 6 + (
        P("segment", None, None),
        P("segment", None),
        P("segment", None),
        P(),
        P(SLABS, None),
    )
    out_specs = (
        field,
        field,
        field,
        P("segment", SLABS, None),
        P("segment", None),
        P("segment", None),
    )
    return jax.shard_map(
        per_device, mesh=grid, in_specs=in_specs, out_specs=out_specs, check_vma=False
    )
```

```python
import functools

import jax
import jax.numpy as jnp
from jax import lax
from jax.experimental import pallas as pl
from jax.experimental.pallas import tpu as pltpu
from jax.sharding import Mesh
from jax.sharding import PartitionSpec as P

ROWS = 8
COLS = 16
AREA = ROWS * COLS
TAPS = 27
SLABS = ("y", "z")

epsilon = 1e-05
leak_slope = 0.01

F32 = jnp.float32
BF16 = jnp.bfloat16
HBM = pl.BlockSpec(memory_space=pltpu.HBM)
VMEM = pl.BlockSpec(memory_space=pltpu.VMEM)
SMEM = pl.BlockSpec(memory_space=pltpu.SMEM)


def call(body, outs, scratch, flops, moved, *args, smem=0, hbm=0, limit=24):
    specs = [SMEM] * smem + [HBM] * hbm + [VMEM] * (len(args) - smem - hbm)
    shapes = [jax.ShapeDtypeStruct(shape, kind) for shape, kind in outs]
    places = [pltpu.VMEM(shape, kind) for shape, kind in scratch]
    return pl.pallas_call(
        body,
        out_shape=shapes,
        in_specs=specs,
        out_specs=[VMEM] * len(outs),
        scratch_shapes=places + [pltpu.SemaphoreType.DMA] * (hbm > 0),
        compiler_params=pltpu.CompilerParams(vmem_limit_bytes=limit * 1024 * 1024),
        cost_estimate=pl.CostEstimate(flops=flops, bytes_accessed=moved, transcendentals=0),
        name=getattr(body, "__name__", "kernel"),
    )(*args)


def tap_masks():
    cell = lax.broadcasted_iota(jnp.int32, (1, AREA), 1)
    row = cell // COLS
    col = cell % COLS
    masks = {}
    for b in range(3):
        for c in range(3):
            inside = None
            if b != 1:
                inside = row > 0 if b == 0 else row < ROWS - 1
            if c != 1:
                part = col > 0 if c == 0 else col < COLS - 1
                inside = part if inside is None else jnp.logical_and(inside, part)
            masks[(b, c)] = inside
    return masks


def shifted(plane, b, c, masks):
    step = (b - 1) * COLS + (c - 1)
    if step == 0:
        return plane
    moved = pltpu.roll(plane, (-step) % AREA, 1)
    return jnp.where(masks[(b, c)], moved, 0.0)


def full_tile(tile):
    if tile.shape[0] == 8:
        return tile
    return jnp.concatenate([tile, jnp.zeros((8 - tile.shape[0], AREA), F32)], axis=0)


def columns(tile, row):
    square = jnp.concatenate([tile, jnp.zeros((AREA - 8, AREA), F32)], axis=0).T
    return jnp.concatenate([square[:, row : row + 1], square[:64, row + 1 : row + 2]], axis=0)


def packed_tile(cols):
    lane = lax.broadcasted_iota(jnp.int32, (AREA, AREA), 1)
    square = jnp.zeros((AREA, AREA), F32)
    for index, col in enumerate(cols):
        high = jnp.concatenate([col[128:], jnp.zeros((64, 1), F32)], axis=0)
        square = jnp.where(lane == 2 * index, col[:128], square)
        square = jnp.where(lane == 2 * index + 1, high, square)
    return square.T[:8]


def spread_sums(received, row, cells, peers):
    total = jnp.sum(received, axis=0)
    mean = total / peers
    apart = jnp.sum(jnp.square(received - mean[None]), axis=0)
    return columns(mean, row), columns(total, row + 2) + cells * columns(apart, row)


def local_stats(planes_out, cells):
    mean = sum(jnp.sum(p, axis=1, keepdims=True) for p in planes_out) / cells
    squares = sum(jnp.sum(jnp.square(p - mean), axis=1, keepdims=True) for p in planes_out)
    return [mean, squares]


def turn_weights(w_ref, out_ref):
    for pair in range(14):
        width = 384 if pair < 13 else 192
        block = w_ref[:, pair * 384 : pair * 384 + width].T
        if width == 384:
            block = jnp.concatenate([block[:192], block[192:]], axis=1)
        out_ref[:, pair * 384 : pair * 384 + width] = block


def fill_taps(planes, outputs, x_ref, masks, channels, first):
    for q, plane in enumerate(planes):
        wide = plane.astype(F32)
        for b in range(3):
            for c in range(3):
                view = shifted(wide, b, c, masks).astype(BF16)
                for a in range(3):
                    j = q - a
                    if 0 <= j < outputs:
                        tap = 9 * a + 3 * b + c
                        lanes = (first + j) * AREA
                        x_ref[
                            tap * channels : (tap + 1) * channels, lanes : lanes + AREA
                        ] = view


def conv_both(own_ref, low_ref, high_ref, wt_ref, z_ref, send_ref, x_ref):
    masks = tap_masks()
    for which in range(2):
        rows = slice(192 * which, 192 * which + 192)
        planes = [low_ref[rows], own_ref[0, rows], own_ref[1, rows], high_ref[rows]]
        fill_taps(planes, 2, x_ref, masks, 192, 2 * which)
    z = jnp.dot(wt_ref[...], x_ref[...], preferred_element_type=F32)
    outs = [z[:, j * AREA : (j + 1) * AREA] for j in range(4)]
    for j in range(4):
        z_ref[j] = outs[j]
    tile = packed_tile(
        local_stats(outs[:2], 2.0 * AREA) + local_stats(outs[2:], 2.0 * AREA)
    )
    send_ref[...] = jnp.broadcast_to(tile[None], send_ref.shape)


def head_and_sums(
    flag_ref,
    z_ref,
    recv_ref,
    own_ref,
    out_cot_ref,
    skip_cot_ref,
    label_ref,
    affine_ref,
    head_ref,
    head_turned_ref,
    up_ref,
    share_ref,
    scale_ref,
    send_ref,
):
    decoder = flag_ref[0] == 1
    last = flag_ref[1] == 1
    peers = recv_ref.shape[0]
    cells = 2.0 * AREA
    mean, squares = spread_sums(recv_ref[...], 0, cells, peers)
    inv_std = lax.rsqrt(squares / (cells * peers) + epsilon)
    gain = columns(affine_ref[...], 0)
    shift = columns(affine_ref[...], 2)
    scale_ref[...] = jnp.broadcast_to(gain * inv_std, scale_ref.shape)
    classes = head_ref.shape[1]
    class_id = lax.broadcasted_iota(jnp.int32, (classes, AREA), 0)
    sum_grad = jnp.zeros((192, 1), F32)
    sum_cross = jnp.zeros((192, 1), F32)
    for j in range(2):
        normed = (z_ref[j] - mean) * inv_std
        scaled = normed * gain + shift
        activated = jnp.where(scaled > 0, scaled, leak_slope * scaled)
        output = (own_ref[j, :192].astype(F32) + activated).astype(BF16)
        logits = jnp.dot(head_turned_ref[...], output, preferred_element_type=F32)
        raised = jnp.exp(logits - jnp.max(logits, axis=0, keepdims=True))
        prob = raised / jnp.sum(raised, axis=0, keepdims=True)
        hot = jnp.where(class_id == label_ref[j : j + 1, :], 1.0, 0.0)
        delta = (prob - hot).astype(BF16)
        head_cot = jnp.dot(head_ref[...], delta, preferred_element_type=F32)
        upstream = jnp.where(last, head_cot, out_cot_ref[j].astype(F32)) + jnp.where(
            decoder, 0.0, skip_cot_ref[j].astype(F32)
        )
        grad_act = upstream * jnp.where(scaled > 0, 1.0, leak_slope)
        up_ref[j] = upstream
        share_ref[2 * j] = grad_act.astype(BF16)
        share_ref[2 * j + 1] = normed.astype(BF16)
        sum_grad = sum_grad + jnp.sum(grad_act, axis=1, keepdims=True)
        sum_cross = sum_cross + jnp.sum(grad_act * normed, axis=1, keepdims=True)
    tile = packed_tile([sum_grad, sum_cross])
    send_ref[...] = jnp.broadcast_to(tile[None, : send_ref.shape[1]], send_ref.shape)


def forward_out(recv_ref, z_ref, own_ref, affine_ref, out_ref):
    peers = recv_ref.shape[0]
    cells = 2.0 * AREA
    mean, squares = spread_sums(recv_ref[...], 4, cells, peers)
    inv_std = lax.rsqrt(squares / (cells * peers) + epsilon)
    gain = columns(affine_ref[...], 0)
    shift = columns(affine_ref[...], 2)
    for j in range(2):
        scaled = (z_ref[2 + j] - mean) * inv_std * gain + shift
        activated = jnp.where(scaled > 0, scaled, leak_slope * scaled)
        out_ref[j] = (own_ref[j, 192:].astype(F32) + activated).astype(BF16)


def row_taps(refs, taps_ref, wide_ref, turned_ref):
    masks = tap_masks()
    for peer, ref in enumerate(refs):
        for q in range(4):
            wide_ref[...] = ref[q].astype(F32)
            for r in range(6):
                turned_ref[8 * r : 8 * r + 8, :] = wide_ref[pl.ds(r, 8, stride=6), :]
            plane = turned_ref[...]
            for b in range(3):
                for c in range(3):
                    view = shifted(plane, b, c, masks).astype(BF16)
                    for a in range(3):
                        j = q - a
                        if 0 <= j < 2:
                            tap = 9 * a + 3 * b + c
                            lanes = (2 * peer + j) * AREA
                            taps_ref[tap * 48 : (tap + 1) * 48, lanes : lanes + AREA] = view
    taps_ref[1296:1344, :] = jnp.zeros((48, 8 * AREA), BF16)


def kernel_grads(
    recv_ref,
    own_ref,
    a_ref,
    b_ref,
    c_ref,
    rows_own_ref,
    rows_a_ref,
    rows_b_ref,
    rows_c_ref,
    scale_ref,
    out_ref,
    tot_ref,
    taps_ref,
    gz_ref,
    low_ref,
    rest_ref,
    wide_ref,
    turned_ref,
):
    row_taps((rows_own_ref, rows_a_ref, rows_b_ref, rows_c_ref), taps_ref, wide_ref, turned_ref)
    total_cells = 2.0 * AREA * recv_ref.shape[0]
    total = full_tile(jnp.sum(recv_ref[...], axis=0))
    tot_ref[...] = total * (total_cells ** (-0.5))
    sum_grad = columns(total, 0) / total_cells
    sum_cross = columns(total, 2) / total_cells
    scale = scale_ref[...]
    for peer, ref in enumerate((own_ref, a_ref, b_ref, c_ref)):
        for j in range(2):
            act = ref[2 * j].astype(F32)
            normed = ref[2 * j + 1].astype(F32)
            lanes = (2 * peer + j) * AREA
            gz_ref[:, lanes : lanes + AREA] = (
                scale * (act - sum_grad - normed * sum_cross)
            ).astype(BF16)
    grads = lax.dot_general(
        taps_ref[...], gz_ref[...], (((1,), (1,)), ((), ())), preferred_element_type=F32
    )
    low_ref[...] = grads[:, :128]
    rest_ref[...] = jnp.concatenate([grads[:672, 128:], grads[672:, 128:]], axis=1)
    pad = jnp.zeros((12, 384), F32)
    for z in range(8):
        first = low_ref[pl.ds(z, 84, stride=8), :]
        second = low_ref[pl.ds(z + 672, 84, stride=8), :]
        third = rest_ref[pl.ds(z, 84, stride=8), :]
        both = jnp.concatenate([first, second, third], axis=1)
        out_ref[z] = jnp.concatenate([both, pad], axis=0).astype(BF16)


def input_grads(
    flag_ref,
    w_ref,
    recv_ref,
    share_ref,
    up_ref,
    low_ref,
    high_ref,
    scale_ref,
    fwd_out_ref,
    grad_ref,
    skip_ref,
    x_ref,
    w_here_ref,
    sem,
):
    fetch = pltpu.make_async_copy(w_ref, w_here_ref, sem)
    fetch.start()
    decoder = flag_ref[0] == 1
    total_cells = 2.0 * AREA * recv_ref.shape[0]
    masks = tap_masks()
    total = full_tile(jnp.sum(recv_ref[...], axis=0))
    sum_grad = columns(total, 0) / total_cells
    sum_cross = columns(total, 2) / total_cells
    scale = scale_ref[...]
    acts = [low_ref[0], share_ref[0], share_ref[2], high_ref[0]]
    norms = [low_ref[1], share_ref[1], share_ref[3], high_ref[1]]
    for q in range(4):
        grad_z = scale * (acts[q].astype(F32) - sum_grad - norms[q].astype(F32) * sum_cross)
        if q == 0:
            grad_z = jnp.where(flag_ref[2] == 1, grad_z, 0.0)
        if q == 3:
            grad_z = jnp.where(flag_ref[3] == 1, grad_z, 0.0)
        for b in range(3):
            for c in range(3):
                view = shifted(grad_z, 2 - b, 2 - c, masks).astype(BF16)
                for a in range(3):
                    j = q + a - 2
                    if 0 <= j < 2:
                        tap = 9 * a + 3 * b + c
                        x_ref[tap * 192 : (tap + 1) * 192, j * AREA : (j + 1) * AREA] = view
    fetch.wait()
    back = jnp.dot(w_here_ref[...], x_ref[...], preferred_element_type=F32)
    for j in range(2):
        grad = (up_ref[j] + back[:, j * AREA : (j + 1) * AREA]).astype(BF16)
        grad_ref[j] = grad
        skip_ref[j] = jnp.where(
            decoder, grad.astype(F32), fwd_out_ref[j].astype(F32)
        ).astype(BF16)


def sum_rows(scale_out, recv_ref, out_ref, wide_ref):
    total = jnp.sum(recv_ref[...].astype(F32), axis=0) * scale_out

    def block(tap):
        half, row = tap // 14, 6 * (tap % 14)
        low = total[row : row + 6, half * 128 : half * 128 + 128]
        rest = total[row : row + 6, 256 + half * 64 : 320 + half * 64]
        return [low, rest]

    for tap in range(0, TAPS, 2):
        parts = block(tap) + (block(tap + 1) if tap + 1 < TAPS else [])
        width = 192 if tap + 1 == TAPS else 384
        wide_ref[0:6, tap * 192 : tap * 192 + width] = jnp.concatenate(parts, axis=1)
    for r in range(6):
        out_ref[r] = wide_ref[r : r + 1, :]


def pair_rows(values):
    padded = jnp.pad(values, ((0, 2), (0, 64)))
    return padded.reshape(8, AREA)


def moved(block, axis, distance, wrap=True):
    count = lax.axis_size(axis)
    route = [(i, (i + distance) % count) for i in range(count) if wrap or 0 <= i + distance < count]
    return lax.ppermute(block, axis, route)


def per_device(
    fwd_input,
    fwd_skip,
    bwd_input,
    bwd_skip,
    out_cot,
    skip_cot,
    kernel,
    norm_gain,
    norm_shift,
    head_weight,
    labels,
):
    segments = lax.axis_size("segment")
    slabs = lax.axis_size("y") * lax.axis_size("z")
    segment_id = lax.axis_index("segment")
    y_id = lax.axis_index("y")
    slab_id = y_id * lax.axis_size("z") + lax.axis_index("z")
    is_decoder = segment_id * 2 >= segments
    flags = jnp.stack(
        [is_decoder, segment_id == segments - 1, slab_id > 0, slab_id < slabs - 1]
    ).astype(jnp.int32)
    kernel_mat = kernel[0]
    affine = pair_rows(jnp.concatenate([norm_gain, norm_shift], axis=0))

    def by_plane(block):
        return jnp.swapaxes(block[0], 0, 1)

    def joined(block, skip):
        added = (block.astype(F32) + skip.astype(F32)).astype(BF16)
        return by_plane(jnp.where(is_decoder, added, block))

    own = jnp.concatenate([joined(bwd_input, bwd_skip), joined(fwd_input, fwd_skip)], axis=1)
    low = moved(own[1], SLABS, 1, False)
    high = moved(own[0], SLABS, -1, False)
    (turned,) = call(turn_weights, [((192, 5184), BF16)], [], 0, 4 * 192 * 5184, kernel_mat)
    z, stats_send = call(
        conv_both,
        [((4, 192, AREA), F32), ((slabs, 8, AREA), F32)],
        [((5184, 512), BF16)],
        2 * 5184 * 192 * 512,
        5000000,
        own,
        low,
        high,
        turned,
    )
    stats = lax.all_to_all(stats_send, SLABS, 0, 0, tiled=True)
    out_cots = by_plane(out_cot)
    skip_cots = by_plane(skip_cot)
    window = jnp.concatenate([low[None, :192], own[:, :192], high[None, :192]], axis=0)

    def rows_for(distance):
        start = 48 * ((y_id + distance) % 4)
        return lax.dynamic_slice_in_dim(window, start, 48, axis=1)

    row_parts = [rows_for(0)] + [moved(rows_for(d), "y", d) for d in (1, 2, 3)]
    stats, row_parts = lax.optimization_barrier((stats, row_parts))
    upstream, share, scale, sums_send = call(
        head_and_sums,
        [
            ((2, 192, AREA), F32),
            ((4, 192, AREA), BF16),
            ((192, AREA), F32),
            ((slabs, 4, AREA), F32),
        ],
        [],
        4 * 192 * 105 * 512,
        4000000,
        flags,
        z,
        stats,
        own,
        out_cots,
        skip_cots,
        labels,
        affine,
        head_weight,
        head_weight.T,
        smem=1,
    )
    sums = lax.all_to_all(sums_send, SLABS, 0, 0, tiled=True)
    shares = [share] + [moved(share, "y", d) for d in (1, 2, 3)]
    rim_low = moved(share[2:], SLABS, 1, False)
    rim_high = moved(share[:2], SLABS, -1, False)
    (fwd_out,) = call(
        forward_out, [((2, 192, AREA), BF16)], [], 0, 1000000, stats, z, own, affine
    )
    sums, rim_low, rim_high, fwd_out = lax.optimization_barrier((sums, rim_low, rim_high, fwd_out))
    parts, totals = call(
        kernel_grads,
        [((8, 96, 384), BF16), ((8, AREA), F32)],
        [
            ((1344, 1024), BF16),
            ((192, 1024), BF16),
            ((1344, AREA), F32),
            ((672, AREA), F32),
            ((48, AREA), F32),
            ((48, AREA), F32),
        ],
        2 * 1296 * 1024 * 192,
        5000000,
        sums,
        *shares,
        *row_parts,
        scale,
    )
    summed = lax.all_to_all(parts, "z", 0, 0, tiled=True)
    grad_joined, outgoing = call(
        input_grads,
        [((2, 192, AREA), BF16)] * 2,
        [((5184, 256), BF16), ((192, 5184), BF16)],
        2 * 5184 * 192 * 256,
        4000000,
        flags,
        kernel_mat,
        sums,
        share,
        upstream,
        rim_low,
        rim_high,
        scale,
        fwd_out,
        smem=1,
        hbm=1,
        limit=52,
    )
    fwd_out, grad_joined, outgoing = lax.optimization_barrier((fwd_out, grad_joined, outgoing))
    prev_block = moved(grad_joined, "segment", -1)
    next_block = moved(fwd_out, "segment", 1)
    mirrored = lax.ppermute(outgoing, "segment", [(i, segments - 1 - i) for i in range(segments)])
    total_cells = float(2 * slabs * AREA)
    (kernel_grad,) = call(
        functools.partial(sum_rows, total_cells ** (-0.5)),
        [((6, 1, 5184), F32)],
        [((8, 5184), F32)],
        0,
        1000000,
        summed,
    )
    flat = totals.reshape(-1)

    def by_channel(block):
        return jnp.swapaxes(block, 0, 1)[None]

    return (
        by_channel(next_block),
        by_channel(prev_block),
        by_channel(mirrored),
        jnp.swapaxes(kernel_grad, 0, 1),
        flat[256:448][None],
        flat[:192][None],
    )


def solution(mesh):
    grid = Mesh(mesh.devices.reshape(mesh.devices.shape[0], 4, 8), ("segment", "y", "z"))
    field = P("segment", None, SLABS, None)
    in_specs = (field,) * 6 + (
        P("segment", None, None),
        P("segment", None),
        P("segment", None),
        P(),
        P(SLABS, None),
    )
    out_specs = (
        field,
        field,
        field,
        P("segment", SLABS, None),
        P("segment", None),
        P("segment", None),
    )
    return jax.shard_map(
        per_device, mesh=grid, in_specs=in_specs, out_specs=out_specs, check_vma=False
    )
```

```python
import functools

import jax
import jax.numpy as jnp
from jax import lax
from jax.experimental import pallas as pl
from jax.experimental.pallas import tpu as pltpu
from jax.sharding import Mesh
from jax.sharding import PartitionSpec as P

ROWS = 8
COLS = 16
AREA = ROWS * COLS
TAPS = 27
SLABS = ("y", "z")

epsilon = 1e-05
leak_slope = 0.01

F32 = jnp.float32
BF16 = jnp.bfloat16
HBM = pl.BlockSpec(memory_space=pltpu.HBM)
VMEM = pl.BlockSpec(memory_space=pltpu.VMEM)
SMEM = pl.BlockSpec(memory_space=pltpu.SMEM)


def call(body, outs, scratch, flops, moved, *args, smem=0, hbm=0, limit=24):
    specs = [SMEM] * smem + [HBM] * hbm + [VMEM] * (len(args) - smem - hbm)
    shapes = [jax.ShapeDtypeStruct(shape, kind) for shape, kind in outs]
    places = [pltpu.VMEM(shape, kind) for shape, kind in scratch]
    return pl.pallas_call(
        body,
        out_shape=shapes,
        in_specs=specs,
        out_specs=[VMEM] * len(outs),
        scratch_shapes=places + [pltpu.SemaphoreType.DMA((4,))] * (hbm > 0),
        compiler_params=pltpu.CompilerParams(vmem_limit_bytes=limit * 1024 * 1024),
        cost_estimate=pl.CostEstimate(flops=flops, bytes_accessed=moved, transcendentals=0),
        name=getattr(body, "__name__", "kernel"),
    )(*args)


def tap_masks():
    cell = lax.broadcasted_iota(jnp.int32, (1, AREA), 1)
    row = cell // COLS
    col = cell % COLS
    masks = {}
    for b in range(3):
        for c in range(3):
            inside = None
            if b != 1:
                inside = row > 0 if b == 0 else row < ROWS - 1
            if c != 1:
                part = col > 0 if c == 0 else col < COLS - 1
                inside = part if inside is None else jnp.logical_and(inside, part)
            masks[(b, c)] = inside
    return masks


def shifted(plane, b, c, masks):
    step = (b - 1) * COLS + (c - 1)
    if step == 0:
        return plane
    moved = pltpu.roll(plane, (-step) % AREA, 1)
    return jnp.where(masks[(b, c)], moved, 0.0)


def full_tile(tile):
    if tile.shape[0] == 8:
        return tile
    return jnp.concatenate([tile, jnp.zeros((8 - tile.shape[0], AREA), F32)], axis=0)


def columns(tile, pair):
    square = jnp.concatenate([full_tile(tile), jnp.zeros((AREA - 8, AREA), F32)], axis=0).T
    row = 3 * pair
    rest = square[:, row + 2 : row + 3]
    first = jnp.concatenate([square[:, row : row + 1], rest[:64]], axis=0)
    second = jnp.concatenate([square[:, row + 1 : row + 2], rest[64:]], axis=0)
    return first, second


def packed_tile(cols):
    lane = lax.broadcasted_iota(jnp.int32, (AREA, AREA), 1)
    square = jnp.zeros((AREA, AREA), F32)
    for pair in range(len(cols) // 2):
        one, two = cols[2 * pair], cols[2 * pair + 1]
        rest = jnp.concatenate([one[128:], two[128:]], axis=0)
        for k, col in enumerate((one[:128], two[:128], rest)):
            square = jnp.where(lane == 3 * pair + k, col, square)
    return square.T[:8]


def spread_sums(received, pair, cells, peers):
    total = jnp.sum(received, axis=0)
    apart = jnp.sum(jnp.square(received - (total / peers)[None]), axis=0)
    mean, squares = columns(total, pair)
    return mean / peers, squares + cells * columns(apart, pair)[0]


def local_stats(planes_out, cells):
    mean = sum(jnp.sum(p, axis=1, keepdims=True) for p in planes_out) / cells
    squares = sum(jnp.sum(jnp.square(p - mean), axis=1, keepdims=True) for p in planes_out)
    return [mean, squares]


def turn_weights(w_ref, out_ref, here_ref, sems):
    bounds = (0, 4, 8, 12, 14)
    copies = []
    for part in range(4):
        start = bounds[part] * 384
        band = pl.ds(start, min(bounds[part + 1] * 384, 5184) - start)
        copies.append(
            pltpu.make_async_copy(w_ref.at[:, band], here_ref.at[:, band], sems.at[part])
        )
        copies[part].start()
    for part in range(4):
        copies[part].wait()
        for pair in range(bounds[part], bounds[part + 1]):
            width = 384 if pair < 13 else 192
            block = here_ref[:, pair * 384 : pair * 384 + width].T
            if width == 384:
                block = jnp.concatenate([block[:192], block[192:]], axis=1)
            out_ref[:, pair * 384 : pair * 384 + width] = block


def fill_taps(planes, outputs, x_ref, masks, channels, first):
    for q, plane in enumerate(planes):
        wide = plane.astype(F32)
        for b in range(3):
            for c in range(3):
                view = shifted(wide, b, c, masks).astype(BF16)
                for a in range(3):
                    j = q - a
                    if 0 <= j < outputs:
                        tap = 9 * a + 3 * b + c
                        lanes = (first + j) * AREA
                        x_ref[
                            tap * channels : (tap + 1) * channels, lanes : lanes + AREA
                        ] = view


def conv_both(own_ref, low_ref, high_ref, wt_ref, z_ref, send_ref, x_ref):
    masks = tap_masks()
    for which in range(2):
        rows = slice(192 * which, 192 * which + 192)
        planes = [low_ref[rows], own_ref[0, rows], own_ref[1, rows], high_ref[rows]]
        fill_taps(planes, 2, x_ref, masks, 192, 2 * which)
    z = jnp.dot(wt_ref[...], x_ref[...], preferred_element_type=F32)
    outs = [z[:, j * AREA : (j + 1) * AREA] for j in range(4)]
    for j in range(4):
        z_ref[j] = outs[j]
    tile = packed_tile(
        local_stats(outs[:2], 2.0 * AREA) + local_stats(outs[2:], 2.0 * AREA)
    )
    send_ref[...] = jnp.broadcast_to(tile[None, : send_ref.shape[1]], send_ref.shape)


def head_and_sums(
    flag_ref,
    z_ref,
    recv_ref,
    own_ref,
    low_ref,
    high_ref,
    out_cot_ref,
    skip_cot_ref,
    label_ref,
    affine_ref,
    head_ref,
    head_turned_ref,
    up_ref,
    share_ref,
    share_a_ref,
    share_b_ref,
    share_c_ref,
    scale_ref,
    send_ref,
):
    shares = (share_ref, share_a_ref, share_b_ref, share_c_ref)
    for distance, ref in enumerate(shares):
        rows = pl.ds(pl.multiple_of(48 * ((flag_ref[4] + distance) % 4), 16), 48)
        ref[4, :48] = low_ref[rows]
        ref[4, 48:96] = own_ref[0, rows]
        ref[4, 96:144] = own_ref[1, rows]
        ref[4, 144:] = high_ref[rows]
    decoder = flag_ref[0] == 1
    last = flag_ref[1] == 1
    peers = recv_ref.shape[0]
    cells = 2.0 * AREA
    mean, squares = spread_sums(recv_ref[...], 0, cells, peers)
    inv_std = lax.rsqrt(squares / (cells * peers) + epsilon)
    gain, shift = columns(affine_ref[...], 0)
    scale_ref[...] = jnp.broadcast_to(gain * inv_std, scale_ref.shape)
    classes = head_ref.shape[1]
    class_id = lax.broadcasted_iota(jnp.int32, (classes, AREA), 0)
    sum_grad = jnp.zeros((192, 1), F32)
    sum_cross = jnp.zeros((192, 1), F32)
    for j in range(2):
        normed = (z_ref[j] - mean) * inv_std
        scaled = normed * gain + shift
        activated = jnp.where(scaled > 0, scaled, leak_slope * scaled)
        output = (own_ref[j, :192].astype(F32) + activated).astype(BF16)
        logits = jnp.dot(head_turned_ref[...], output, preferred_element_type=F32)
        raised = jnp.exp(logits - jnp.max(logits, axis=0, keepdims=True))
        prob = raised / jnp.sum(raised, axis=0, keepdims=True)
        hot = jnp.where(class_id == label_ref[j : j + 1, :], 1.0, 0.0)
        delta = (prob - hot).astype(BF16)
        head_cot = jnp.dot(head_ref[...], delta, preferred_element_type=F32)
        upstream = jnp.where(last, head_cot, out_cot_ref[j].astype(F32)) + jnp.where(
            decoder, 0.0, skip_cot_ref[j].astype(F32)
        )
        grad_act = upstream * jnp.where(scaled > 0, 1.0, leak_slope)
        up_ref[j] = upstream
        for k, part in enumerate((grad_act.astype(BF16), normed.astype(BF16))):
            for ref in shares:
                ref[2 * j + k] = part
        sum_grad = sum_grad + jnp.sum(grad_act, axis=1, keepdims=True)
        sum_cross = sum_cross + jnp.sum(grad_act * normed, axis=1, keepdims=True)
    tile = packed_tile([sum_grad, sum_cross])
    send_ref[...] = jnp.broadcast_to(tile[None, : send_ref.shape[1]], send_ref.shape)


def forward_out(
    recv_ref, z_ref, own_ref, affine_ref, share_ref, out_ref, rim_low_ref, rim_high_ref, mix_ref
):
    rim_high_ref[...] = share_ref[:2]
    rim_low_ref[...] = share_ref[2:4]
    peers = recv_ref.shape[0]
    cells = 2.0 * AREA
    mean, squares = spread_sums(recv_ref[...], 1, cells, peers)
    inv_std = lax.rsqrt(squares / (cells * peers) + epsilon)
    gain, shift = columns(affine_ref[...], 0)
    for j in range(2):
        scaled = (z_ref[2 + j] - mean) * inv_std * gain + shift
        activated = jnp.where(scaled > 0, scaled, leak_slope * scaled)
        mix_ref[pl.ds(j, 192, stride=2), :] = own_ref[j, 192:].astype(F32) + activated
    out_ref[...] = mix_ref[...].astype(BF16)


def row_taps(refs, taps_ref, wide_ref, turned_ref):
    masks = tap_masks()
    for peer, ref in enumerate(refs):
        for q in range(4):
            wide_ref[...] = ref[4, 48 * q : 48 * q + 48].astype(F32)
            for r in range(6):
                turned_ref[8 * r : 8 * r + 8, :] = wide_ref[pl.ds(r, 8, stride=6), :]
            plane = turned_ref[...]
            for b in range(3):
                for c in range(3):
                    view = shifted(plane, b, c, masks).astype(BF16)
                    for a in range(3):
                        j = q - a
                        if 0 <= j < 2:
                            tap = 9 * a + 3 * b + c
                            lanes = (2 * peer + j) * AREA
                            taps_ref[tap * 48 : (tap + 1) * 48, lanes : lanes + AREA] = view
    taps_ref[1296:1344, :] = jnp.zeros((48, 8 * AREA), BF16)


def kernel_grads(
    recv_ref,
    own_ref,
    a_ref,
    b_ref,
    c_ref,
    scale_ref,
    out_ref,
    shift_grad_ref,
    gain_grad_ref,
    taps_ref,
    gz_ref,
    low_ref,
    rest_ref,
    wide_ref,
    turned_ref,
):
    row_taps((own_ref, a_ref, b_ref, c_ref), taps_ref, wide_ref, turned_ref)
    total_cells = 2.0 * AREA * recv_ref.shape[0]
    total = full_tile(jnp.sum(recv_ref[...], axis=0))
    whole = total * (total_cells ** (-0.5))
    shift_grad_ref[...] = jnp.concatenate([whole[:1], whole[2:3, :64]], axis=1)
    gain_grad_ref[...] = jnp.concatenate([whole[1:2], whole[2:3, 64:]], axis=1)
    sum_grad, sum_cross = (col / total_cells for col in columns(total, 0))
    scale = scale_ref[...]
    for peer, ref in enumerate((own_ref, a_ref, b_ref, c_ref)):
        for j in range(2):
            act = ref[2 * j].astype(F32)
            normed = ref[2 * j + 1].astype(F32)
            lanes = (2 * peer + j) * AREA
            gz_ref[:, lanes : lanes + AREA] = (
                scale * (act - sum_grad - normed * sum_cross)
            ).astype(BF16)
    grads = lax.dot_general(
        taps_ref[...], gz_ref[...], (((1,), (1,)), ((), ())), preferred_element_type=F32
    )
    low_ref[...] = grads[:, :128]
    rest_ref[...] = jnp.concatenate([grads[:672, 128:], grads[672:, 128:]], axis=1)
    pad = jnp.zeros((4, 384), F32)
    for z in range(8):
        first = low_ref[pl.ds(z, 84, stride=8), :]
        second = low_ref[pl.ds(z + 672, 84, stride=8), :]
        third = rest_ref[pl.ds(z, 84, stride=8), :]
        both = jnp.concatenate([first, second, third], axis=1)
        out_ref[z] = jnp.concatenate([both, pad], axis=0).astype(BF16)


def input_grads(
    flag_ref,
    w_ref,
    recv_ref,
    share_ref,
    up_ref,
    low_ref,
    high_ref,
    scale_ref,
    fwd_out_ref,
    grad_ref,
    skip_ref,
    x_ref,
    w_here_ref,
    mix_ref,
    sems,
):
    spans = ((0, 1920), (1920, 3840), (3840, 5184))
    copies = []
    for part, (start, stop) in enumerate(spans):
        band = pl.ds(start, stop - start)
        copies.append(
            pltpu.make_async_copy(w_ref.at[:, band], w_here_ref.at[:, band], sems.at[part])
        )
        copies[part].start()
    decoder = flag_ref[0] == 1
    total_cells = 2.0 * AREA * recv_ref.shape[0]
    masks = tap_masks()
    total = full_tile(jnp.sum(recv_ref[...], axis=0))
    sum_grad, sum_cross = (col / total_cells for col in columns(total, 0))
    scale = scale_ref[...]
    acts = [low_ref[0], share_ref[0], share_ref[2], high_ref[0]]
    norms = [low_ref[1], share_ref[1], share_ref[3], high_ref[1]]
    for q in range(4):
        grad_z = scale * (acts[q].astype(F32) - sum_grad - norms[q].astype(F32) * sum_cross)
        if q == 0:
            grad_z = jnp.where(flag_ref[2] == 1, grad_z, 0.0)
        if q == 3:
            grad_z = jnp.where(flag_ref[3] == 1, grad_z, 0.0)
        for b in range(3):
            for c in range(3):
                view = shifted(grad_z, 2 - b, 2 - c, masks).astype(BF16)
                for a in range(3):
                    j = q + a - 2
                    if 0 <= j < 2:
                        tap = 9 * a + 3 * b + c
                        x_ref[tap * 192 : (tap + 1) * 192, j * AREA : (j + 1) * AREA] = view
    back = None
    for copy, (start, stop) in zip(copies, spans):
        copy.wait()
        part = jnp.dot(
            w_here_ref[:, start:stop], x_ref[start:stop, :], preferred_element_type=F32
        )
        back = part if back is None else back + part
    for j in range(2):
        mix_ref[pl.ds(j, 192, stride=2), :] = up_ref[j] + back[:, j * AREA : (j + 1) * AREA]
    grad = mix_ref[...]
    grad_ref[...] = grad.astype(BF16)
    skip_ref[...] = jnp.where(decoder, grad, fwd_out_ref[...].astype(F32)).astype(BF16)


def hand_over(one_ref, two_ref, three_ref, out_one_ref, out_two_ref, out_three_ref):
    out_one_ref[...] = one_ref[...]
    out_two_ref[...] = two_ref[...]
    out_three_ref[...] = three_ref[...]


def sum_rows(scale_out, recv_ref, out_ref, wide_ref):
    total = jnp.sum(recv_ref[...].astype(F32), axis=0) * scale_out

    def block(tap):
        half, row = tap // 14, 6 * (tap % 14)
        low = total[row : row + 6, half * 128 : half * 128 + 128]
        rest = total[row : row + 6, 256 + half * 64 : 320 + half * 64]
        return [low, rest]

    for tap in range(0, TAPS, 2):
        parts = block(tap) + (block(tap + 1) if tap + 1 < TAPS else [])
        width = 192 if tap + 1 == TAPS else 384
        wide_ref[0:6, tap * 192 : tap * 192 + width] = jnp.concatenate(parts, axis=1)
    for r in range(6):
        out_ref[r] = wide_ref[r : r + 1, :]


def pair_rows(one, two):
    rest = jnp.concatenate([one[:, 128:], two[:, 128:]], axis=1)
    return jnp.concatenate([one[:, :128], two[:, :128], rest], axis=0)


def moved(block, axis, distance, wrap=True):
    count = lax.axis_size(axis)
    route = [(i, (i + distance) % count) for i in range(count) if wrap or 0 <= i + distance < count]
    return lax.ppermute(block, axis, route)


def per_device(
    fwd_input,
    fwd_skip,
    bwd_input,
    bwd_skip,
    out_cot,
    skip_cot,
    kernel,
    norm_gain,
    norm_shift,
    head_weight,
    labels,
):
    segments = lax.axis_size("segment")
    slabs = lax.axis_size("y") * lax.axis_size("z")
    segment_id = lax.axis_index("segment")
    y_id = lax.axis_index("y")
    slab_id = y_id * lax.axis_size("z") + lax.axis_index("z")
    is_decoder = segment_id * 2 >= segments
    flags = jnp.stack(
        [
            is_decoder.astype(jnp.int32),
            (segment_id == segments - 1).astype(jnp.int32),
            (slab_id > 0).astype(jnp.int32),
            (slab_id < slabs - 1).astype(jnp.int32),
            y_id.astype(jnp.int32),
        ]
    )
    kernel_mat = kernel[0]
    affine = pair_rows(norm_gain, norm_shift)

    def by_plane(block):
        return jnp.swapaxes(block[0], 0, 1)

    def joined(block, skip):
        added = (block.astype(F32) + skip.astype(F32)).astype(BF16)
        return by_plane(jnp.where(is_decoder, added, block))

    own = jnp.concatenate([joined(bwd_input, bwd_skip), joined(fwd_input, fwd_skip)], axis=1)
    low = moved(own[1], SLABS, 1, False)
    high = moved(own[0], SLABS, -1, False)
    (turned,) = call(
        turn_weights,
        [((192, 5184), BF16)],
        [((192, 5184), BF16)],
        0,
        4 * 192 * 5184,
        kernel_mat,
        hbm=1,
        limit=52,
    )
    z, stats_send = call(
        conv_both,
        [((4, 192, AREA), F32), ((slabs, 6, AREA), F32)],
        [((5184, 512), BF16)],
        2 * 5184 * 192 * 512,
        5000000,
        own,
        low,
        high,
        turned,
    )
    stats = lax.all_to_all(stats_send, SLABS, 0, 0, tiled=True)
    out_cots = by_plane(out_cot)
    skip_cots = by_plane(skip_cot)
    upstream, *shares, scale, sums_send = call(
        head_and_sums,
        [
            ((2, 192, AREA), F32),
            *[((5, 192, AREA), BF16)] * 4,
            ((192, AREA), F32),
            ((slabs, 4, AREA), F32),
        ],
        [],
        4 * 192 * 105 * 512,
        4000000,
        flags,
        z,
        stats,
        own,
        low,
        high,
        out_cots,
        skip_cots,
        labels,
        affine,
        head_weight,
        head_weight.T,
        smem=1,
    )
    sums = lax.all_to_all(sums_send, SLABS, 0, 0, tiled=True)
    share = shares[0]
    shares = [share] + [moved(shares[d], "y", d) for d in (1, 2, 3)]
    fwd_out, rim_low, rim_high = call(
        forward_out,
        [((384, AREA), BF16), ((2, 192, AREA), BF16), ((2, 192, AREA), BF16)],
        [((384, AREA), F32)],
        0,
        1000000,
        stats,
        z,
        own,
        affine,
        share,
    )
    rim_low = moved(rim_low, SLABS, 1, False)
    rim_high = moved(rim_high, SLABS, -1, False)
    sums, fwd_out = lax.optimization_barrier((sums, fwd_out))
    parts, shift_grad, gain_grad = call(
        kernel_grads,
        [((8, 88, 384), BF16), ((1, 192), F32), ((1, 192), F32)],
        [
            ((1344, 1024), BF16),
            ((192, 1024), BF16),
            ((1344, AREA), F32),
            ((672, AREA), F32),
            ((48, AREA), F32),
            ((48, AREA), F32),
        ],
        0,
        1000,
        sums,
        *shares,
        scale,
    )
    parts, rim_low, rim_high = lax.optimization_barrier((parts, rim_low, rim_high))
    summed = lax.all_to_all(parts, "z", 0, 0, tiled=True)
    grad_joined, outgoing = call(
        input_grads,
        [((384, AREA), BF16)] * 2,
        [((5184, 256), BF16), ((192, 5184), BF16), ((384, AREA), F32)],
        2 * 5184 * 192 * 256,
        4000000,
        flags,
        kernel_mat,
        sums,
        share,
        upstream,
        rim_low,
        rim_high,
        scale,
        fwd_out,
        smem=1,
        hbm=1,
        limit=52,
    )
    fwd_out, grad_joined, outgoing = lax.optimization_barrier((fwd_out, grad_joined, outgoing))
    prev_block = moved(grad_joined, "segment", -1)
    next_block = moved(fwd_out, "segment", 1)
    mirrored = lax.ppermute(outgoing, "segment", [(i, segments - 1 - i) for i in range(segments)])
    total_cells = float(2 * slabs * AREA)

    def by_channel(block):
        return block.reshape(1, 192, 2, AREA)

    blocks = call(
        hand_over,
        [((384, AREA), BF16)] * 3,
        [],
        0,
        600000,
        next_block,
        prev_block,
        mirrored,
    )
    handed = [by_channel(block) for block in blocks]
    (kernel_grad,) = call(
        functools.partial(sum_rows, total_cells ** (-0.5)),
        [((6, 1, 5184), F32)],
        [((8, 5184), F32)],
        0,
        1000000,
        summed,
    )
    return (
        *handed,
        jnp.swapaxes(kernel_grad, 0, 1),
        gain_grad,
        shift_grad,
    )


def solution(mesh):
    grid = Mesh(mesh.devices.reshape(mesh.devices.shape[0], 4, 8), ("segment", "y", "z"))
    field = P("segment", None, SLABS, None)
    in_specs = (field,) * 6 + (
        P("segment", None, None),
        P("segment", None),
        P("segment", None),
        P(),
        P(SLABS, None),
    )
    out_specs = (
        field,
        field,
        field,
        P("segment", SLABS, None),
        P("segment", None),
        P("segment", None),
    )
    return jax.shard_map(
        per_device, mesh=grid, in_specs=in_specs, out_specs=out_specs, check_vma=False
    )
```

```python
import functools

import jax
import jax.numpy as jnp
from jax import lax
from jax.experimental import pallas as pl
from jax.experimental.pallas import tpu as pltpu
from jax.sharding import Mesh
from jax.sharding import PartitionSpec as P

ROWS = 8
COLS = 16
AREA = ROWS * COLS
TAPS = 27
SLABS = ("y", "z")

epsilon = 1e-05
leak_slope = 0.01

F32 = jnp.float32
BF16 = jnp.bfloat16
HBM = pl.BlockSpec(memory_space=pltpu.HBM)
VMEM = pl.BlockSpec(memory_space=pltpu.VMEM)
SMEM = pl.BlockSpec(memory_space=pltpu.SMEM)


HEAD_SCRATCH = [((2, 192, AREA), F32)]


def call(body, outs, scratch, flops, moved, *args, smem=0, hbm=0, limit=24):
    specs = [SMEM] * smem + [HBM] * hbm + [VMEM] * (len(args) - smem - hbm)
    shapes = [jax.ShapeDtypeStruct(shape, kind) for shape, kind in outs]
    places = [pltpu.VMEM(shape, kind) for shape, kind in scratch]
    return pl.pallas_call(
        body,
        out_shape=shapes,
        in_specs=specs,
        out_specs=[VMEM] * len(outs),
        scratch_shapes=places + [pltpu.SemaphoreType.DMA((4,))] * (hbm > 0),
        compiler_params=pltpu.CompilerParams(vmem_limit_bytes=limit * 1024 * 1024),
        cost_estimate=pl.CostEstimate(flops=flops, bytes_accessed=moved, transcendentals=0),
        name=getattr(body, "__name__", "kernel"),
    )(*args)


def tap_masks():
    cell = lax.broadcasted_iota(jnp.int32, (1, AREA), 1)
    row = cell // COLS
    col = cell % COLS
    masks = {}
    for b in range(3):
        for c in range(3):
            inside = None
            if b != 1:
                inside = row > 0 if b == 0 else row < ROWS - 1
            if c != 1:
                part = col > 0 if c == 0 else col < COLS - 1
                inside = part if inside is None else jnp.logical_and(inside, part)
            masks[(b, c)] = inside
    return masks


def shifted(plane, b, c, masks):
    step = (b - 1) * COLS + (c - 1)
    if step == 0:
        return plane
    moved = pltpu.roll(plane, (-step) % AREA, 1)
    return jnp.where(masks[(b, c)], moved, jnp.zeros_like(moved))


def full_tile(tile):
    if tile.shape[0] == 8:
        return tile
    return jnp.concatenate([tile, jnp.zeros((8 - tile.shape[0], AREA), F32)], axis=0)


def columns(tile, pair):
    square = jnp.concatenate([full_tile(tile), jnp.zeros((AREA - 8, AREA), F32)], axis=0).T
    row = 3 * pair
    rest = square[:, row + 2 : row + 3]
    first = jnp.concatenate([square[:, row : row + 1], rest[:64]], axis=0)
    second = jnp.concatenate([square[:, row + 1 : row + 2], rest[64:]], axis=0)
    return first, second


def packed_tile(cols):
    lane = lax.broadcasted_iota(jnp.int32, (AREA, AREA), 1)
    square = jnp.zeros((AREA, AREA), F32)
    for pair in range(len(cols) // 2):
        one, two = cols[2 * pair], cols[2 * pair + 1]
        rest = jnp.concatenate([one[128:], two[128:]], axis=0)
        for k, col in enumerate((one[:128], two[:128], rest)):
            square = jnp.where(lane == 3 * pair + k, col, square)
    return square.T[:8]


def spread_sums(received, pair, cells, peers):
    total = jnp.sum(received, axis=0)
    apart = jnp.sum(jnp.square(received - (total / peers)[None]), axis=0)
    mean, squares = columns(total, pair)
    return mean / peers, squares + cells * columns(apart, pair)[0]


def local_stats(planes_out, cells):
    mean = sum(jnp.sum(p, axis=1, keepdims=True) for p in planes_out) / cells
    squares = sum(jnp.sum(jnp.square(p - mean), axis=1, keepdims=True) for p in planes_out)
    return [mean, squares]


def turn_weights(w_ref, out_ref, here_ref, sems):
    bounds = (0, 4, 8, 12, 14)
    copies = []
    for part in range(4):
        start = bounds[part] * 384
        band = pl.ds(start, min(bounds[part + 1] * 384, 5184) - start)
        copies.append(
            pltpu.make_async_copy(w_ref.at[:, band], here_ref.at[:, band], sems.at[part])
        )
        copies[part].start()
    for part in range(4):
        copies[part].wait()
        for pair in range(bounds[part], bounds[part + 1]):
            width = 384 if pair < 13 else 192
            block = here_ref[:, pair * 384 : pair * 384 + width].T
            if width == 384:
                block = jnp.concatenate([block[:192], block[192:]], axis=1)
            out_ref[:, pair * 384 : pair * 384 + width] = block


def fill_taps(planes, outputs, x_ref, masks, channels, first):
    for q, plane in enumerate(planes):
        for b in range(3):
            for c in range(3):
                view = shifted(plane, b, c, masks)
                for a in range(3):
                    j = q - a
                    if 0 <= j < outputs:
                        tap = 9 * a + 3 * b + c
                        lanes = (first + j) * AREA
                        x_ref[
                            tap * channels : (tap + 1) * channels, lanes : lanes + AREA
                        ] = view


def conv_both(own_ref, low_ref, high_ref, wt_ref, z_ref, send_ref, x_ref):
    masks = tap_masks()
    for which in range(2):
        rows = slice(192 * which, 192 * which + 192)
        planes = [low_ref[rows], own_ref[0, rows], own_ref[1, rows], high_ref[rows]]
        fill_taps(planes, 2, x_ref, masks, 192, 2 * which)
    z = jnp.dot(wt_ref[...], x_ref[...], preferred_element_type=F32)
    outs = [z[:, j * AREA : (j + 1) * AREA] for j in range(4)]
    for j in range(4):
        z_ref[j] = outs[j]
    tile = packed_tile(
        local_stats(outs[:2], 2.0 * AREA) + local_stats(outs[2:], 2.0 * AREA)
    )
    send_ref[...] = jnp.broadcast_to(tile[None, : send_ref.shape[1]], send_ref.shape)


def head_and_sums(
    flag_ref,
    z_ref,
    recv_ref,
    own_ref,
    low_ref,
    high_ref,
    out_cot_ref,
    skip_cot_ref,
    label_ref,
    affine_ref,
    head_ref,
    head_turned_ref,
    up_ref,
    share_ref,
    share_a_ref,
    share_b_ref,
    share_c_ref,
    scale_ref,
    send_ref,
    head_cot_ref,
):
    shares = (share_ref, share_a_ref, share_b_ref, share_c_ref)
    for distance, ref in enumerate(shares):
        rows = pl.ds(pl.multiple_of(48 * ((flag_ref[4] + distance) % 4), 16), 48)
        ref[4, :48] = low_ref[rows]
        ref[4, 48:96] = own_ref[0, rows]
        ref[4, 96:144] = own_ref[1, rows]
        ref[4, 144:] = high_ref[rows]
    decoder = flag_ref[0] == 1
    last = flag_ref[1] == 1
    peers = recv_ref.shape[0]
    cells = 2.0 * AREA
    mean, squares = spread_sums(recv_ref[...], 0, cells, peers)
    inv_std = lax.rsqrt(squares / (cells * peers) + epsilon)
    gain, shift = columns(affine_ref[...], 0)
    scale_ref[...] = jnp.broadcast_to(gain * inv_std, scale_ref.shape)
    classes = head_ref.shape[1]
    class_id = lax.broadcasted_iota(jnp.int32, (classes, AREA), 0)
    sum_grad = jnp.zeros((192, 1), F32)
    sum_cross = jnp.zeros((192, 1), F32)
    for j in range(2):
        normed = (z_ref[j] - mean) * inv_std
        scaled = normed * gain + shift
        activated = jnp.where(scaled > 0, scaled, leak_slope * scaled)
        output = (own_ref[j, :192].astype(F32) + activated).astype(BF16)

        @pl.when(last)
        def head(output=output, j=j):
            logits = jnp.dot(head_turned_ref[...], output, preferred_element_type=F32)
            raised = jnp.exp(logits - jnp.max(logits, axis=0, keepdims=True))
            prob = raised / jnp.sum(raised, axis=0, keepdims=True)
            hot = jnp.where(class_id == label_ref[j : j + 1, :], 1.0, 0.0)
            delta = (prob - hot).astype(BF16)
            head_cot_ref[j] = jnp.dot(head_ref[...], delta, preferred_element_type=F32)

        @pl.when(jnp.logical_not(last))
        def given(j=j):
            head_cot_ref[j] = out_cot_ref[j].astype(F32)

        upstream = head_cot_ref[j] + jnp.where(decoder, 0.0, skip_cot_ref[j].astype(F32))
        grad_act = upstream * jnp.where(scaled > 0, 1.0, leak_slope)
        up_ref[j] = upstream
        for k, part in enumerate((grad_act.astype(BF16), normed.astype(BF16))):
            for ref in shares:
                ref[2 * j + k] = part
        sum_grad = sum_grad + jnp.sum(grad_act, axis=1, keepdims=True)
        sum_cross = sum_cross + jnp.sum(grad_act * normed, axis=1, keepdims=True)
    tile = packed_tile([sum_grad, sum_cross])
    send_ref[...] = jnp.broadcast_to(tile[None, : send_ref.shape[1]], send_ref.shape)


def forward_out(
    recv_ref, z_ref, own_ref, affine_ref, share_ref, out_ref, rim_low_ref, rim_high_ref, mix_ref
):
    rim_high_ref[...] = share_ref[:2]
    rim_low_ref[...] = share_ref[2:4]
    peers = recv_ref.shape[0]
    cells = 2.0 * AREA
    mean, squares = spread_sums(recv_ref[...], 1, cells, peers)
    inv_std = lax.rsqrt(squares / (cells * peers) + epsilon)
    gain, shift = columns(affine_ref[...], 0)
    for j in range(2):
        scaled = (z_ref[2 + j] - mean) * inv_std * gain + shift
        activated = jnp.where(scaled > 0, scaled, leak_slope * scaled)
        mix_ref[pl.ds(j, 192, stride=2), :] = own_ref[j, 192:].astype(F32) + activated
    out_ref[...] = mix_ref[...].astype(BF16)


def row_taps(refs, taps_ref, wide_ref, turned_ref):
    masks = tap_masks()
    for peer, ref in enumerate(refs):
        for q in range(4):
            wide_ref[...] = ref[4, 48 * q : 48 * q + 48].astype(F32)
            for r in range(6):
                turned_ref[8 * r : 8 * r + 8, :] = wide_ref[pl.ds(r, 8, stride=6), :]
            plane = turned_ref[...].astype(BF16)
            for b in range(3):
                for c in range(3):
                    view = shifted(plane, b, c, masks)
                    for a in range(3):
                        j = q - a
                        if 0 <= j < 2:
                            tap = 9 * a + 3 * b + c
                            lanes = (2 * peer + j) * AREA
                            taps_ref[tap * 48 : (tap + 1) * 48, lanes : lanes + AREA] = view


def kernel_grads(
    recv_ref,
    own_ref,
    a_ref,
    b_ref,
    c_ref,
    scale_ref,
    out_ref,
    shift_grad_ref,
    gain_grad_ref,
    taps_ref,
    gz_ref,
    low_ref,
    rest_ref,
    wide_ref,
    turned_ref,
):
    row_taps((own_ref, a_ref, b_ref, c_ref), taps_ref, wide_ref, turned_ref)
    total_cells = 2.0 * AREA * recv_ref.shape[0]
    total = full_tile(jnp.sum(recv_ref[...], axis=0))
    whole = total * (total_cells ** (-0.5))
    shift_grad_ref[...] = jnp.concatenate([whole[:1], whole[2:3, :64]], axis=1)
    gain_grad_ref[...] = jnp.concatenate([whole[1:2], whole[2:3, 64:]], axis=1)
    sum_grad, sum_cross = (col / total_cells for col in columns(total, 0))
    scale = scale_ref[...]
    for peer, ref in enumerate((own_ref, a_ref, b_ref, c_ref)):
        for j in range(2):
            act = ref[2 * j].astype(F32)
            normed = ref[2 * j + 1].astype(F32)
            lanes = (2 * peer + j) * AREA
            gz_ref[:, lanes : lanes + AREA] = (
                scale * (act - sum_grad - normed * sum_cross)
            ).astype(BF16)
    grads = lax.dot_general(
        taps_ref[...], gz_ref[...], (((1,), (1,)), ((), ())), preferred_element_type=F32
    )
    low_ref[...] = grads[:, :128]
    rest_ref[...] = jnp.concatenate([grads[:648, 128:], grads[648:, 128:]], axis=1)
    pad = jnp.zeros((5, AREA), F32)
    for z in range(8):
        first = low_ref[pl.ds(z, 162, stride=8), :]
        second = rest_ref[pl.ds(z, 81, stride=8), :]
        out_ref[z] = jnp.concatenate([first, second, pad], axis=0).astype(BF16)


def input_grads(
    flag_ref,
    w_ref,
    recv_ref,
    share_ref,
    up_ref,
    low_ref,
    high_ref,
    scale_ref,
    fwd_out_ref,
    grad_ref,
    skip_ref,
    x_ref,
    w_here_ref,
    mix_ref,
    sems,
):
    fetch = pltpu.make_async_copy(w_ref, w_here_ref, sems.at[0])
    fetch.start()
    decoder = flag_ref[0] == 1
    total_cells = 2.0 * AREA * recv_ref.shape[0]
    masks = tap_masks()
    total = full_tile(jnp.sum(recv_ref[...], axis=0))
    sum_grad, sum_cross = (col / total_cells for col in columns(total, 0))
    scale = scale_ref[...]
    acts = [low_ref[0], share_ref[0], share_ref[2], high_ref[0]]
    norms = [low_ref[1], share_ref[1], share_ref[3], high_ref[1]]
    for q in range(4):
        grad_z = scale * (acts[q].astype(F32) - sum_grad - norms[q].astype(F32) * sum_cross)
        if q == 0:
            grad_z = jnp.where(flag_ref[2] == 1, grad_z, 0.0)
        if q == 3:
            grad_z = jnp.where(flag_ref[3] == 1, grad_z, 0.0)
        grad_z = grad_z.astype(BF16)
        for b in range(3):
            for c in range(3):
                view = shifted(grad_z, 2 - b, 2 - c, masks)
                for a in range(3):
                    j = q + a - 2
                    if 0 <= j < 2:
                        tap = 9 * a + 3 * b + c
                        x_ref[tap * 192 : (tap + 1) * 192, j * AREA : (j + 1) * AREA] = view
    fetch.wait()
    back = jnp.dot(w_here_ref[...], x_ref[...], preferred_element_type=F32)
    for j in range(2):
        mix_ref[pl.ds(j, 192, stride=2), :] = up_ref[j] + back[:, j * AREA : (j + 1) * AREA]
    grad = mix_ref[...]
    grad_ref[...] = grad.astype(BF16)
    skip_ref[...] = jnp.where(decoder, grad, fwd_out_ref[...].astype(F32)).astype(BF16)


def hand_over(one_ref, two_ref, three_ref, out_one_ref, out_two_ref, out_three_ref):
    out_one_ref[...] = one_ref[...]
    out_two_ref[...] = two_ref[...]
    out_three_ref[...] = three_ref[...]


def sum_rows(scale_out, recv_ref, out_ref, wide_ref):
    total = jnp.sum(recv_ref[...].astype(F32), axis=0) * scale_out
    rest = jnp.concatenate([total[162:243, :64], total[162:243, 64:]], axis=0)

    def block(tap):
        rows = slice(6 * tap, 6 * tap + 6)
        return [total[rows], rest[rows]]

    for tap in range(0, TAPS, 2):
        parts = block(tap) + (block(tap + 1) if tap + 1 < TAPS else [])
        width = 192 if tap + 1 == TAPS else 384
        wide_ref[0:6, tap * 192 : tap * 192 + width] = jnp.concatenate(parts, axis=1)
    for r in range(6):
        out_ref[r] = wide_ref[r : r + 1, :]


def pair_rows(one, two):
    rest = jnp.concatenate([one[:, 128:], two[:, 128:]], axis=1)
    return jnp.concatenate([one[:, :128], two[:, :128], rest], axis=0)


def moved(block, axis, distance, wrap=True):
    count = lax.axis_size(axis)
    route = [(i, (i + distance) % count) for i in range(count) if wrap or 0 <= i + distance < count]
    return lax.ppermute(block, axis, route)


def per_device(
    fwd_input,
    fwd_skip,
    bwd_input,
    bwd_skip,
    out_cot,
    skip_cot,
    kernel,
    norm_gain,
    norm_shift,
    head_weight,
    labels,
):
    segments = lax.axis_size("segment")
    slabs = lax.axis_size("y") * lax.axis_size("z")
    segment_id = lax.axis_index("segment")
    y_id = lax.axis_index("y")
    slab_id = y_id * lax.axis_size("z") + lax.axis_index("z")
    is_decoder = segment_id * 2 >= segments
    flags = jnp.stack(
        [
            is_decoder.astype(jnp.int32),
            (segment_id == segments - 1).astype(jnp.int32),
            (slab_id > 0).astype(jnp.int32),
            (slab_id < slabs - 1).astype(jnp.int32),
            y_id.astype(jnp.int32),
        ]
    )
    kernel_mat = kernel[0]
    affine = pair_rows(norm_gain, norm_shift)

    def by_plane(block):
        return jnp.swapaxes(block[0], 0, 1)

    def joined(block, skip):
        added = (block.astype(F32) + skip.astype(F32)).astype(BF16)
        return by_plane(jnp.where(is_decoder, added, block))

    own = jnp.concatenate([joined(bwd_input, bwd_skip), joined(fwd_input, fwd_skip)], axis=1)
    low = moved(own[1], SLABS, 1, False)
    high = moved(own[0], SLABS, -1, False)
    (turned,) = call(
        turn_weights,
        [((192, 5184), BF16)],
        [((192, 5184), BF16)],
        0,
        4 * 192 * 5184,
        kernel_mat,
        hbm=1,
        limit=52,
    )
    z, stats_send = call(
        conv_both,
        [((4, 192, AREA), F32), ((slabs, 6, AREA), F32)],
        [((5184, 512), BF16)],
        2 * 5184 * 192 * 512,
        5000000,
        own,
        low,
        high,
        turned,
    )
    stats = lax.all_to_all(stats_send, SLABS, 0, 0, tiled=True)
    out_cots = by_plane(out_cot)
    skip_cots = by_plane(skip_cot)
    upstream, *shares, scale, sums_send = call(
        head_and_sums,
        [
            ((2, 192, AREA), F32),
            *[((5, 192, AREA), BF16)] * 4,
            ((192, AREA), F32),
            ((slabs, 4, AREA), F32),
        ],
        HEAD_SCRATCH,
        4 * 192 * 105 * 512,
        4000000,
        flags,
        z,
        stats,
        own,
        low,
        high,
        out_cots,
        skip_cots,
        labels,
        affine,
        head_weight,
        head_weight.T,
        smem=1,
    )
    sums = lax.all_to_all(sums_send, SLABS, 0, 0, tiled=True)
    share = shares[0]
    shares = [share] + [moved(shares[d], "y", d) for d in (1, 2, 3)]
    fwd_out, rim_low, rim_high = call(
        forward_out,
        [((384, AREA), BF16), ((2, 192, AREA), BF16), ((2, 192, AREA), BF16)],
        [((384, AREA), F32)],
        0,
        1000000,
        stats,
        z,
        own,
        affine,
        share,
    )
    rim_low = moved(rim_low, SLABS, 1, False)
    rim_high = moved(rim_high, SLABS, -1, False)
    sums, fwd_out = lax.optimization_barrier((sums, fwd_out))
    parts, shift_grad, gain_grad = call(
        kernel_grads,
        [((8, 248, AREA), BF16), ((1, 192), F32), ((1, 192), F32)],
        [
            ((1296, 1024), BF16),
            ((192, 1024), BF16),
            ((1296, AREA), F32),
            ((648, AREA), F32),
            ((48, AREA), F32),
            ((48, AREA), F32),
        ],
        0,
        1000,
        sums,
        *shares,
        scale,
    )
    parts, rim_low, rim_high = lax.optimization_barrier((parts, rim_low, rim_high))
    summed = lax.all_to_all(parts, "z", 0, 0, tiled=True)
    grad_joined, outgoing = call(
        input_grads,
        [((384, AREA), BF16)] * 2,
        [((5184, 256), BF16), ((192, 5184), BF16), ((384, AREA), F32)],
        2 * 5184 * 192 * 256,
        4000000,
        flags,
        kernel_mat,
        sums,
        share,
        upstream,
        rim_low,
        rim_high,
        scale,
        fwd_out,
        smem=1,
        hbm=1,
        limit=52,
    )
    fwd_out, grad_joined, outgoing = lax.optimization_barrier((fwd_out, grad_joined, outgoing))
    prev_block = moved(grad_joined, "segment", -1)
    next_block = moved(fwd_out, "segment", 1)
    mirrored = lax.ppermute(outgoing, "segment", [(i, segments - 1 - i) for i in range(segments)])
    total_cells = float(2 * slabs * AREA)

    def by_channel(block):
        return block.reshape(1, 192, 2, AREA)

    blocks = call(
        hand_over,
        [((384, AREA), BF16)] * 3,
        [],
        0,
        600000,
        next_block,
        prev_block,
        mirrored,
    )
    handed = [by_channel(block) for block in blocks]
    (kernel_grad,) = call(
        functools.partial(sum_rows, total_cells ** (-0.5)),
        [((6, 1, 5184), F32)],
        [((8, 5184), F32)],
        0,
        1000000,
        summed,
    )
    return (
        *handed,
        jnp.swapaxes(kernel_grad, 0, 1),
        gain_grad,
        shift_grad,
    )


def solution(mesh):
    grid = Mesh(mesh.devices.reshape(mesh.devices.shape[0], 4, 8), ("segment", "y", "z"))
    field = P("segment", None, SLABS, None)
    in_specs = (field,) * 6 + (
        P("segment", None, None),
        P("segment", None),
        P("segment", None),
        P(),
        P(SLABS, None),
    )
    out_specs = (
        field,
        field,
        field,
        P("segment", SLABS, None),
        P("segment", None),
        P("segment", None),
    )
    return jax.shard_map(
        per_device, mesh=grid, in_specs=in_specs, out_specs=out_specs, check_vma=False
    )
```

```python
import functools

import jax
import jax.numpy as jnp
from jax import lax
from jax.experimental import pallas as pl
from jax.experimental.pallas import tpu as pltpu
from jax.sharding import Mesh
from jax.sharding import PartitionSpec as P

ROWS = 8
COLS = 16
AREA = ROWS * COLS
TAPS = 27
SLABS = ("y", "z")

epsilon = 1e-05
leak_slope = 0.01

F32 = jnp.float32
BF16 = jnp.bfloat16
HBM = pl.BlockSpec(memory_space=pltpu.HBM)
VMEM = pl.BlockSpec(memory_space=pltpu.VMEM)
SMEM = pl.BlockSpec(memory_space=pltpu.SMEM)


HEAD_SCRATCH = [((2, 192, AREA), F32)]


def call(body, outs, scratch, flops, moved, *args, smem=0, hbm=0, limit=24):
    specs = [SMEM] * smem + [HBM] * hbm + [VMEM] * (len(args) - smem - hbm)
    shapes = [jax.ShapeDtypeStruct(shape, kind) for shape, kind in outs]
    places = [pltpu.VMEM(shape, kind) for shape, kind in scratch]
    return pl.pallas_call(
        body,
        out_shape=shapes,
        in_specs=specs,
        out_specs=[VMEM] * len(outs),
        scratch_shapes=places + [pltpu.SemaphoreType.DMA((4,))] * (hbm > 0),
        compiler_params=pltpu.CompilerParams(vmem_limit_bytes=limit * 1024 * 1024),
        cost_estimate=pl.CostEstimate(flops=flops, bytes_accessed=moved, transcendentals=0),
        name=getattr(body, "__name__", "kernel"),
    )(*args)


def tap_masks():
    cell = lax.broadcasted_iota(jnp.int32, (1, AREA), 1)
    row = cell // COLS
    col = cell % COLS
    masks = {}
    for b in range(3):
        for c in range(3):
            inside = None
            if b != 1:
                inside = row > 0 if b == 0 else row < ROWS - 1
            if c != 1:
                part = col > 0 if c == 0 else col < COLS - 1
                inside = part if inside is None else jnp.logical_and(inside, part)
            masks[(b, c)] = inside
    return masks


def shifted(plane, b, c, masks):
    step = (b - 1) * COLS + (c - 1)
    if step == 0:
        return plane
    moved = pltpu.roll(plane, (-step) % AREA, 1)
    return jnp.where(masks[(b, c)], moved, jnp.zeros_like(moved))


def full_tile(tile):
    if tile.shape[0] == 8:
        return tile
    return jnp.concatenate([tile, jnp.zeros((8 - tile.shape[0], AREA), F32)], axis=0)


def columns(tile, pair):
    square = jnp.concatenate([full_tile(tile), jnp.zeros((AREA - 8, AREA), F32)], axis=0).T
    row = 3 * pair
    rest = square[:, row + 2 : row + 3]
    first = jnp.concatenate([square[:, row : row + 1], rest[:64]], axis=0)
    second = jnp.concatenate([square[:, row + 1 : row + 2], rest[64:]], axis=0)
    return first, second


def packed_tile(cols):
    lane = lax.broadcasted_iota(jnp.int32, (AREA, AREA), 1)
    square = jnp.zeros((AREA, AREA), F32)
    for pair in range(len(cols) // 2):
        one, two = cols[2 * pair], cols[2 * pair + 1]
        rest = jnp.concatenate([one[128:], two[128:]], axis=0)
        for k, col in enumerate((one[:128], two[:128], rest)):
            square = jnp.where(lane == 3 * pair + k, col, square)
    return square.T[:8]


def spread_sums(received, pair, cells, peers):
    total = jnp.sum(received, axis=0)
    apart = jnp.sum(jnp.square(received - (total / peers)[None]), axis=0)
    mean, squares = columns(total, pair)
    return mean / peers, squares + cells * columns(apart, pair)[0]


def local_stats(planes_out, cells):
    mean = sum(jnp.sum(p, axis=1, keepdims=True) for p in planes_out) / cells
    squares = sum(jnp.sum(jnp.square(p - mean), axis=1, keepdims=True) for p in planes_out)
    return [mean, squares]


def turn_weights(w_ref, out_ref, here_ref, sems):
    bounds = (0, 4, 8, 12, 14)
    copies = []
    for part in range(4):
        start = bounds[part] * 384
        band = pl.ds(start, min(bounds[part + 1] * 384, 5184) - start)
        copies.append(
            pltpu.make_async_copy(w_ref.at[:, band], here_ref.at[:, band], sems.at[part])
        )
        copies[part].start()
    for part in range(4):
        copies[part].wait()
        for pair in range(bounds[part], bounds[part + 1]):
            width = 384 if pair < 13 else 192
            block = here_ref[:, pair * 384 : pair * 384 + width].T
            if width == 384:
                block = jnp.concatenate([block[:192], block[192:]], axis=1)
            out_ref[:, pair * 384 : pair * 384 + width] = block


def fill_taps(planes, outputs, x_ref, masks, channels, first):
    for q, plane in enumerate(planes):
        for b in range(3):
            for c in range(3):
                view = shifted(plane, b, c, masks)
                for a in range(3):
                    j = q - a
                    if 0 <= j < outputs:
                        tap = 9 * a + 3 * b + c
                        lanes = (first + j) * AREA
                        x_ref[
                            tap * channels : (tap + 1) * channels, lanes : lanes + AREA
                        ] = view


def inside(flag, rows):
    return jnp.where(flag == 1, rows, jnp.zeros_like(rows))


def conv_both(flag_ref, own_ref, low_ref, high_ref, wt_ref, z_ref, send_ref, x_ref):
    masks = tap_masks()
    for which in range(2):
        rows = slice(192 * which, 192 * which + 192)
        planes = [
            inside(flag_ref[2], low_ref[rows]),
            own_ref[0, rows],
            own_ref[1, rows],
            inside(flag_ref[3], high_ref[rows]),
        ]
        fill_taps(planes, 2, x_ref, masks, 192, 2 * which)
    z = jnp.dot(wt_ref[...], x_ref[...], preferred_element_type=F32)
    outs = [z[:, j * AREA : (j + 1) * AREA] for j in range(4)]
    for j in range(4):
        z_ref[j] = outs[j]
    tile = packed_tile(
        local_stats(outs[:2], 2.0 * AREA) + local_stats(outs[2:], 2.0 * AREA)
    )
    send_ref[...] = jnp.broadcast_to(tile[None, : send_ref.shape[1]], send_ref.shape)


def head_and_sums(
    flag_ref,
    z_ref,
    recv_ref,
    own_ref,
    low_ref,
    high_ref,
    out_cot_ref,
    skip_cot_ref,
    label_ref,
    affine_ref,
    head_ref,
    head_turned_ref,
    up_ref,
    share_ref,
    share_a_ref,
    share_b_ref,
    share_c_ref,
    scale_ref,
    send_ref,
    head_cot_ref,
):
    shares = (share_ref, share_a_ref, share_b_ref, share_c_ref)
    for distance, ref in enumerate(shares):
        rows = pl.ds(pl.multiple_of(48 * ((flag_ref[4] + distance) % 4), 16), 48)
        ref[4, :48] = inside(flag_ref[2], low_ref[rows])
        ref[4, 48:96] = own_ref[0, rows]
        ref[4, 96:144] = own_ref[1, rows]
        ref[4, 144:] = inside(flag_ref[3], high_ref[rows])
    decoder = flag_ref[0] == 1
    last = flag_ref[1] == 1
    peers = recv_ref.shape[0]
    cells = 2.0 * AREA
    mean, squares = spread_sums(recv_ref[...], 0, cells, peers)
    inv_std = lax.rsqrt(squares / (cells * peers) + epsilon)
    gain, shift = columns(affine_ref[...], 0)
    scale_ref[...] = jnp.broadcast_to(gain * inv_std, scale_ref.shape)
    classes = head_ref.shape[1]
    class_id = lax.broadcasted_iota(jnp.int32, (classes, AREA), 0)
    sum_grad = jnp.zeros((192, 1), F32)
    sum_cross = jnp.zeros((192, 1), F32)
    for j in range(2):
        normed = (z_ref[j] - mean) * inv_std
        scaled = normed * gain + shift
        activated = jnp.where(scaled > 0, scaled, leak_slope * scaled)
        output = (own_ref[j, :192].astype(F32) + activated).astype(BF16)

        @pl.when(last)
        def head(output=output, j=j):
            logits = jnp.dot(head_turned_ref[...], output, preferred_element_type=F32)
            raised = jnp.exp(logits - jnp.max(logits, axis=0, keepdims=True))
            prob = raised / jnp.sum(raised, axis=0, keepdims=True)
            hot = jnp.where(class_id == label_ref[j : j + 1, :], 1.0, 0.0)
            delta = (prob - hot).astype(BF16)
            head_cot_ref[j] = jnp.dot(head_ref[...], delta, preferred_element_type=F32)

        @pl.when(jnp.logical_not(last))
        def given(j=j):
            head_cot_ref[j] = out_cot_ref[j].astype(F32)

        upstream = head_cot_ref[j] + jnp.where(decoder, 0.0, skip_cot_ref[j].astype(F32))
        grad_act = upstream * jnp.where(scaled > 0, 1.0, leak_slope)
        up_ref[j] = upstream
        for k, part in enumerate((grad_act.astype(BF16), normed.astype(BF16))):
            for ref in shares:
                ref[2 * j + k] = part
        sum_grad = sum_grad + jnp.sum(grad_act, axis=1, keepdims=True)
        sum_cross = sum_cross + jnp.sum(grad_act * normed, axis=1, keepdims=True)
    tile = packed_tile([sum_grad, sum_cross])
    send_ref[...] = jnp.broadcast_to(tile[None, : send_ref.shape[1]], send_ref.shape)


def forward_out(
    recv_ref, z_ref, own_ref, affine_ref, share_ref, out_ref, rim_low_ref, rim_high_ref, mix_ref
):
    rim_high_ref[...] = share_ref[:2]
    rim_low_ref[...] = share_ref[2:4]
    peers = recv_ref.shape[0]
    cells = 2.0 * AREA
    mean, squares = spread_sums(recv_ref[...], 1, cells, peers)
    inv_std = lax.rsqrt(squares / (cells * peers) + epsilon)
    gain, shift = columns(affine_ref[...], 0)
    for j in range(2):
        scaled = (z_ref[2 + j] - mean) * inv_std * gain + shift
        activated = jnp.where(scaled > 0, scaled, leak_slope * scaled)
        mix_ref[pl.ds(j, 192, stride=2), :] = own_ref[j, 192:].astype(F32) + activated
    out_ref[...] = mix_ref[...].astype(BF16)


def row_taps(refs, taps_ref, wide_ref, turned_ref):
    masks = tap_masks()
    for peer, ref in enumerate(refs):
        for q in range(4):
            wide_ref[...] = ref[4, 48 * q : 48 * q + 48].astype(F32)
            for r in range(6):
                turned_ref[8 * r : 8 * r + 8, :] = wide_ref[pl.ds(r, 8, stride=6), :]
            plane = turned_ref[...].astype(BF16)
            for b in range(3):
                for c in range(3):
                    view = shifted(plane, b, c, masks)
                    for a in range(3):
                        j = q - a
                        if 0 <= j < 2:
                            tap = 9 * a + 3 * b + c
                            lanes = (2 * peer + j) * AREA
                            taps_ref[tap * 48 : (tap + 1) * 48, lanes : lanes + AREA] = view


def kernel_grads(
    recv_ref,
    own_ref,
    a_ref,
    b_ref,
    c_ref,
    scale_ref,
    out_ref,
    shift_grad_ref,
    gain_grad_ref,
    taps_ref,
    gz_ref,
    low_ref,
    rest_ref,
    wide_ref,
    turned_ref,
):
    row_taps((own_ref, a_ref, b_ref, c_ref), taps_ref, wide_ref, turned_ref)
    total_cells = 2.0 * AREA * recv_ref.shape[0]
    total = full_tile(jnp.sum(recv_ref[...], axis=0))
    whole = total * (total_cells ** (-0.5))
    shift_grad_ref[...] = jnp.concatenate([whole[:1], whole[2:3, :64]], axis=1)
    gain_grad_ref[...] = jnp.concatenate([whole[1:2], whole[2:3, 64:]], axis=1)
    sum_grad, sum_cross = (col / total_cells for col in columns(total, 0))
    scale = scale_ref[...]
    for peer, ref in enumerate((own_ref, a_ref, b_ref, c_ref)):
        for j in range(2):
            act = ref[2 * j].astype(F32)
            normed = ref[2 * j + 1].astype(F32)
            lanes = (2 * peer + j) * AREA
            gz_ref[:, lanes : lanes + AREA] = (
                scale * (act - sum_grad - normed * sum_cross)
            ).astype(BF16)
    grads = lax.dot_general(
        taps_ref[...], gz_ref[...], (((1,), (1,)), ((), ())), preferred_element_type=F32
    )
    low_ref[...] = grads[:, :128]
    rest_ref[...] = jnp.concatenate([grads[:648, 128:], grads[648:, 128:]], axis=1)
    pad = jnp.zeros((5, AREA), F32)
    for z in range(8):
        first = low_ref[pl.ds(z, 162, stride=8), :]
        second = rest_ref[pl.ds(z, 81, stride=8), :]
        out_ref[z] = jnp.concatenate([first, second, pad], axis=0).astype(BF16)


def input_grads(
    flag_ref,
    w_ref,
    recv_ref,
    share_ref,
    up_ref,
    low_ref,
    high_ref,
    scale_ref,
    fwd_out_ref,
    grad_ref,
    skip_ref,
    x_ref,
    w_here_ref,
    mix_ref,
    sems,
):
    fetch = pltpu.make_async_copy(w_ref, w_here_ref, sems.at[0])
    fetch.start()
    decoder = flag_ref[0] == 1
    total_cells = 2.0 * AREA * recv_ref.shape[0]
    masks = tap_masks()
    total = full_tile(jnp.sum(recv_ref[...], axis=0))
    sum_grad, sum_cross = (col / total_cells for col in columns(total, 0))
    scale = scale_ref[...]
    acts = [low_ref[0], share_ref[0], share_ref[2], high_ref[0]]
    norms = [low_ref[1], share_ref[1], share_ref[3], high_ref[1]]
    for q in range(4):
        grad_z = scale * (acts[q].astype(F32) - sum_grad - norms[q].astype(F32) * sum_cross)
        if q == 0:
            grad_z = jnp.where(flag_ref[2] == 1, grad_z, 0.0)
        if q == 3:
            grad_z = jnp.where(flag_ref[3] == 1, grad_z, 0.0)
        grad_z = grad_z.astype(BF16)
        for b in range(3):
            for c in range(3):
                view = shifted(grad_z, 2 - b, 2 - c, masks)
                for a in range(3):
                    j = q + a - 2
                    if 0 <= j < 2:
                        tap = 9 * a + 3 * b + c
                        x_ref[tap * 192 : (tap + 1) * 192, j * AREA : (j + 1) * AREA] = view
    fetch.wait()
    back = jnp.dot(w_here_ref[...], x_ref[...], preferred_element_type=F32)
    for j in range(2):
        mix_ref[pl.ds(j, 192, stride=2), :] = up_ref[j] + back[:, j * AREA : (j + 1) * AREA]
    grad = mix_ref[...]
    grad_ref[...] = grad.astype(BF16)
    skip_ref[...] = jnp.where(decoder, grad, fwd_out_ref[...].astype(F32)).astype(BF16)


def hand_over(one_ref, two_ref, three_ref, out_one_ref, out_two_ref, out_three_ref):
    out_one_ref[...] = one_ref[...]
    out_two_ref[...] = two_ref[...]
    out_three_ref[...] = three_ref[...]


def sum_rows(scale_out, recv_ref, out_ref, wide_ref):
    total = jnp.sum(recv_ref[...].astype(F32), axis=0) * scale_out
    rest = jnp.concatenate([total[162:243, :64], total[162:243, 64:]], axis=0)

    def block(tap):
        rows = slice(6 * tap, 6 * tap + 6)
        return [total[rows], rest[rows]]

    for tap in range(0, TAPS, 2):
        parts = block(tap) + (block(tap + 1) if tap + 1 < TAPS else [])
        width = 192 if tap + 1 == TAPS else 384
        wide_ref[0:6, tap * 192 : tap * 192 + width] = jnp.concatenate(parts, axis=1)
    for r in range(6):
        out_ref[r] = wide_ref[r : r + 1, :]


def pair_rows(one, two):
    rest = jnp.concatenate([one[:, 128:], two[:, 128:]], axis=1)
    return jnp.concatenate([one[:, :128], two[:, :128], rest], axis=0)


def moved(block, axis, distance):
    count = lax.axis_size(axis)
    route = [(i, (i + distance) % count) for i in range(count)]
    return lax.ppermute(block, axis, route)


def per_device(
    fwd_input,
    fwd_skip,
    bwd_input,
    bwd_skip,
    out_cot,
    skip_cot,
    kernel,
    norm_gain,
    norm_shift,
    head_weight,
    labels,
):
    segments = lax.axis_size("segment")
    slabs = lax.axis_size("y") * lax.axis_size("z")
    segment_id = lax.axis_index("segment")
    y_id = lax.axis_index("y")
    slab_id = y_id * lax.axis_size("z") + lax.axis_index("z")
    is_decoder = segment_id * 2 >= segments
    flags = jnp.stack(
        [
            is_decoder.astype(jnp.int32),
            (segment_id == segments - 1).astype(jnp.int32),
            (slab_id > 0).astype(jnp.int32),
            (slab_id < slabs - 1).astype(jnp.int32),
            y_id.astype(jnp.int32),
        ]
    )
    kernel_mat = kernel[0]
    affine = pair_rows(norm_gain, norm_shift)

    def by_plane(block):
        return jnp.swapaxes(block[0], 0, 1)

    def joined(block, skip):
        added = (block.astype(F32) + skip.astype(F32)).astype(BF16)
        return by_plane(jnp.where(is_decoder, added, block))

    own = jnp.concatenate([joined(bwd_input, bwd_skip), joined(fwd_input, fwd_skip)], axis=1)
    low = moved(own[1], SLABS, 1)
    high = moved(own[0], SLABS, -1)
    (turned,) = call(
        turn_weights,
        [((192, 5184), BF16)],
        [((192, 5184), BF16)],
        0,
        4 * 192 * 5184,
        kernel_mat,
        hbm=1,
        limit=52,
    )
    z, stats_send = call(
        conv_both,
        [((4, 192, AREA), F32), ((slabs, 6, AREA), F32)],
        [((5184, 512), BF16)],
        2 * 5184 * 192 * 512,
        5000000,
        flags,
        own,
        low,
        high,
        turned,
        smem=1,
    )
    stats = lax.all_to_all(stats_send, SLABS, 0, 0, tiled=True)
    out_cots = by_plane(out_cot)
    skip_cots = by_plane(skip_cot)
    upstream, *shares, scale, sums_send = call(
        head_and_sums,
        [
            ((2, 192, AREA), F32),
            *[((5, 192, AREA), BF16)] * 4,
            ((192, AREA), F32),
            ((slabs, 4, AREA), F32),
        ],
        HEAD_SCRATCH,
        4 * 192 * 105 * 512,
        4000000,
        flags,
        z,
        stats,
        own,
        low,
        high,
        out_cots,
        skip_cots,
        labels,
        affine,
        head_weight,
        head_weight.T,
        smem=1,
    )
    sums = lax.all_to_all(sums_send, SLABS, 0, 0, tiled=True)
    share = shares[0]
    shares = [share] + [moved(shares[d], "y", d) for d in (1, 2, 3)]
    fwd_out, rim_low, rim_high = call(
        forward_out,
        [((384, AREA), BF16), ((2, 192, AREA), BF16), ((2, 192, AREA), BF16)],
        [((384, AREA), F32)],
        0,
        1000000,
        stats,
        z,
        own,
        affine,
        share,
    )
    rim_low = moved(rim_low, SLABS, 1)
    rim_high = moved(rim_high, SLABS, -1)
    sums, fwd_out = lax.optimization_barrier((sums, fwd_out))
    parts, shift_grad, gain_grad = call(
        kernel_grads,
        [((8, 248, AREA), BF16), ((1, 192), F32), ((1, 192), F32)],
        [
            ((1296, 1024), BF16),
            ((192, 1024), BF16),
            ((1296, AREA), F32),
            ((648, AREA), F32),
            ((48, AREA), F32),
            ((48, AREA), F32),
        ],
        0,
        1000,
        sums,
        *shares,
        scale,
    )
    parts, rim_low, rim_high = lax.optimization_barrier((parts, rim_low, rim_high))
    summed = lax.all_to_all(parts, "z", 0, 0, tiled=True)
    grad_joined, outgoing = call(
        input_grads,
        [((384, AREA), BF16)] * 2,
        [((5184, 256), BF16), ((192, 5184), BF16), ((384, AREA), F32)],
        2 * 5184 * 192 * 256,
        4000000,
        flags,
        kernel_mat,
        sums,
        share,
        upstream,
        rim_low,
        rim_high,
        scale,
        fwd_out,
        smem=1,
        hbm=1,
        limit=52,
    )
    fwd_out, grad_joined, outgoing = lax.optimization_barrier((fwd_out, grad_joined, outgoing))
    prev_block = moved(grad_joined, "segment", -1)
    next_block = moved(fwd_out, "segment", 1)
    mirrored = lax.ppermute(outgoing, "segment", [(i, segments - 1 - i) for i in range(segments)])
    total_cells = float(2 * slabs * AREA)

    def by_channel(block):
        return block.reshape(1, 192, 2, AREA)

    blocks = call(
        hand_over,
        [((384, AREA), BF16)] * 3,
        [],
        0,
        600000,
        next_block,
        prev_block,
        mirrored,
    )
    handed = [by_channel(block) for block in blocks]
    (kernel_grad,) = call(
        functools.partial(sum_rows, total_cells ** (-0.5)),
        [((6, 1, 5184), F32)],
        [((8, 5184), F32)],
        0,
        1000000,
        summed,
    )
    return (
        *handed,
        jnp.swapaxes(kernel_grad, 0, 1),
        gain_grad,
        shift_grad,
    )


def solution(mesh):
    grid = Mesh(mesh.devices.reshape(mesh.devices.shape[0], 4, 8), ("segment", "y", "z"))
    field = P("segment", None, SLABS, None)
    in_specs = (field,) * 6 + (
        P("segment", None, None),
        P("segment", None),
        P("segment", None),
        P(),
        P(SLABS, None),
    )
    out_specs = (
        field,
        field,
        field,
        P("segment", SLABS, None),
        P("segment", None),
        P("segment", None),
    )
    return jax.shard_map(
        per_device, mesh=grid, in_specs=in_specs, out_specs=out_specs, check_vma=False
    )
```

```python
import functools

import jax
import jax.numpy as jnp
from jax import lax
from jax.experimental import pallas as pl
from jax.experimental.pallas import tpu as pltpu
from jax.sharding import Mesh
from jax.sharding import PartitionSpec as P

ROWS = 8
COLS = 16
AREA = ROWS * COLS
TAPS = 27
SLABS = ("y", "z")

epsilon = 1e-05
leak_slope = 0.01

F32 = jnp.float32
BF16 = jnp.bfloat16
HBM = pl.BlockSpec(memory_space=pltpu.HBM)
VMEM = pl.BlockSpec(memory_space=pltpu.VMEM)
SMEM = pl.BlockSpec(memory_space=pltpu.SMEM)


HEAD_SCRATCH = [((2, 192, AREA), F32)]


def call(body, outs, scratch, flops, moved, *args, smem=0, hbm=0, limit=24):
    specs = [SMEM] * smem + [HBM] * hbm + [VMEM] * (len(args) - smem - hbm)
    shapes = [jax.ShapeDtypeStruct(shape, kind) for shape, kind in outs]
    places = [pltpu.VMEM(shape, kind) for shape, kind in scratch]
    return pl.pallas_call(
        body,
        out_shape=shapes,
        in_specs=specs,
        out_specs=[VMEM] * len(outs),
        scratch_shapes=places + [pltpu.SemaphoreType.DMA((4,))] * (hbm > 0),
        compiler_params=pltpu.CompilerParams(vmem_limit_bytes=limit * 1024 * 1024),
        cost_estimate=pl.CostEstimate(flops=flops, bytes_accessed=moved, transcendentals=0),
        name=getattr(body, "__name__", "kernel"),
    )(*args)


def tap_masks():
    cell = lax.broadcasted_iota(jnp.int32, (1, AREA), 1)
    row = cell // COLS
    col = cell % COLS
    masks = {}
    for b in range(3):
        for c in range(3):
            inside = None
            if b != 1:
                inside = row > 0 if b == 0 else row < ROWS - 1
            if c != 1:
                part = col > 0 if c == 0 else col < COLS - 1
                inside = part if inside is None else jnp.logical_and(inside, part)
            masks[(b, c)] = inside
    return masks


def shifted(plane, b, c, masks):
    step = (b - 1) * COLS + (c - 1)
    if step == 0:
        return plane
    moved = pltpu.roll(plane, (-step) % AREA, 1)
    return jnp.where(masks[(b, c)], moved, jnp.zeros_like(moved))


def full_tile(tile):
    if tile.shape[0] == 8:
        return tile
    return jnp.concatenate([tile, jnp.zeros((8 - tile.shape[0], AREA), F32)], axis=0)


def columns(tile, pair):
    square = jnp.concatenate([full_tile(tile), jnp.zeros((AREA - 8, AREA), F32)], axis=0).T
    row = 3 * pair
    rest = square[:, row + 2 : row + 3]
    first = jnp.concatenate([square[:, row : row + 1], rest[:64]], axis=0)
    second = jnp.concatenate([square[:, row + 1 : row + 2], rest[64:]], axis=0)
    return first, second


def packed_tile(cols):
    lane = lax.broadcasted_iota(jnp.int32, (AREA, AREA), 1)
    square = jnp.zeros((AREA, AREA), F32)
    for pair in range(len(cols) // 2):
        one, two = cols[2 * pair], cols[2 * pair + 1]
        rest = jnp.concatenate([one[128:], two[128:]], axis=0)
        for k, col in enumerate((one[:128], two[:128], rest)):
            square = jnp.where(lane == 3 * pair + k, col, square)
    return square.T[:8]


def spread_sums(received, pair, cells, peers):
    total = jnp.sum(received, axis=0)
    apart = jnp.sum(jnp.square(received - (total / peers)[None]), axis=0)
    mean, squares = columns(total, pair)
    return mean / peers, squares + cells * columns(apart, pair)[0]


def local_stats(planes_out, cells):
    mean = sum(jnp.sum(p, axis=1, keepdims=True) for p in planes_out) / cells
    squares = sum(jnp.sum(jnp.square(p - mean), axis=1, keepdims=True) for p in planes_out)
    return [mean, squares]


def turn_weights(w_ref, out_ref, here_ref, sems):
    bounds = (0, 4, 8, 12, 14)
    copies = []
    for part in range(4):
        start = bounds[part] * 384
        band = pl.ds(start, min(bounds[part + 1] * 384, 5184) - start)
        copies.append(
            pltpu.make_async_copy(w_ref.at[:, band], here_ref.at[:, band], sems.at[part])
        )
        copies[part].start()
    for part in range(4):
        copies[part].wait()
        for pair in range(bounds[part], bounds[part + 1]):
            width = 384 if pair < 13 else 192
            block = here_ref[:, pair * 384 : pair * 384 + width].T
            if width == 384:
                block = jnp.concatenate([block[:192], block[192:]], axis=1)
            out_ref[:, pair * 384 : pair * 384 + width] = block


def fill_taps(planes, outputs, x_ref, masks, channels, first):
    for q, plane in enumerate(planes):
        for b in range(3):
            for c in range(3):
                view = shifted(plane, b, c, masks)
                for a in range(3):
                    j = q - a
                    if 0 <= j < outputs:
                        tap = 9 * a + 3 * b + c
                        lanes = (first + j) * AREA
                        x_ref[
                            tap * channels : (tap + 1) * channels, lanes : lanes + AREA
                        ] = view


def conv_both(own_ref, low_ref, high_ref, wt_ref, z_ref, send_ref, x_ref):
    masks = tap_masks()
    for which in range(2):
        rows = slice(192 * which, 192 * which + 192)
        planes = [low_ref[rows], own_ref[0, rows], own_ref[1, rows], high_ref[rows]]
        fill_taps(planes, 2, x_ref, masks, 192, 2 * which)
    z = jnp.dot(wt_ref[...], x_ref[...], preferred_element_type=F32)
    outs = [z[:, j * AREA : (j + 1) * AREA] for j in range(4)]
    for j in range(4):
        z_ref[j] = outs[j]
    tile = packed_tile(
        local_stats(outs[:2], 2.0 * AREA) + local_stats(outs[2:], 2.0 * AREA)
    )
    send_ref[...] = jnp.broadcast_to(tile[None, : send_ref.shape[1]], send_ref.shape)


def head_and_sums(
    flag_ref,
    z_ref,
    recv_ref,
    own_ref,
    low_ref,
    high_ref,
    out_cot_ref,
    skip_cot_ref,
    label_ref,
    affine_ref,
    head_ref,
    head_turned_ref,
    up_ref,
    share_ref,
    share_a_ref,
    share_b_ref,
    share_c_ref,
    scale_ref,
    send_ref,
    head_cot_ref,
):
    shares = (share_ref, share_a_ref, share_b_ref, share_c_ref)
    for distance, ref in enumerate(shares):
        rows = pl.ds(pl.multiple_of(48 * ((flag_ref[4] + distance) % 4), 16), 48)
        ref[4, :48] = low_ref[rows]
        ref[4, 48:96] = own_ref[0, rows]
        ref[4, 96:144] = own_ref[1, rows]
        ref[4, 144:] = high_ref[rows]
    decoder = flag_ref[0] == 1
    last = flag_ref[1] == 1
    peers = recv_ref.shape[0]
    cells = 2.0 * AREA
    mean, squares = spread_sums(recv_ref[...], 0, cells, peers)
    inv_std = lax.rsqrt(squares / (cells * peers) + epsilon)
    gain, shift = columns(affine_ref[...], 0)
    scale_ref[...] = jnp.broadcast_to(gain * inv_std, scale_ref.shape)
    classes = head_ref.shape[1]
    class_id = lax.broadcasted_iota(jnp.int32, (classes, AREA), 0)
    sum_grad = jnp.zeros((192, 1), F32)
    sum_cross = jnp.zeros((192, 1), F32)
    for j in range(2):
        normed = (z_ref[j] - mean) * inv_std
        scaled = normed * gain + shift
        activated = jnp.where(scaled > 0, scaled, leak_slope * scaled)
        output = (own_ref[j, :192].astype(F32) + activated).astype(BF16)

        @pl.when(last)
        def head(output=output, j=j):
            logits = jnp.dot(head_turned_ref[...], output, preferred_element_type=F32)
            raised = jnp.exp(logits - jnp.max(logits, axis=0, keepdims=True))
            prob = raised / jnp.sum(raised, axis=0, keepdims=True)
            hot = jnp.where(class_id == label_ref[j : j + 1, :], 1.0, 0.0)
            delta = (prob - hot).astype(BF16)
            head_cot_ref[j] = jnp.dot(head_ref[...], delta, preferred_element_type=F32)

        @pl.when(jnp.logical_not(last))
        def given(j=j):
            head_cot_ref[j] = out_cot_ref[j].astype(F32)

        upstream = head_cot_ref[j] + jnp.where(decoder, 0.0, skip_cot_ref[j].astype(F32))
        grad_act = upstream * jnp.where(scaled > 0, 1.0, leak_slope)
        up_ref[j] = upstream
        for k, part in enumerate((grad_act.astype(BF16), normed.astype(BF16))):
            for ref in shares:
                ref[2 * j + k] = part
        sum_grad = sum_grad + jnp.sum(grad_act, axis=1, keepdims=True)
        sum_cross = sum_cross + jnp.sum(grad_act * normed, axis=1, keepdims=True)
    tile = packed_tile([sum_grad, sum_cross])
    send_ref[...] = jnp.broadcast_to(tile[None, : send_ref.shape[1]], send_ref.shape)


def forward_out(
    recv_ref, z_ref, own_ref, affine_ref, share_ref, out_ref, rim_low_ref, rim_high_ref, mix_ref
):
    rim_high_ref[...] = share_ref[:2]
    rim_low_ref[...] = share_ref[2:4]
    peers = recv_ref.shape[0]
    cells = 2.0 * AREA
    mean, squares = spread_sums(recv_ref[...], 1, cells, peers)
    inv_std = lax.rsqrt(squares / (cells * peers) + epsilon)
    gain, shift = columns(affine_ref[...], 0)
    for j in range(2):
        scaled = (z_ref[2 + j] - mean) * inv_std * gain + shift
        activated = jnp.where(scaled > 0, scaled, leak_slope * scaled)
        mix_ref[pl.ds(j, 192, stride=2), :] = own_ref[j, 192:].astype(F32) + activated
    out_ref[...] = mix_ref[...].astype(BF16)


def row_taps(refs, taps_ref, wide_ref, turned_ref):
    masks = tap_masks()
    for peer, ref in enumerate(refs):
        for q in range(4):
            wide_ref[...] = ref[4, 48 * q : 48 * q + 48].astype(F32)
            for r in range(6):
                turned_ref[8 * r : 8 * r + 8, :] = wide_ref[pl.ds(r, 8, stride=6), :]
            plane = turned_ref[...].astype(BF16)
            for b in range(3):
                for c in range(3):
                    view = shifted(plane, b, c, masks)
                    for a in range(3):
                        j = q - a
                        if 0 <= j < 2:
                            tap = 9 * a + 3 * b + c
                            lanes = (2 * peer + j) * AREA
                            taps_ref[tap * 48 : (tap + 1) * 48, lanes : lanes + AREA] = view


def kernel_grads(
    recv_ref,
    own_ref,
    a_ref,
    b_ref,
    c_ref,
    scale_ref,
    out_ref,
    shift_grad_ref,
    gain_grad_ref,
    taps_ref,
    gz_ref,
    low_ref,
    rest_ref,
    wide_ref,
    turned_ref,
):
    row_taps((own_ref, a_ref, b_ref, c_ref), taps_ref, wide_ref, turned_ref)
    total_cells = 2.0 * AREA * recv_ref.shape[0]
    total = full_tile(jnp.sum(recv_ref[...], axis=0))
    whole = total * (total_cells ** (-0.5))
    shift_grad_ref[...] = jnp.concatenate([whole[:1], whole[2:3, :64]], axis=1)
    gain_grad_ref[...] = jnp.concatenate([whole[1:2], whole[2:3, 64:]], axis=1)
    sum_grad, sum_cross = (col / total_cells for col in columns(total, 0))
    scale = scale_ref[...]
    for peer, ref in enumerate((own_ref, a_ref, b_ref, c_ref)):
        for j in range(2):
            act = ref[2 * j].astype(F32)
            normed = ref[2 * j + 1].astype(F32)
            lanes = (2 * peer + j) * AREA
            gz_ref[:, lanes : lanes + AREA] = (
                scale * (act - sum_grad - normed * sum_cross)
            ).astype(BF16)
    grads = lax.dot_general(
        taps_ref[...], gz_ref[...], (((1,), (1,)), ((), ())), preferred_element_type=F32
    )
    low_ref[...] = grads[:, :128]
    rest_ref[...] = jnp.concatenate([grads[:648, 128:], grads[648:, 128:]], axis=1)
    pad = jnp.zeros((5, AREA), F32)
    for z in range(8):
        first = low_ref[pl.ds(z, 162, stride=8), :]
        second = rest_ref[pl.ds(z, 81, stride=8), :]
        out_ref[z] = jnp.concatenate([first, second, pad], axis=0).astype(BF16)


def input_grads(
    flag_ref,
    w_ref,
    recv_ref,
    share_ref,
    up_ref,
    low_ref,
    high_ref,
    scale_ref,
    fwd_out_ref,
    grad_ref,
    skip_ref,
    x_ref,
    w_here_ref,
    mix_ref,
    sems,
):
    fetch = pltpu.make_async_copy(w_ref, w_here_ref, sems.at[0])
    fetch.start()
    decoder = flag_ref[0] == 1
    total_cells = 2.0 * AREA * recv_ref.shape[0]
    masks = tap_masks()
    total = full_tile(jnp.sum(recv_ref[...], axis=0))
    sum_grad, sum_cross = (col / total_cells for col in columns(total, 0))
    scale = scale_ref[...]
    acts = [low_ref[0], share_ref[0], share_ref[2], high_ref[0]]
    norms = [low_ref[1], share_ref[1], share_ref[3], high_ref[1]]
    for q in range(4):
        grad_z = scale * (acts[q].astype(F32) - sum_grad - norms[q].astype(F32) * sum_cross)
        if q == 0:
            grad_z = jnp.where(flag_ref[2] == 1, grad_z, 0.0)
        if q == 3:
            grad_z = jnp.where(flag_ref[3] == 1, grad_z, 0.0)
        grad_z = grad_z.astype(BF16)
        for b in range(3):
            for c in range(3):
                view = shifted(grad_z, 2 - b, 2 - c, masks)
                for a in range(3):
                    j = q + a - 2
                    if 0 <= j < 2:
                        tap = 9 * a + 3 * b + c
                        x_ref[tap * 192 : (tap + 1) * 192, j * AREA : (j + 1) * AREA] = view
    fetch.wait()
    back = jnp.dot(w_here_ref[...], x_ref[...], preferred_element_type=F32)
    for j in range(2):
        mix_ref[pl.ds(j, 192, stride=2), :] = up_ref[j] + back[:, j * AREA : (j + 1) * AREA]
    grad = mix_ref[...]
    grad_ref[...] = grad.astype(BF16)
    skip_ref[...] = jnp.where(decoder, grad, fwd_out_ref[...].astype(F32)).astype(BF16)


def hand_over(one_ref, two_ref, three_ref, out_one_ref, out_two_ref, out_three_ref):
    out_one_ref[...] = one_ref[...]
    out_two_ref[...] = two_ref[...]
    out_three_ref[...] = three_ref[...]


def sum_rows(scale_out, recv_ref, out_ref, wide_ref):
    total = jnp.sum(recv_ref[...].astype(F32), axis=0) * scale_out
    rest = jnp.concatenate([total[162:243, :64], total[162:243, 64:]], axis=0)

    def block(tap):
        rows = slice(6 * tap, 6 * tap + 6)
        return [total[rows], rest[rows]]

    for tap in range(0, TAPS, 2):
        parts = block(tap) + (block(tap + 1) if tap + 1 < TAPS else [])
        width = 192 if tap + 1 == TAPS else 384
        wide_ref[0:6, tap * 192 : tap * 192 + width] = jnp.concatenate(parts, axis=1)
    for r in range(6):
        out_ref[r] = wide_ref[r : r + 1, :]


def pair_rows(one, two):
    rest = jnp.concatenate([one[:, 128:], two[:, 128:]], axis=1)
    return jnp.concatenate([one[:, :128], two[:, :128], rest], axis=0)


def moved(block, axis, distance):
    count = lax.axis_size(axis)
    route = [(i, (i + distance) % count) for i in range(count)]
    return lax.ppermute(block, axis, route)


def per_device(
    fwd_input,
    fwd_skip,
    bwd_input,
    bwd_skip,
    out_cot,
    skip_cot,
    kernel,
    norm_gain,
    norm_shift,
    head_weight,
    labels,
):
    segments = lax.axis_size("segment")
    slabs = lax.axis_size("y") * lax.axis_size("z")
    segment_id = lax.axis_index("segment")
    y_id = lax.axis_index("y")
    slab_id = y_id * lax.axis_size("z") + lax.axis_index("z")
    is_decoder = segment_id * 2 >= segments
    flags = jnp.stack(
        [
            is_decoder.astype(jnp.int32),
            (segment_id == segments - 1).astype(jnp.int32),
            (slab_id > 0).astype(jnp.int32),
            (slab_id < slabs - 1).astype(jnp.int32),
            y_id.astype(jnp.int32),
        ]
    )
    kernel_mat = kernel[0]
    affine = pair_rows(norm_gain, norm_shift)

    def by_plane(block):
        return jnp.swapaxes(block[0], 0, 1)

    def joined(block, skip):
        added = (block.astype(F32) + skip.astype(F32)).astype(BF16)
        return by_plane(jnp.where(is_decoder, added, block))

    own = jnp.concatenate([joined(bwd_input, bwd_skip), joined(fwd_input, fwd_skip)], axis=1)
    nothing = jnp.zeros_like(own[0])
    low = moved(jnp.where(slab_id < slabs - 1, own[1], nothing), SLABS, 1)
    high = moved(jnp.where(slab_id > 0, own[0], nothing), SLABS, -1)
    (turned,) = call(
        turn_weights,
        [((192, 5184), BF16)],
        [((192, 5184), BF16)],
        0,
        4 * 192 * 5184,
        kernel_mat,
        hbm=1,
        limit=52,
    )
    z, stats_send = call(
        conv_both,
        [((4, 192, AREA), F32), ((slabs, 6, AREA), F32)],
        [((5184, 512), BF16)],
        2 * 5184 * 192 * 512,
        5000000,
        own,
        low,
        high,
        turned,
    )
    stats = lax.all_to_all(stats_send, SLABS, 0, 0, tiled=True)
    out_cots = by_plane(out_cot)
    skip_cots = by_plane(skip_cot)
    upstream, *shares, scale, sums_send = call(
        head_and_sums,
        [
            ((2, 192, AREA), F32),
            *[((5, 192, AREA), BF16)] * 4,
            ((192, AREA), F32),
            ((slabs, 4, AREA), F32),
        ],
        HEAD_SCRATCH,
        4 * 192 * 105 * 512,
        4000000,
        flags,
        z,
        stats,
        own,
        low,
        high,
        out_cots,
        skip_cots,
        labels,
        affine,
        head_weight,
        head_weight.T,
        smem=1,
    )
    sums = lax.all_to_all(sums_send, SLABS, 0, 0, tiled=True)
    share = shares[0]
    shares = [share] + [moved(shares[d], "y", d) for d in (1, 2, 3)]
    fwd_out, rim_low, rim_high = call(
        forward_out,
        [((384, AREA), BF16), ((2, 192, AREA), BF16), ((2, 192, AREA), BF16)],
        [((384, AREA), F32)],
        0,
        1000000,
        stats,
        z,
        own,
        affine,
        share,
    )
    rim_low = moved(rim_low, SLABS, 1)
    rim_high = moved(rim_high, SLABS, -1)
    sums, fwd_out = lax.optimization_barrier((sums, fwd_out))
    parts, shift_grad, gain_grad = call(
        kernel_grads,
        [((8, 248, AREA), BF16), ((1, 192), F32), ((1, 192), F32)],
        [
            ((1296, 1024), BF16),
            ((192, 1024), BF16),
            ((1296, AREA), F32),
            ((648, AREA), F32),
            ((48, AREA), F32),
            ((48, AREA), F32),
        ],
        0,
        1000,
        sums,
        *shares,
        scale,
    )
    parts, rim_low, rim_high = lax.optimization_barrier((parts, rim_low, rim_high))
    summed = lax.all_to_all(parts, "z", 0, 0, tiled=True)
    grad_joined, outgoing = call(
        input_grads,
        [((384, AREA), BF16)] * 2,
        [((5184, 256), BF16), ((192, 5184), BF16), ((384, AREA), F32)],
        2 * 5184 * 192 * 256,
        4000000,
        flags,
        kernel_mat,
        sums,
        share,
        upstream,
        rim_low,
        rim_high,
        scale,
        fwd_out,
        smem=1,
        hbm=1,
        limit=52,
    )
    fwd_out, grad_joined, outgoing = lax.optimization_barrier((fwd_out, grad_joined, outgoing))
    prev_block = moved(grad_joined, "segment", -1)
    next_block = moved(fwd_out, "segment", 1)
    mirrored = lax.ppermute(outgoing, "segment", [(i, segments - 1 - i) for i in range(segments)])
    total_cells = float(2 * slabs * AREA)

    def by_channel(block):
        return block.reshape(1, 192, 2, AREA)

    blocks = call(
        hand_over,
        [((384, AREA), BF16)] * 3,
        [],
        0,
        600000,
        next_block,
        prev_block,
        mirrored,
    )
    handed = [by_channel(block) for block in blocks]
    (kernel_grad,) = call(
        functools.partial(sum_rows, total_cells ** (-0.5)),
        [((6, 1, 5184), F32)],
        [((8, 5184), F32)],
        0,
        1000000,
        summed,
    )
    return (
        *handed,
        jnp.swapaxes(kernel_grad, 0, 1),
        gain_grad,
        shift_grad,
    )


def solution(mesh):
    grid = Mesh(mesh.devices.reshape(mesh.devices.shape[0], 4, 8), ("segment", "y", "z"))
    field = P("segment", None, SLABS, None)
    in_specs = (field,) * 6 + (
        P("segment", None, None),
        P("segment", None),
        P("segment", None),
        P(),
        P(SLABS, None),
    )
    out_specs = (
        field,
        field,
        field,
        P("segment", SLABS, None),
        P("segment", None),
        P("segment", None),
    )
    return jax.shard_map(
        per_device, mesh=grid, in_specs=in_specs, out_specs=out_specs, check_vma=False
    )
```

```python
import functools

import jax
import jax.numpy as jnp
from jax import lax
from jax.experimental import pallas as pl
from jax.experimental.pallas import tpu as pltpu
from jax.sharding import Mesh
from jax.sharding import PartitionSpec as P

ROWS = 8
COLS = 16
AREA = ROWS * COLS
TAPS = 27
SLABS = ("y", "z")

epsilon = 1e-05
leak_slope = 0.01

F32 = jnp.float32
BF16 = jnp.bfloat16
HBM = pl.BlockSpec(memory_space=pltpu.HBM)
VMEM = pl.BlockSpec(memory_space=pltpu.VMEM)
SMEM = pl.BlockSpec(memory_space=pltpu.SMEM)


HEAD_SCRATCH = [((2, 192, AREA), F32)]


def call(body, outs, scratch, flops, moved, *args, smem=0, hbm=0, limit=24):
    specs = [SMEM] * smem + [HBM] * hbm + [VMEM] * (len(args) - smem - hbm)
    shapes = [jax.ShapeDtypeStruct(shape, kind) for shape, kind in outs]
    places = [pltpu.VMEM(shape, kind) for shape, kind in scratch]
    return pl.pallas_call(
        body,
        out_shape=shapes,
        in_specs=specs,
        out_specs=[VMEM] * len(outs),
        scratch_shapes=places + [pltpu.SemaphoreType.DMA((4,))] * (hbm > 0),
        compiler_params=pltpu.CompilerParams(vmem_limit_bytes=limit * 1024 * 1024),
        cost_estimate=pl.CostEstimate(flops=flops, bytes_accessed=moved, transcendentals=0),
        name=getattr(body, "__name__", "kernel"),
    )(*args)


def tap_masks():
    cell = lax.broadcasted_iota(jnp.int32, (1, AREA), 1)
    row = cell // COLS
    col = cell % COLS
    masks = {}
    for b in range(3):
        for c in range(3):
            inside = None
            if b != 1:
                inside = row > 0 if b == 0 else row < ROWS - 1
            if c != 1:
                part = col > 0 if c == 0 else col < COLS - 1
                inside = part if inside is None else jnp.logical_and(inside, part)
            masks[(b, c)] = inside
    return masks


def shifted(plane, b, c, masks):
    step = (b - 1) * COLS + (c - 1)
    if step == 0:
        return plane
    moved = pltpu.roll(plane, (-step) % AREA, 1)
    return jnp.where(masks[(b, c)], moved, jnp.zeros_like(moved))


def full_tile(tile):
    if tile.shape[0] == 8:
        return tile
    return jnp.concatenate([tile, jnp.zeros((8 - tile.shape[0], AREA), F32)], axis=0)


def columns(tile, pair):
    square = jnp.concatenate([full_tile(tile), jnp.zeros((AREA - 8, AREA), F32)], axis=0).T
    row = 3 * pair
    rest = square[:, row + 2 : row + 3]
    first = jnp.concatenate([square[:, row : row + 1], rest[:64]], axis=0)
    second = jnp.concatenate([square[:, row + 1 : row + 2], rest[64:]], axis=0)
    return first, second


def packed_tile(cols):
    lane = lax.broadcasted_iota(jnp.int32, (AREA, AREA), 1)
    square = jnp.zeros((AREA, AREA), F32)
    for pair in range(len(cols) // 2):
        one, two = cols[2 * pair], cols[2 * pair + 1]
        rest = jnp.concatenate([one[128:], two[128:]], axis=0)
        for k, col in enumerate((one[:128], two[:128], rest)):
            square = jnp.where(lane == 3 * pair + k, col, square)
    return square.T[:8]


def spread_sums(received, pair, cells, peers):
    total = jnp.sum(received, axis=0)
    apart = jnp.sum(jnp.square(received - (total / peers)[None]), axis=0)
    mean, squares = columns(total, pair)
    return mean / peers, squares + cells * columns(apart, pair)[0]


def local_stats(planes_out, cells):
    mean = sum(jnp.sum(p, axis=1, keepdims=True) for p in planes_out) / cells
    squares = sum(jnp.sum(jnp.square(p - mean), axis=1, keepdims=True) for p in planes_out)
    return [mean, squares]


def turn_weights(w_ref, out_ref, here_ref, sems):
    bounds = (0, 4, 8, 12, 14)
    copies = []
    for part in range(4):
        start = bounds[part] * 384
        band = pl.ds(start, min(bounds[part + 1] * 384, 5184) - start)
        copies.append(
            pltpu.make_async_copy(w_ref.at[:, band], here_ref.at[:, band], sems.at[part])
        )
        copies[part].start()
    for part in range(4):
        copies[part].wait()
        for pair in range(bounds[part], bounds[part + 1]):
            width = 384 if pair < 13 else 192
            block = here_ref[:, pair * 384 : pair * 384 + width].T
            if width == 384:
                block = jnp.concatenate([block[:192], block[192:]], axis=1)
            out_ref[:, pair * 384 : pair * 384 + width] = block


def fill_taps(planes, outputs, x_ref, masks, channels, first):
    for q, plane in enumerate(planes):
        for b in range(3):
            for c in range(3):
                view = shifted(plane, b, c, masks)
                for a in range(3):
                    j = q - a
                    if 0 <= j < outputs:
                        tap = 9 * a + 3 * b + c
                        lanes = (first + j) * AREA
                        x_ref[
                            tap * channels : (tap + 1) * channels, lanes : lanes + AREA
                        ] = view


def convolution(which, own_ref, low_ref, high_ref, wt_ref, z_ref, x_ref):
    rows = slice(192 * which, 192 * which + 192)
    planes = [low_ref[...], own_ref[0, rows], own_ref[1, rows], high_ref[...]]
    fill_taps(planes, 2, x_ref, tap_masks(), 192, 0)
    z = jnp.dot(wt_ref[...], x_ref[...], preferred_element_type=F32)
    outs = [z[:, :AREA], z[:, AREA:]]
    z_ref[0] = outs[0]
    z_ref[1] = outs[1]
    return local_stats(outs, 2.0 * AREA)


def conv_bwd(own_ref, low_ref, high_ref, wt_ref, z_ref, send_ref, x_ref):
    tile = packed_tile(convolution(0, own_ref, low_ref, high_ref, wt_ref, z_ref, x_ref))
    send_ref[...] = jnp.broadcast_to(tile[None, : send_ref.shape[1]], send_ref.shape)


def conv_fwd(own_ref, low_ref, high_ref, wt_ref, z_ref, tile_ref, x_ref):
    mean, squares = convolution(1, own_ref, low_ref, high_ref, wt_ref, z_ref, x_ref)
    tile_ref[...] = packed_tile([jnp.zeros_like(mean), jnp.zeros_like(mean), mean, squares])


def rims(share_ref, rim_low_ref, rim_high_ref):
    rim_high_ref[...] = share_ref[:2]
    rim_low_ref[...] = share_ref[2:4]


def head_and_sums(
    flag_ref,
    z_ref,
    recv_ref,
    own_ref,
    low_ref,
    high_ref,
    out_cot_ref,
    skip_cot_ref,
    label_ref,
    affine_ref,
    head_ref,
    head_turned_ref,
    fwd_tile_ref,
    up_ref,
    share_ref,
    share_a_ref,
    share_b_ref,
    share_c_ref,
    scale_ref,
    send_ref,
    head_cot_ref,
):
    shares = (share_ref, share_a_ref, share_b_ref, share_c_ref)
    for distance, ref in enumerate(shares):
        rows = pl.ds(pl.multiple_of(48 * ((flag_ref[4] + distance) % 4), 16), 48)
        ref[4, :48] = low_ref[rows]
        ref[4, 48:96] = own_ref[0, rows]
        ref[4, 96:144] = own_ref[1, rows]
        ref[4, 144:] = high_ref[rows]
    decoder = flag_ref[0] == 1
    last = flag_ref[1] == 1
    peers = recv_ref.shape[0]
    cells = 2.0 * AREA
    mean, squares = spread_sums(recv_ref[...], 0, cells, peers)
    inv_std = lax.rsqrt(squares / (cells * peers) + epsilon)
    gain, shift = columns(affine_ref[...], 0)
    scale_ref[...] = jnp.broadcast_to(gain * inv_std, scale_ref.shape)
    classes = head_ref.shape[1]
    class_id = lax.broadcasted_iota(jnp.int32, (classes, AREA), 0)
    sum_grad = jnp.zeros((192, 1), F32)
    sum_cross = jnp.zeros((192, 1), F32)
    for j in range(2):
        normed = (z_ref[j] - mean) * inv_std
        scaled = normed * gain + shift
        activated = jnp.where(scaled > 0, scaled, leak_slope * scaled)
        output = (own_ref[j, :192].astype(F32) + activated).astype(BF16)

        @pl.when(last)
        def head(output=output, j=j):
            logits = jnp.dot(head_turned_ref[...], output, preferred_element_type=F32)
            raised = jnp.exp(logits - jnp.max(logits, axis=0, keepdims=True))
            prob = raised / jnp.sum(raised, axis=0, keepdims=True)
            hot = jnp.where(class_id == label_ref[j : j + 1, :], 1.0, 0.0)
            delta = (prob - hot).astype(BF16)
            head_cot_ref[j] = jnp.dot(head_ref[...], delta, preferred_element_type=F32)

        @pl.when(jnp.logical_not(last))
        def given(j=j):
            head_cot_ref[j] = out_cot_ref[j].astype(F32)

        upstream = head_cot_ref[j] + jnp.where(decoder, 0.0, skip_cot_ref[j].astype(F32))
        grad_act = upstream * jnp.where(scaled > 0, 1.0, leak_slope)
        up_ref[j] = upstream
        for k, part in enumerate((grad_act.astype(BF16), normed.astype(BF16))):
            for ref in shares:
                ref[2 * j + k] = part
        sum_grad = sum_grad + jnp.sum(grad_act, axis=1, keepdims=True)
        sum_cross = sum_cross + jnp.sum(grad_act * normed, axis=1, keepdims=True)
    tile = packed_tile([sum_grad, sum_cross]) + fwd_tile_ref[...]
    send_ref[...] = jnp.broadcast_to(tile[None, : send_ref.shape[1]], send_ref.shape)


def forward_out(recv_ref, z_ref, own_ref, affine_ref, out_ref, mix_ref):
    peers = recv_ref.shape[0]
    cells = 2.0 * AREA
    mean, squares = spread_sums(recv_ref[...], 1, cells, peers)
    inv_std = lax.rsqrt(squares / (cells * peers) + epsilon)
    gain, shift = columns(affine_ref[...], 0)
    for j in range(2):
        scaled = (z_ref[j] - mean) * inv_std * gain + shift
        activated = jnp.where(scaled > 0, scaled, leak_slope * scaled)
        mix_ref[pl.ds(j, 192, stride=2), :] = own_ref[j, 192:].astype(F32) + activated
    out_ref[...] = mix_ref[...].astype(BF16)


def row_taps(refs, taps_ref, wide_ref, turned_ref):
    masks = tap_masks()
    for peer, ref in enumerate(refs):
        for q in range(4):
            wide_ref[...] = ref[4, 48 * q : 48 * q + 48].astype(F32)
            for r in range(6):
                turned_ref[8 * r : 8 * r + 8, :] = wide_ref[pl.ds(r, 8, stride=6), :]
            plane = turned_ref[...].astype(BF16)
            for b in range(3):
                for c in range(3):
                    view = shifted(plane, b, c, masks)
                    for a in range(3):
                        j = q - a
                        if 0 <= j < 2:
                            tap = 9 * a + 3 * b + c
                            lanes = (2 * peer + j) * AREA
                            taps_ref[tap * 48 : (tap + 1) * 48, lanes : lanes + AREA] = view


def kernel_grads(
    recv_ref,
    own_ref,
    a_ref,
    b_ref,
    c_ref,
    scale_ref,
    out_ref,
    shift_grad_ref,
    gain_grad_ref,
    taps_ref,
    gz_ref,
    low_ref,
    rest_ref,
    wide_ref,
    turned_ref,
):
    row_taps((own_ref, a_ref, b_ref, c_ref), taps_ref, wide_ref, turned_ref)
    total_cells = 2.0 * AREA * recv_ref.shape[0]
    total = full_tile(jnp.sum(recv_ref[...], axis=0))
    whole = total * (total_cells ** (-0.5))
    shift_grad_ref[...] = jnp.concatenate([whole[:1], whole[2:3, :64]], axis=1)
    gain_grad_ref[...] = jnp.concatenate([whole[1:2], whole[2:3, 64:]], axis=1)
    sum_grad, sum_cross = (col / total_cells for col in columns(total, 0))
    scale = scale_ref[...]
    for peer, ref in enumerate((own_ref, a_ref, b_ref, c_ref)):
        for j in range(2):
            act = ref[2 * j].astype(F32)
            normed = ref[2 * j + 1].astype(F32)
            lanes = (2 * peer + j) * AREA
            gz_ref[:, lanes : lanes + AREA] = (
                scale * (act - sum_grad - normed * sum_cross)
            ).astype(BF16)
    grads = lax.dot_general(
        taps_ref[...], gz_ref[...], (((1,), (1,)), ((), ())), preferred_element_type=F32
    )
    low_ref[...] = grads[:, :128]
    rest_ref[...] = jnp.concatenate([grads[:648, 128:], grads[648:, 128:]], axis=1)
    pad = jnp.zeros((5, AREA), F32)
    for z in range(8):
        first = low_ref[pl.ds(z, 162, stride=8), :]
        second = rest_ref[pl.ds(z, 81, stride=8), :]
        out_ref[z] = jnp.concatenate([first, second, pad], axis=0).astype(BF16)


def input_grads(
    flag_ref,
    w_ref,
    recv_ref,
    share_ref,
    up_ref,
    low_ref,
    high_ref,
    scale_ref,
    fwd_out_ref,
    grad_ref,
    skip_ref,
    x_ref,
    w_here_ref,
    mix_ref,
    sems,
):
    fetch = pltpu.make_async_copy(w_ref, w_here_ref, sems.at[0])
    fetch.start()
    decoder = flag_ref[0] == 1
    total_cells = 2.0 * AREA * recv_ref.shape[0]
    masks = tap_masks()
    total = full_tile(jnp.sum(recv_ref[...], axis=0))
    sum_grad, sum_cross = (col / total_cells for col in columns(total, 0))
    scale = scale_ref[...]
    acts = [low_ref[0], share_ref[0], share_ref[2], high_ref[0]]
    norms = [low_ref[1], share_ref[1], share_ref[3], high_ref[1]]
    for q in range(4):
        grad_z = scale * (acts[q].astype(F32) - sum_grad - norms[q].astype(F32) * sum_cross)
        if q == 0:
            grad_z = jnp.where(flag_ref[2] == 1, grad_z, 0.0)
        if q == 3:
            grad_z = jnp.where(flag_ref[3] == 1, grad_z, 0.0)
        grad_z = grad_z.astype(BF16)
        for b in range(3):
            for c in range(3):
                view = shifted(grad_z, 2 - b, 2 - c, masks)
                for a in range(3):
                    j = q + a - 2
                    if 0 <= j < 2:
                        tap = 9 * a + 3 * b + c
                        x_ref[tap * 192 : (tap + 1) * 192, j * AREA : (j + 1) * AREA] = view
    fetch.wait()
    back = jnp.dot(w_here_ref[...], x_ref[...], preferred_element_type=F32)
    for j in range(2):
        mix_ref[pl.ds(j, 192, stride=2), :] = up_ref[j] + back[:, j * AREA : (j + 1) * AREA]
    grad = mix_ref[...]
    grad_ref[...] = grad.astype(BF16)
    skip_ref[...] = jnp.where(decoder, grad, fwd_out_ref[...].astype(F32)).astype(BF16)


def hand_over(one_ref, two_ref, three_ref, out_one_ref, out_two_ref, out_three_ref):
    out_one_ref[...] = one_ref[...]
    out_two_ref[...] = two_ref[...]
    out_three_ref[...] = three_ref[...]


def sum_rows(scale_out, recv_ref, out_ref, wide_ref):
    total = jnp.sum(recv_ref[...].astype(F32), axis=0) * scale_out
    rest = jnp.concatenate([total[162:243, :64], total[162:243, 64:]], axis=0)

    def block(tap):
        rows = slice(6 * tap, 6 * tap + 6)
        return [total[rows], rest[rows]]

    for tap in range(0, TAPS, 2):
        parts = block(tap) + (block(tap + 1) if tap + 1 < TAPS else [])
        width = 192 if tap + 1 == TAPS else 384
        wide_ref[0:6, tap * 192 : tap * 192 + width] = jnp.concatenate(parts, axis=1)
    for r in range(6):
        out_ref[r] = wide_ref[r : r + 1, :]


def pair_rows(one, two):
    rest = jnp.concatenate([one[:, 128:], two[:, 128:]], axis=1)
    return jnp.concatenate([one[:, :128], two[:, :128], rest], axis=0)


def moved(block, axis, distance):
    count = lax.axis_size(axis)
    route = [(i, (i + distance) % count) for i in range(count)]
    return lax.ppermute(block, axis, route)


def per_device(
    fwd_input,
    fwd_skip,
    bwd_input,
    bwd_skip,
    out_cot,
    skip_cot,
    kernel,
    norm_gain,
    norm_shift,
    head_weight,
    labels,
):
    segments = lax.axis_size("segment")
    slabs = lax.axis_size("y") * lax.axis_size("z")
    segment_id = lax.axis_index("segment")
    y_id = lax.axis_index("y")
    slab_id = y_id * lax.axis_size("z") + lax.axis_index("z")
    is_decoder = segment_id * 2 >= segments
    flags = jnp.stack(
        [
            is_decoder.astype(jnp.int32),
            (segment_id == segments - 1).astype(jnp.int32),
            (slab_id > 0).astype(jnp.int32),
            (slab_id < slabs - 1).astype(jnp.int32),
            y_id.astype(jnp.int32),
        ]
    )
    kernel_mat = kernel[0]
    affine = pair_rows(norm_gain, norm_shift)

    def by_plane(block):
        return jnp.swapaxes(block[0], 0, 1)

    def joined(block, skip):
        added = (block.astype(F32) + skip.astype(F32)).astype(BF16)
        return by_plane(jnp.where(is_decoder, added, block))

    own = jnp.concatenate([joined(bwd_input, bwd_skip), joined(fwd_input, fwd_skip)], axis=1)
    nothing = jnp.zeros((192, AREA), BF16)
    upper, lower = slab_id < slabs - 1, slab_id > 0
    low = moved(jnp.where(upper, own[1, :192], nothing), SLABS, 1)
    high = moved(jnp.where(lower, own[0, :192], nothing), SLABS, -1)
    fwd_low = moved(jnp.where(upper, own[1, 192:], nothing), SLABS, 1)
    fwd_high = moved(jnp.where(lower, own[0, 192:], nothing), SLABS, -1)
    (turned,) = call(
        turn_weights,
        [((192, 5184), BF16)],
        [((192, 5184), BF16)],
        0,
        4 * 192 * 5184,
        kernel_mat,
        hbm=1,
        limit=52,
    )
    z, stats_send = call(
        conv_bwd,
        [((2, 192, AREA), F32), ((slabs, 3, AREA), F32)],
        [((5184, 256), BF16)],
        2 * 5184 * 192 * 256,
        5000000,
        own,
        low,
        high,
        turned,
    )
    fwd_z, fwd_tile = call(
        conv_fwd,
        [((2, 192, AREA), F32), ((8, AREA), F32)],
        [((5184, 256), BF16)],
        2 * 5184 * 192 * 256,
        5000000,
        own,
        fwd_low,
        fwd_high,
        turned,
    )
    stats = lax.all_to_all(stats_send, SLABS, 0, 0, tiled=True)
    out_cots = by_plane(out_cot)
    skip_cots = by_plane(skip_cot)
    upstream, *shares, scale, sums_send = call(
        head_and_sums,
        [
            ((2, 192, AREA), F32),
            *[((5, 192, AREA), BF16)] * 4,
            ((192, AREA), F32),
            ((slabs, 6, AREA), F32),
        ],
        HEAD_SCRATCH,
        4 * 192 * 105 * 512,
        4000000,
        flags,
        z,
        stats,
        own,
        low,
        high,
        out_cots,
        skip_cots,
        labels,
        affine,
        head_weight,
        head_weight.T,
        fwd_tile,
        smem=1,
    )
    sums = lax.all_to_all(sums_send, SLABS, 0, 0, tiled=True)
    share = shares[0]
    shares = [share] + [moved(shares[d], "y", d) for d in (1, 2, 3)]
    rim_low, rim_high = call(rims, [((2, 192, AREA), BF16)] * 2, [], 0, 400000, share)
    (fwd_out,) = call(
        forward_out,
        [((384, AREA), BF16)],
        [((384, AREA), F32)],
        0,
        1000000,
        sums,
        fwd_z,
        own,
        affine,
    )
    rim_low = moved(rim_low, SLABS, 1)
    rim_high = moved(rim_high, SLABS, -1)
    parts, shift_grad, gain_grad = call(
        kernel_grads,
        [((8, 248, AREA), BF16), ((1, 192), F32), ((1, 192), F32)],
        [
            ((1296, 1024), BF16),
            ((192, 1024), BF16),
            ((1296, AREA), F32),
            ((648, AREA), F32),
            ((48, AREA), F32),
            ((48, AREA), F32),
        ],
        0,
        1000,
        sums,
        *shares,
        scale,
    )
    parts, rim_low, rim_high = lax.optimization_barrier((parts, rim_low, rim_high))
    summed = lax.all_to_all(parts, "z", 0, 0, tiled=True)
    grad_joined, outgoing = call(
        input_grads,
        [((384, AREA), BF16)] * 2,
        [((5184, 256), BF16), ((192, 5184), BF16), ((384, AREA), F32)],
        2 * 5184 * 192 * 256,
        4000000,
        flags,
        kernel_mat,
        sums,
        share,
        upstream,
        rim_low,
        rim_high,
        scale,
        fwd_out,
        smem=1,
        hbm=1,
        limit=52,
    )
    fwd_out, grad_joined, outgoing = lax.optimization_barrier((fwd_out, grad_joined, outgoing))
    prev_block = moved(grad_joined, "segment", -1)
    next_block = moved(fwd_out, "segment", 1)
    mirrored = lax.ppermute(outgoing, "segment", [(i, segments - 1 - i) for i in range(segments)])
    total_cells = float(2 * slabs * AREA)

    def by_channel(block):
        return block.reshape(1, 192, 2, AREA)

    blocks = call(
        hand_over,
        [((384, AREA), BF16)] * 3,
        [],
        0,
        600000,
        next_block,
        prev_block,
        mirrored,
    )
    handed = [by_channel(block) for block in blocks]
    (kernel_grad,) = call(
        functools.partial(sum_rows, total_cells ** (-0.5)),
        [((6, 1, 5184), F32)],
        [((8, 5184), F32)],
        0,
        1000000,
        summed,
    )
    return (
        *handed,
        jnp.swapaxes(kernel_grad, 0, 1),
        gain_grad,
        shift_grad,
    )


def solution(mesh):
    grid = Mesh(mesh.devices.reshape(mesh.devices.shape[0], 4, 8), ("segment", "y", "z"))
    field = P("segment", None, SLABS, None)
    in_specs = (field,) * 6 + (
        P("segment", None, None),
        P("segment", None),
        P("segment", None),
        P(),
        P(SLABS, None),
    )
    out_specs = (
        field,
        field,
        field,
        P("segment", SLABS, None),
        P("segment", None),
        P("segment", None),
    )
    return jax.shard_map(
        per_device, mesh=grid, in_specs=in_specs, out_specs=out_specs, check_vma=False
    )
```

```python
import functools

import jax
import jax.numpy as jnp
from jax import lax
from jax.experimental import pallas as pl
from jax.experimental.pallas import tpu as pltpu
from jax.sharding import Mesh
from jax.sharding import PartitionSpec as P

ROWS = 8
COLS = 16
AREA = ROWS * COLS
TAPS = 27
SLABS = ("y", "z")

epsilon = 1e-05
leak_slope = 0.01

F32 = jnp.float32
BF16 = jnp.bfloat16
HBM = pl.BlockSpec(memory_space=pltpu.HBM)
VMEM = pl.BlockSpec(memory_space=pltpu.VMEM)
SMEM = pl.BlockSpec(memory_space=pltpu.SMEM)


HEAD_SCRATCH = [((2, 192, AREA), F32)]


def call(body, outs, scratch, flops, moved, *args, smem=0, hbm=0, limit=24):
    specs = [SMEM] * smem + [HBM] * hbm + [VMEM] * (len(args) - smem - hbm)
    shapes = [jax.ShapeDtypeStruct(shape, kind) for shape, kind in outs]
    places = [pltpu.VMEM(shape, kind) for shape, kind in scratch]
    return pl.pallas_call(
        body,
        out_shape=shapes,
        in_specs=specs,
        out_specs=[VMEM] * len(outs),
        scratch_shapes=places + [pltpu.SemaphoreType.DMA((4,))] * (hbm > 0),
        compiler_params=pltpu.CompilerParams(vmem_limit_bytes=limit * 1024 * 1024),
        cost_estimate=pl.CostEstimate(flops=flops, bytes_accessed=moved, transcendentals=0),
        name=getattr(body, "__name__", "kernel"),
    )(*args)


def tap_masks():
    cell = lax.broadcasted_iota(jnp.int32, (1, AREA), 1)
    row = cell // COLS
    col = cell % COLS
    masks = {}
    for b in range(3):
        for c in range(3):
            inside = None
            if b != 1:
                inside = row > 0 if b == 0 else row < ROWS - 1
            if c != 1:
                part = col > 0 if c == 0 else col < COLS - 1
                inside = part if inside is None else jnp.logical_and(inside, part)
            masks[(b, c)] = inside
    return masks


def shifted(plane, b, c, masks):
    step = (b - 1) * COLS + (c - 1)
    if step == 0:
        return plane
    moved = pltpu.roll(plane, (-step) % AREA, 1)
    return jnp.where(masks[(b, c)], moved, jnp.zeros_like(moved))


def full_tile(tile):
    if tile.shape[0] == 8:
        return tile
    return jnp.concatenate([tile, jnp.zeros((8 - tile.shape[0], AREA), F32)], axis=0)


def columns(tile, pair):
    square = jnp.concatenate([full_tile(tile), jnp.zeros((AREA - 8, AREA), F32)], axis=0).T
    row = 3 * pair
    rest = square[:, row + 2 : row + 3]
    first = jnp.concatenate([square[:, row : row + 1], rest[:64]], axis=0)
    second = jnp.concatenate([square[:, row + 1 : row + 2], rest[64:]], axis=0)
    return first, second


def packed_tile(cols):
    lane = lax.broadcasted_iota(jnp.int32, (AREA, AREA), 1)
    square = jnp.zeros((AREA, AREA), F32)
    for pair in range(len(cols) // 2):
        one, two = cols[2 * pair], cols[2 * pair + 1]
        rest = jnp.concatenate([one[128:], two[128:]], axis=0)
        for k, col in enumerate((one[:128], two[:128], rest)):
            square = jnp.where(lane == 3 * pair + k, col, square)
    return square.T[:8]


def spread_sums(received, pair, cells, peers):
    total = jnp.sum(received, axis=0)
    apart = jnp.sum(jnp.square(received - (total / peers)[None]), axis=0)
    mean, squares = columns(total, pair)
    return mean / peers, squares + cells * columns(apart, pair)[0]


def local_stats(planes_out, cells):
    mean = sum(jnp.sum(p, axis=1, keepdims=True) for p in planes_out) / cells
    squares = sum(jnp.sum(jnp.square(p - mean), axis=1, keepdims=True) for p in planes_out)
    return [mean, squares]


def turn_weights(w_ref, out_ref, here_ref, sems):
    bounds = (0, 4, 8, 12, 14)
    copies = []
    for part in range(4):
        start = bounds[part] * 384
        band = pl.ds(start, min(bounds[part + 1] * 384, 5184) - start)
        copies.append(
            pltpu.make_async_copy(w_ref.at[:, band], here_ref.at[:, band], sems.at[part])
        )
        copies[part].start()
    for part in range(4):
        copies[part].wait()
        for pair in range(bounds[part], bounds[part + 1]):
            width = 384 if pair < 13 else 192
            block = here_ref[:, pair * 384 : pair * 384 + width].T
            if width == 384:
                block = jnp.concatenate([block[:192], block[192:]], axis=1)
            out_ref[:, pair * 384 : pair * 384 + width] = block


def fill_taps(planes, outputs, x_ref, masks, channels, first):
    for q, plane in enumerate(planes):
        for b in range(3):
            for c in range(3):
                view = shifted(plane, b, c, masks)
                for a in range(3):
                    j = q - a
                    if 0 <= j < outputs:
                        tap = 9 * a + 3 * b + c
                        lanes = (first + j) * AREA
                        x_ref[
                            tap * channels : (tap + 1) * channels, lanes : lanes + AREA
                        ] = view


def convolution(which, own_ref, low_ref, high_ref, wt_ref, z_ref, x_ref):
    rows = slice(192 * which, 192 * which + 192)
    planes = [low_ref[...], own_ref[0, rows], own_ref[1, rows], high_ref[...]]
    fill_taps(planes, 2, x_ref, tap_masks(), 192, 0)
    z = jnp.dot(wt_ref[...], x_ref[...], preferred_element_type=F32)
    outs = [z[:, :AREA], z[:, AREA:]]
    z_ref[0] = outs[0]
    z_ref[1] = outs[1]
    return local_stats(outs, 2.0 * AREA)


def conv_bwd(own_ref, low_ref, high_ref, wt_ref, z_ref, send_ref, x_ref):
    tile = packed_tile(convolution(0, own_ref, low_ref, high_ref, wt_ref, z_ref, x_ref))
    send_ref[...] = jnp.broadcast_to(tile[None, : send_ref.shape[1]], send_ref.shape)


def conv_fwd(own_ref, low_ref, high_ref, wt_ref, z_ref, tile_ref, x_ref):
    mean, squares = convolution(1, own_ref, low_ref, high_ref, wt_ref, z_ref, x_ref)
    tile_ref[...] = packed_tile([jnp.zeros_like(mean), jnp.zeros_like(mean), mean, squares])


def fwd_edges(flag_ref, own_ref, z_ref, low_ref, high_ref):
    low_ref[...] = jnp.where(flag_ref[3] == 1, own_ref[1, 192:], jnp.zeros((192, AREA), BF16))
    high_ref[...] = jnp.where(flag_ref[2] == 1, own_ref[0, 192:], jnp.zeros((192, AREA), BF16))


def rims(share_ref, rim_low_ref, rim_high_ref):
    rim_high_ref[...] = share_ref[:2]
    rim_low_ref[...] = share_ref[2:4]


def head_and_sums(
    flag_ref,
    z_ref,
    recv_ref,
    own_ref,
    low_ref,
    high_ref,
    out_cot_ref,
    skip_cot_ref,
    label_ref,
    affine_ref,
    head_ref,
    head_turned_ref,
    fwd_tile_ref,
    up_ref,
    share_ref,
    share_a_ref,
    share_b_ref,
    share_c_ref,
    scale_ref,
    send_ref,
    head_cot_ref,
):
    shares = (share_ref, share_a_ref, share_b_ref, share_c_ref)
    for distance, ref in enumerate(shares):
        rows = pl.ds(pl.multiple_of(48 * ((flag_ref[4] + distance) % 4), 16), 48)
        ref[4, :48] = low_ref[rows]
        ref[4, 48:96] = own_ref[0, rows]
        ref[4, 96:144] = own_ref[1, rows]
        ref[4, 144:] = high_ref[rows]
    decoder = flag_ref[0] == 1
    last = flag_ref[1] == 1
    peers = recv_ref.shape[0]
    cells = 2.0 * AREA
    mean, squares = spread_sums(recv_ref[...], 0, cells, peers)
    inv_std = lax.rsqrt(squares / (cells * peers) + epsilon)
    gain, shift = columns(affine_ref[...], 0)
    scale_ref[...] = jnp.broadcast_to(gain * inv_std, scale_ref.shape)
    classes = head_ref.shape[1]
    class_id = lax.broadcasted_iota(jnp.int32, (classes, AREA), 0)
    sum_grad = jnp.zeros((192, 1), F32)
    sum_cross = jnp.zeros((192, 1), F32)
    for j in range(2):
        normed = (z_ref[j] - mean) * inv_std
        scaled = normed * gain + shift
        activated = jnp.where(scaled > 0, scaled, leak_slope * scaled)
        output = (own_ref[j, :192].astype(F32) + activated).astype(BF16)

        @pl.when(last)
        def head(output=output, j=j):
            logits = jnp.dot(head_turned_ref[...], output, preferred_element_type=F32)
            raised = jnp.exp(logits - jnp.max(logits, axis=0, keepdims=True))
            prob = raised / jnp.sum(raised, axis=0, keepdims=True)
            hot = jnp.where(class_id == label_ref[j : j + 1, :], 1.0, 0.0)
            delta = (prob - hot).astype(BF16)
            head_cot_ref[j] = jnp.dot(head_ref[...], delta, preferred_element_type=F32)

        @pl.when(jnp.logical_not(last))
        def given(j=j):
            head_cot_ref[j] = out_cot_ref[j].astype(F32)

        upstream = head_cot_ref[j] + jnp.where(decoder, 0.0, skip_cot_ref[j].astype(F32))
        grad_act = upstream * jnp.where(scaled > 0, 1.0, leak_slope)
        up_ref[j] = upstream
        for k, part in enumerate((grad_act.astype(BF16), normed.astype(BF16))):
            for ref in shares:
                ref[2 * j + k] = part
        sum_grad = sum_grad + jnp.sum(grad_act, axis=1, keepdims=True)
        sum_cross = sum_cross + jnp.sum(grad_act * normed, axis=1, keepdims=True)
    tile = packed_tile([sum_grad, sum_cross]) + fwd_tile_ref[...]
    send_ref[...] = jnp.broadcast_to(tile[None, : send_ref.shape[1]], send_ref.shape)


def forward_out(recv_ref, z_ref, own_ref, affine_ref, out_ref, mix_ref):
    peers = recv_ref.shape[0]
    cells = 2.0 * AREA
    mean, squares = spread_sums(recv_ref[...], 1, cells, peers)
    inv_std = lax.rsqrt(squares / (cells * peers) + epsilon)
    gain, shift = columns(affine_ref[...], 0)
    for j in range(2):
        scaled = (z_ref[j] - mean) * inv_std * gain + shift
        activated = jnp.where(scaled > 0, scaled, leak_slope * scaled)
        mix_ref[pl.ds(j, 192, stride=2), :] = own_ref[j, 192:].astype(F32) + activated
    out_ref[...] = mix_ref[...].astype(BF16)


def row_taps(refs, taps_ref, wide_ref, turned_ref):
    masks = tap_masks()
    for peer, ref in enumerate(refs):
        for q in range(4):
            wide_ref[...] = ref[4, 48 * q : 48 * q + 48].astype(F32)
            for r in range(6):
                turned_ref[8 * r : 8 * r + 8, :] = wide_ref[pl.ds(r, 8, stride=6), :]
            plane = turned_ref[...].astype(BF16)
            for b in range(3):
                for c in range(3):
                    view = shifted(plane, b, c, masks)
                    for a in range(3):
                        j = q - a
                        if 0 <= j < 2:
                            tap = 9 * a + 3 * b + c
                            lanes = (2 * peer + j) * AREA
                            taps_ref[tap * 48 : (tap + 1) * 48, lanes : lanes + AREA] = view


def kernel_grads(
    recv_ref,
    own_ref,
    a_ref,
    b_ref,
    c_ref,
    scale_ref,
    out_ref,
    shift_grad_ref,
    gain_grad_ref,
    taps_ref,
    gz_ref,
    low_ref,
    rest_ref,
    wide_ref,
    turned_ref,
):
    row_taps((own_ref, a_ref, b_ref, c_ref), taps_ref, wide_ref, turned_ref)
    total_cells = 2.0 * AREA * recv_ref.shape[0]
    total = full_tile(jnp.sum(recv_ref[...], axis=0))
    whole = total * (total_cells ** (-0.5))
    shift_grad_ref[...] = jnp.concatenate([whole[:1], whole[2:3, :64]], axis=1)
    gain_grad_ref[...] = jnp.concatenate([whole[1:2], whole[2:3, 64:]], axis=1)
    sum_grad, sum_cross = (col / total_cells for col in columns(total, 0))
    scale = scale_ref[...]
    for peer, ref in enumerate((own_ref, a_ref, b_ref, c_ref)):
        for j in range(2):
            act = ref[2 * j].astype(F32)
            normed = ref[2 * j + 1].astype(F32)
            lanes = (2 * peer + j) * AREA
            gz_ref[:, lanes : lanes + AREA] = (
                scale * (act - sum_grad - normed * sum_cross)
            ).astype(BF16)
    grads = lax.dot_general(
        taps_ref[...], gz_ref[...], (((1,), (1,)), ((), ())), preferred_element_type=F32
    )
    low_ref[...] = grads[:, :128]
    rest_ref[...] = jnp.concatenate([grads[:648, 128:], grads[648:, 128:]], axis=1)
    pad = jnp.zeros((5, AREA), F32)
    for z in range(8):
        first = low_ref[pl.ds(z, 162, stride=8), :]
        second = rest_ref[pl.ds(z, 81, stride=8), :]
        out_ref[z] = jnp.concatenate([first, second, pad], axis=0).astype(BF16)


def input_grads(
    flag_ref,
    w_ref,
    recv_ref,
    share_ref,
    up_ref,
    low_ref,
    high_ref,
    scale_ref,
    fwd_out_ref,
    grad_ref,
    skip_ref,
    x_ref,
    w_here_ref,
    mix_ref,
    sems,
):
    fetch = pltpu.make_async_copy(w_ref, w_here_ref, sems.at[0])
    fetch.start()
    decoder = flag_ref[0] == 1
    total_cells = 2.0 * AREA * recv_ref.shape[0]
    masks = tap_masks()
    total = full_tile(jnp.sum(recv_ref[...], axis=0))
    sum_grad, sum_cross = (col / total_cells for col in columns(total, 0))
    scale = scale_ref[...]
    acts = [low_ref[0], share_ref[0], share_ref[2], high_ref[0]]
    norms = [low_ref[1], share_ref[1], share_ref[3], high_ref[1]]
    for q in range(4):
        grad_z = scale * (acts[q].astype(F32) - sum_grad - norms[q].astype(F32) * sum_cross)
        if q == 0:
            grad_z = jnp.where(flag_ref[2] == 1, grad_z, 0.0)
        if q == 3:
            grad_z = jnp.where(flag_ref[3] == 1, grad_z, 0.0)
        grad_z = grad_z.astype(BF16)
        for b in range(3):
            for c in range(3):
                view = shifted(grad_z, 2 - b, 2 - c, masks)
                for a in range(3):
                    j = q + a - 2
                    if 0 <= j < 2:
                        tap = 9 * a + 3 * b + c
                        x_ref[tap * 192 : (tap + 1) * 192, j * AREA : (j + 1) * AREA] = view
    fetch.wait()
    back = jnp.dot(w_here_ref[...], x_ref[...], preferred_element_type=F32)
    for j in range(2):
        mix_ref[pl.ds(j, 192, stride=2), :] = up_ref[j] + back[:, j * AREA : (j + 1) * AREA]
    grad = mix_ref[...]
    grad_ref[...] = grad.astype(BF16)
    skip_ref[...] = jnp.where(decoder, grad, fwd_out_ref[...].astype(F32)).astype(BF16)


def hand_over(one_ref, two_ref, three_ref, out_one_ref, out_two_ref, out_three_ref):
    out_one_ref[...] = one_ref[...]
    out_two_ref[...] = two_ref[...]
    out_three_ref[...] = three_ref[...]


def sum_rows(scale_out, recv_ref, out_ref, wide_ref):
    total = jnp.sum(recv_ref[...].astype(F32), axis=0) * scale_out
    rest = jnp.concatenate([total[162:243, :64], total[162:243, 64:]], axis=0)

    def block(tap):
        rows = slice(6 * tap, 6 * tap + 6)
        return [total[rows], rest[rows]]

    for tap in range(0, TAPS, 2):
        parts = block(tap) + (block(tap + 1) if tap + 1 < TAPS else [])
        width = 192 if tap + 1 == TAPS else 384
        wide_ref[0:6, tap * 192 : tap * 192 + width] = jnp.concatenate(parts, axis=1)
    for r in range(6):
        out_ref[r] = wide_ref[r : r + 1, :]


def pair_rows(one, two):
    rest = jnp.concatenate([one[:, 128:], two[:, 128:]], axis=1)
    return jnp.concatenate([one[:, :128], two[:, :128], rest], axis=0)


def moved(block, axis, distance):
    count = lax.axis_size(axis)
    route = [(i, (i + distance) % count) for i in range(count)]
    return lax.ppermute(block, axis, route)


def per_device(
    fwd_input,
    fwd_skip,
    bwd_input,
    bwd_skip,
    out_cot,
    skip_cot,
    kernel,
    norm_gain,
    norm_shift,
    head_weight,
    labels,
):
    segments = lax.axis_size("segment")
    slabs = lax.axis_size("y") * lax.axis_size("z")
    segment_id = lax.axis_index("segment")
    y_id = lax.axis_index("y")
    slab_id = y_id * lax.axis_size("z") + lax.axis_index("z")
    is_decoder = segment_id * 2 >= segments
    flags = jnp.stack(
        [
            is_decoder.astype(jnp.int32),
            (segment_id == segments - 1).astype(jnp.int32),
            (slab_id > 0).astype(jnp.int32),
            (slab_id < slabs - 1).astype(jnp.int32),
            y_id.astype(jnp.int32),
        ]
    )
    kernel_mat = kernel[0]
    affine = pair_rows(norm_gain, norm_shift)

    def by_plane(block):
        return jnp.swapaxes(block[0], 0, 1)

    def joined(block, skip):
        added = (block.astype(F32) + skip.astype(F32)).astype(BF16)
        return by_plane(jnp.where(is_decoder, added, block))

    own = jnp.concatenate([joined(bwd_input, bwd_skip), joined(fwd_input, fwd_skip)], axis=1)
    nothing = jnp.zeros((192, AREA), BF16)
    upper, lower = slab_id < slabs - 1, slab_id > 0
    low = moved(jnp.where(upper, own[1, :192], nothing), SLABS, 1)
    high = moved(jnp.where(lower, own[0, :192], nothing), SLABS, -1)
    (turned,) = call(
        turn_weights,
        [((192, 5184), BF16)],
        [((192, 5184), BF16)],
        0,
        4 * 192 * 5184,
        kernel_mat,
        hbm=1,
        limit=52,
    )
    z, stats_send = call(
        conv_bwd,
        [((2, 192, AREA), F32), ((slabs, 6, AREA), F32)],
        [((5184, 256), BF16)],
        2 * 5184 * 192 * 256,
        5000000,
        own,
        low,
        high,
        turned,
    )
    fwd_low, fwd_high = call(
        fwd_edges, [((192, AREA), BF16)] * 2, [], 0, 400000, flags, own, z, smem=1
    )
    fwd_low = moved(fwd_low, SLABS, 1)
    fwd_high = moved(fwd_high, SLABS, -1)
    fwd_z, fwd_tile = call(
        conv_fwd,
        [((2, 192, AREA), F32), ((8, AREA), F32)],
        [((5184, 256), BF16)],
        2 * 5184 * 192 * 256,
        5000000,
        own,
        fwd_low,
        fwd_high,
        turned,
    )
    stats = lax.all_to_all(stats_send, SLABS, 0, 0, tiled=True)
    out_cots = by_plane(out_cot)
    skip_cots = by_plane(skip_cot)
    upstream, *shares, scale, sums_send = call(
        head_and_sums,
        [
            ((2, 192, AREA), F32),
            *[((5, 192, AREA), BF16)] * 4,
            ((192, AREA), F32),
            ((slabs, 6, AREA), F32),
        ],
        HEAD_SCRATCH,
        4 * 192 * 105 * 512,
        4000000,
        flags,
        z,
        stats,
        own,
        low,
        high,
        out_cots,
        skip_cots,
        labels,
        affine,
        head_weight,
        head_weight.T,
        fwd_tile,
        smem=1,
    )
    sums = lax.all_to_all(sums_send, SLABS, 0, 0, tiled=True)
    share = shares[0]
    shares = [share] + [moved(shares[d], "y", d) for d in (1, 2, 3)]
    rim_low, rim_high = call(rims, [((2, 192, AREA), BF16)] * 2, [], 0, 400000, share)
    (fwd_out,) = call(
        forward_out,
        [((384, AREA), BF16)],
        [((384, AREA), F32)],
        0,
        1000000,
        sums,
        fwd_z,
        own,
        affine,
    )
    rim_low = moved(rim_low, SLABS, 1)
    rim_high = moved(rim_high, SLABS, -1)
    parts, shift_grad, gain_grad = call(
        kernel_grads,
        [((8, 248, AREA), BF16), ((1, 192), F32), ((1, 192), F32)],
        [
            ((1296, 1024), BF16),
            ((192, 1024), BF16),
            ((1296, AREA), F32),
            ((648, AREA), F32),
            ((48, AREA), F32),
            ((48, AREA), F32),
        ],
        0,
        1000,
        sums,
        *shares,
        scale,
    )
    parts, rim_low, rim_high = lax.optimization_barrier((parts, rim_low, rim_high))
    summed = lax.all_to_all(parts, "z", 0, 0, tiled=True)
    grad_joined, outgoing = call(
        input_grads,
        [((384, AREA), BF16)] * 2,
        [((5184, 256), BF16), ((192, 5184), BF16), ((384, AREA), F32)],
        2 * 5184 * 192 * 256,
        4000000,
        flags,
        kernel_mat,
        sums,
        share,
        upstream,
        rim_low,
        rim_high,
        scale,
        fwd_out,
        smem=1,
        hbm=1,
        limit=52,
    )
    fwd_out, grad_joined, outgoing = lax.optimization_barrier((fwd_out, grad_joined, outgoing))
    prev_block = moved(grad_joined, "segment", -1)
    next_block = moved(fwd_out, "segment", 1)
    mirrored = lax.ppermute(outgoing, "segment", [(i, segments - 1 - i) for i in range(segments)])
    total_cells = float(2 * slabs * AREA)

    def by_channel(block):
        return block.reshape(1, 192, 2, AREA)

    blocks = call(
        hand_over,
        [((384, AREA), BF16)] * 3,
        [],
        0,
        600000,
        next_block,
        prev_block,
        mirrored,
    )
    handed = [by_channel(block) for block in blocks]
    (kernel_grad,) = call(
        functools.partial(sum_rows, total_cells ** (-0.5)),
        [((6, 1, 5184), F32)],
        [((8, 5184), F32)],
        0,
        1000000,
        summed,
    )
    return (
        *handed,
        jnp.swapaxes(kernel_grad, 0, 1),
        gain_grad,
        shift_grad,
    )


def solution(mesh):
    grid = Mesh(mesh.devices.reshape(mesh.devices.shape[0], 4, 8), ("segment", "y", "z"))
    field = P("segment", None, SLABS, None)
    in_specs = (field,) * 6 + (
        P("segment", None, None),
        P("segment", None),
        P("segment", None),
        P(),
        P(SLABS, None),
    )
    out_specs = (
        field,
        field,
        field,
        P("segment", SLABS, None),
        P("segment", None),
        P("segment", None),
    )
    return jax.shard_map(
        per_device, mesh=grid, in_specs=in_specs, out_specs=out_specs, check_vma=False
    )
```

```python
import functools

import jax
import jax.numpy as jnp
from jax import lax
from jax.experimental import pallas as pl
from jax.experimental.pallas import tpu as pltpu
from jax.sharding import Mesh
from jax.sharding import PartitionSpec as P

ROWS = 8
COLS = 16
AREA = ROWS * COLS
TAPS = 27
SLABS = ("y", "z")

epsilon = 1e-05
leak_slope = 0.01

F32 = jnp.float32
BF16 = jnp.bfloat16
HBM = pl.BlockSpec(memory_space=pltpu.HBM)
VMEM = pl.BlockSpec(memory_space=pltpu.VMEM)
SMEM = pl.BlockSpec(memory_space=pltpu.SMEM)


HEAD_SCRATCH = [((2, 192, AREA), F32)]


def call(body, outs, scratch, flops, moved, *args, smem=0, hbm=0, limit=24):
    specs = [SMEM] * smem + [HBM] * hbm + [VMEM] * (len(args) - smem - hbm)
    shapes = [jax.ShapeDtypeStruct(shape, kind) for shape, kind in outs]
    places = [pltpu.VMEM(shape, kind) for shape, kind in scratch]
    return pl.pallas_call(
        body,
        out_shape=shapes,
        in_specs=specs,
        out_specs=[VMEM] * len(outs),
        scratch_shapes=places + [pltpu.SemaphoreType.DMA((4,))] * (hbm > 0),
        compiler_params=pltpu.CompilerParams(vmem_limit_bytes=limit * 1024 * 1024),
        cost_estimate=pl.CostEstimate(flops=flops, bytes_accessed=moved, transcendentals=0),
        name=getattr(body, "__name__", "kernel"),
    )(*args)


def tap_masks():
    cell = lax.broadcasted_iota(jnp.int32, (1, AREA), 1)
    row = cell // COLS
    col = cell % COLS
    masks = {}
    for b in range(3):
        for c in range(3):
            inside = None
            if b != 1:
                inside = row > 0 if b == 0 else row < ROWS - 1
            if c != 1:
                part = col > 0 if c == 0 else col < COLS - 1
                inside = part if inside is None else jnp.logical_and(inside, part)
            masks[(b, c)] = inside
    return masks


def shifted(plane, b, c, masks):
    step = (b - 1) * COLS + (c - 1)
    if step == 0:
        return plane
    moved = pltpu.roll(plane, (-step) % AREA, 1)
    return jnp.where(masks[(b, c)], moved, jnp.zeros_like(moved))


def full_tile(tile):
    if tile.shape[0] == 8:
        return tile
    return jnp.concatenate([tile, jnp.zeros((8 - tile.shape[0], AREA), F32)], axis=0)


def columns(tile, pair):
    square = jnp.concatenate([full_tile(tile), jnp.zeros((AREA - 8, AREA), F32)], axis=0).T
    row = 3 * pair
    rest = square[:, row + 2 : row + 3]
    first = jnp.concatenate([square[:, row : row + 1], rest[:64]], axis=0)
    second = jnp.concatenate([square[:, row + 1 : row + 2], rest[64:]], axis=0)
    return first, second


def packed_tile(cols):
    lane = lax.broadcasted_iota(jnp.int32, (AREA, AREA), 1)
    square = jnp.zeros((AREA, AREA), F32)
    for pair in range(len(cols) // 2):
        one, two = cols[2 * pair], cols[2 * pair + 1]
        rest = jnp.concatenate([one[128:], two[128:]], axis=0)
        for k, col in enumerate((one[:128], two[:128], rest)):
            square = jnp.where(lane == 3 * pair + k, col, square)
    return square.T[:8]


def spread_sums(received, pair, cells, peers):
    total = jnp.sum(received, axis=0)
    apart = jnp.sum(jnp.square(received - (total / peers)[None]), axis=0)
    mean, squares = columns(total, pair)
    return mean / peers, squares + cells * columns(apart, pair)[0]


def local_stats(planes_out, cells):
    mean = sum(jnp.sum(p, axis=1, keepdims=True) for p in planes_out) / cells
    squares = sum(jnp.sum(jnp.square(p - mean), axis=1, keepdims=True) for p in planes_out)
    return [mean, squares]


def turn_weights(w_ref, out_ref, here_ref, sems):
    bounds = (0, 4, 8, 12, 14)
    copies = []
    for part in range(4):
        start = bounds[part] * 384
        band = pl.ds(start, min(bounds[part + 1] * 384, 5184) - start)
        copies.append(
            pltpu.make_async_copy(w_ref.at[:, band], here_ref.at[:, band], sems.at[part])
        )
        copies[part].start()
    for part in range(4):
        copies[part].wait()
        for pair in range(bounds[part], bounds[part + 1]):
            width = 384 if pair < 13 else 192
            block = here_ref[:, pair * 384 : pair * 384 + width].T
            if width == 384:
                block = jnp.concatenate([block[:192], block[192:]], axis=1)
            out_ref[:, pair * 384 : pair * 384 + width] = block


def fill_taps(planes, outputs, x_ref, masks, channels, first):
    for q, plane in enumerate(planes):
        for b in range(3):
            for c in range(3):
                view = shifted(plane, b, c, masks)
                for a in range(3):
                    j = q - a
                    if 0 <= j < outputs:
                        tap = 9 * a + 3 * b + c
                        lanes = (first + j) * AREA
                        x_ref[
                            tap * channels : (tap + 1) * channels, lanes : lanes + AREA
                        ] = view


def conv_both(own_ref, low_ref, high_ref, wt_ref, z_ref, send_ref, x_ref):
    masks = tap_masks()
    for which in range(2):
        rows = slice(192 * which, 192 * which + 192)
        planes = [low_ref[rows], own_ref[0, rows], own_ref[1, rows], high_ref[rows]]
        fill_taps(planes, 2, x_ref, masks, 192, 2 * which)
    z = jnp.dot(wt_ref[...], x_ref[...], preferred_element_type=F32)
    outs = [z[:, j * AREA : (j + 1) * AREA] for j in range(4)]
    for j in range(4):
        z_ref[j] = outs[j]
    tile = packed_tile(
        local_stats(outs[:2], 2.0 * AREA) + local_stats(outs[2:], 2.0 * AREA)
    )
    send_ref[...] = jnp.broadcast_to(tile[None, : send_ref.shape[1]], send_ref.shape)


def head_and_sums(
    flag_ref,
    z_ref,
    recv_ref,
    own_ref,
    low_ref,
    high_ref,
    out_cot_ref,
    skip_cot_ref,
    label_ref,
    affine_ref,
    head_ref,
    head_turned_ref,
    up_ref,
    share_ref,
    share_a_ref,
    share_b_ref,
    share_c_ref,
    scale_ref,
    send_ref,
    head_cot_ref,
):
    shares = (share_ref, share_a_ref, share_b_ref, share_c_ref)
    for distance, ref in enumerate(shares):
        rows = pl.ds(pl.multiple_of(48 * ((flag_ref[4] + distance) % 4), 16), 48)
        ref[4, :48] = low_ref[rows]
        ref[4, 48:96] = own_ref[0, rows]
        ref[4, 96:144] = own_ref[1, rows]
        ref[4, 144:] = high_ref[rows]
    decoder = flag_ref[0] == 1
    last = flag_ref[1] == 1
    peers = recv_ref.shape[0]
    cells = 2.0 * AREA
    mean, squares = spread_sums(recv_ref[...], 0, cells, peers)
    inv_std = lax.rsqrt(squares / (cells * peers) + epsilon)
    gain, shift = columns(affine_ref[...], 0)
    scale_ref[...] = jnp.broadcast_to(gain * inv_std, scale_ref.shape)
    classes = head_ref.shape[1]
    class_id = lax.broadcasted_iota(jnp.int32, (classes, AREA), 0)
    sum_grad = jnp.zeros((192, 1), F32)
    sum_cross = jnp.zeros((192, 1), F32)
    for j in range(2):
        normed = (z_ref[j] - mean) * inv_std
        scaled = normed * gain + shift
        activated = jnp.where(scaled > 0, scaled, leak_slope * scaled)
        output = (own_ref[j, :192].astype(F32) + activated).astype(BF16)

        @pl.when(last)
        def head(output=output, j=j):
            logits = jnp.dot(head_turned_ref[...], output, preferred_element_type=F32)
            raised = jnp.exp(logits - jnp.max(logits, axis=0, keepdims=True))
            prob = raised / jnp.sum(raised, axis=0, keepdims=True)
            hot = jnp.where(class_id == label_ref[j : j + 1, :], 1.0, 0.0)
            delta = (prob - hot).astype(BF16)
            head_cot_ref[j] = jnp.dot(head_ref[...], delta, preferred_element_type=F32)

        @pl.when(jnp.logical_not(last))
        def given(j=j):
            head_cot_ref[j] = out_cot_ref[j].astype(F32)

        upstream = head_cot_ref[j] + jnp.where(decoder, 0.0, skip_cot_ref[j].astype(F32))
        grad_act = upstream * jnp.where(scaled > 0, 1.0, leak_slope)
        up_ref[j] = upstream
        for k, part in enumerate((grad_act.astype(BF16), normed.astype(BF16))):
            for ref in shares:
                ref[2 * j + k] = part
        sum_grad = sum_grad + jnp.sum(grad_act, axis=1, keepdims=True)
        sum_cross = sum_cross + jnp.sum(grad_act * normed, axis=1, keepdims=True)
    tile = packed_tile([sum_grad, sum_cross])
    send_ref[...] = jnp.broadcast_to(tile[None, : send_ref.shape[1]], send_ref.shape)


def forward_out(
    recv_ref, z_ref, own_ref, affine_ref, share_ref, out_ref, rim_low_ref, rim_high_ref, mix_ref
):
    rim_high_ref[...] = share_ref[:2]
    rim_low_ref[...] = share_ref[2:4]
    peers = recv_ref.shape[0]
    cells = 2.0 * AREA
    mean, squares = spread_sums(recv_ref[...], 1, cells, peers)
    inv_std = lax.rsqrt(squares / (cells * peers) + epsilon)
    gain, shift = columns(affine_ref[...], 0)
    for j in range(2):
        scaled = (z_ref[2 + j] - mean) * inv_std * gain + shift
        activated = jnp.where(scaled > 0, scaled, leak_slope * scaled)
        mix_ref[pl.ds(j, 192, stride=2), :] = own_ref[j, 192:].astype(F32) + activated
    out_ref[...] = mix_ref[...].astype(BF16)


def row_taps(refs, taps_ref, wide_ref, turned_ref):
    masks = tap_masks()
    for peer, ref in enumerate(refs):
        for q in range(4):
            wide_ref[...] = ref[4, 48 * q : 48 * q + 48].astype(F32)
            for r in range(6):
                turned_ref[8 * r : 8 * r + 8, :] = wide_ref[pl.ds(r, 8, stride=6), :]
            plane = turned_ref[...].astype(BF16)
            for b in range(3):
                for c in range(3):
                    view = shifted(plane, b, c, masks)
                    for a in range(3):
                        j = q - a
                        if 0 <= j < 2:
                            tap = 9 * a + 3 * b + c
                            lanes = (2 * peer + j) * AREA
                            taps_ref[tap * 48 : (tap + 1) * 48, lanes : lanes + AREA] = view


def kernel_grads(
    recv_ref,
    own_ref,
    a_ref,
    b_ref,
    c_ref,
    scale_ref,
    out_ref,
    shift_grad_ref,
    gain_grad_ref,
    taps_ref,
    gz_ref,
    low_ref,
    rest_ref,
    wide_ref,
    turned_ref,
):
    row_taps((own_ref, a_ref, b_ref, c_ref), taps_ref, wide_ref, turned_ref)
    total_cells = 2.0 * AREA * recv_ref.shape[0]
    total = full_tile(jnp.sum(recv_ref[...], axis=0))
    whole = total * (total_cells ** (-0.5))
    shift_grad_ref[...] = jnp.concatenate([whole[:1], whole[2:3, :64]], axis=1)
    gain_grad_ref[...] = jnp.concatenate([whole[1:2], whole[2:3, 64:]], axis=1)
    sum_grad, sum_cross = (col / total_cells for col in columns(total, 0))
    scale = scale_ref[...]
    for peer, ref in enumerate((own_ref, a_ref, b_ref, c_ref)):
        for j in range(2):
            act = ref[2 * j].astype(F32)
            normed = ref[2 * j + 1].astype(F32)
            lanes = (2 * peer + j) * AREA
            gz_ref[:, lanes : lanes + AREA] = (
                scale * (act - sum_grad - normed * sum_cross)
            ).astype(BF16)
    grads = lax.dot_general(
        taps_ref[...], gz_ref[...], (((1,), (1,)), ((), ())), preferred_element_type=F32
    )
    low_ref[...] = grads[:, :128]
    rest_ref[...] = jnp.concatenate([grads[:648, 128:], grads[648:, 128:]], axis=1)
    pad = jnp.zeros((5, AREA), F32)
    for z in range(8):
        first = low_ref[pl.ds(z, 162, stride=8), :]
        second = rest_ref[pl.ds(z, 81, stride=8), :]
        out_ref[z] = jnp.concatenate([first, second, pad], axis=0).astype(BF16)


def input_grads(
    flag_ref,
    w_ref,
    recv_ref,
    share_ref,
    up_ref,
    low_ref,
    high_ref,
    scale_ref,
    fwd_out_ref,
    grad_ref,
    skip_ref,
    x_ref,
    w_here_ref,
    mix_ref,
    sems,
):
    fetch = pltpu.make_async_copy(w_ref, w_here_ref, sems.at[0])
    fetch.start()
    decoder = flag_ref[0] == 1
    total_cells = 2.0 * AREA * recv_ref.shape[0]
    masks = tap_masks()
    total = full_tile(jnp.sum(recv_ref[...], axis=0))
    sum_grad, sum_cross = (col / total_cells for col in columns(total, 0))
    scale = scale_ref[...]
    acts = [low_ref[0], share_ref[0], share_ref[2], high_ref[0]]
    norms = [low_ref[1], share_ref[1], share_ref[3], high_ref[1]]
    for q in range(4):
        grad_z = scale * (acts[q].astype(F32) - sum_grad - norms[q].astype(F32) * sum_cross)
        if q == 0:
            grad_z = jnp.where(flag_ref[2] == 1, grad_z, 0.0)
        if q == 3:
            grad_z = jnp.where(flag_ref[3] == 1, grad_z, 0.0)
        grad_z = grad_z.astype(BF16)
        for b in range(3):
            for c in range(3):
                view = shifted(grad_z, 2 - b, 2 - c, masks)
                for a in range(3):
                    j = q + a - 2
                    if 0 <= j < 2:
                        tap = 9 * a + 3 * b + c
                        x_ref[tap * 192 : (tap + 1) * 192, j * AREA : (j + 1) * AREA] = view
    fetch.wait()
    back = jnp.dot(w_here_ref[...], x_ref[...], preferred_element_type=F32)
    for j in range(2):
        mix_ref[pl.ds(j, 192, stride=2), :] = up_ref[j] + back[:, j * AREA : (j + 1) * AREA]
    grad = mix_ref[...]
    grad_ref[...] = grad.astype(BF16)
    skip_ref[...] = jnp.where(decoder, grad, fwd_out_ref[...].astype(F32)).astype(BF16)


def hand_over(one_ref, two_ref, three_ref, out_one_ref, out_two_ref, out_three_ref):
    out_one_ref[...] = one_ref[...]
    out_two_ref[...] = two_ref[...]
    out_three_ref[...] = three_ref[...]


def sum_rows(scale_out, recv_ref, out_ref, wide_ref):
    total = jnp.sum(recv_ref[...].astype(F32), axis=0) * scale_out
    rest = jnp.concatenate([total[162:243, :64], total[162:243, 64:]], axis=0)

    def block(tap):
        rows = slice(6 * tap, 6 * tap + 6)
        return [total[rows], rest[rows]]

    for tap in range(0, TAPS, 2):
        parts = block(tap) + (block(tap + 1) if tap + 1 < TAPS else [])
        width = 192 if tap + 1 == TAPS else 384
        wide_ref[0:6, tap * 192 : tap * 192 + width] = jnp.concatenate(parts, axis=1)
    for r in range(6):
        out_ref[r] = wide_ref[r : r + 1, :]


def pair_rows(one, two):
    rest = jnp.concatenate([one[:, 128:], two[:, 128:]], axis=1)
    return jnp.concatenate([one[:, :128], two[:, :128], rest], axis=0)


def moved(block, axis, distance):
    count = lax.axis_size(axis)
    route = [(i, (i + distance) % count) for i in range(count)]
    return lax.ppermute(block, axis, route)


def per_device(
    fwd_input,
    fwd_skip,
    bwd_input,
    bwd_skip,
    out_cot,
    skip_cot,
    kernel,
    norm_gain,
    norm_shift,
    head_weight,
    labels,
):
    segments = lax.axis_size("segment")
    slabs = lax.axis_size("y") * lax.axis_size("z")
    segment_id = lax.axis_index("segment")
    y_id = lax.axis_index("y")
    slab_id = y_id * lax.axis_size("z") + lax.axis_index("z")
    is_decoder = segment_id * 2 >= segments
    flags = jnp.stack(
        [
            is_decoder.astype(jnp.int32),
            (segment_id == segments - 1).astype(jnp.int32),
            (slab_id > 0).astype(jnp.int32),
            (slab_id < slabs - 1).astype(jnp.int32),
            y_id.astype(jnp.int32),
        ]
    )
    kernel_mat = kernel[0]
    affine = pair_rows(norm_gain, norm_shift)

    def by_plane(block):
        return jnp.swapaxes(block[0], 0, 1)

    def joined(block, skip):
        added = (block.astype(F32) + skip.astype(F32)).astype(BF16)
        return by_plane(jnp.where(is_decoder, added, block))

    own = jnp.concatenate([joined(bwd_input, bwd_skip), joined(fwd_input, fwd_skip)], axis=1)
    nothing = jnp.zeros_like(own[0])
    low = moved(jnp.where(slab_id < slabs - 1, own[1], nothing), SLABS, 1)
    high = moved(jnp.where(slab_id > 0, own[0], nothing), SLABS, -1)
    (turned,) = call(
        turn_weights,
        [((192, 5184), BF16)],
        [((192, 5184), BF16)],
        0,
        4 * 192 * 5184,
        kernel_mat,
        hbm=1,
        limit=52,
    )
    z, stats_send = call(
        conv_both,
        [((4, 192, AREA), F32), ((slabs, 6, AREA), F32)],
        [((5184, 512), BF16)],
        2 * 5184 * 192 * 512,
        5000000,
        own,
        low,
        high,
        turned,
    )
    stats = lax.all_to_all(stats_send, SLABS, 0, 0, tiled=True)
    out_cots = by_plane(out_cot)
    skip_cots = by_plane(skip_cot)
    upstream, *shares, scale, sums_send = call(
        head_and_sums,
        [
            ((2, 192, AREA), F32),
            *[((5, 192, AREA), BF16)] * 4,
            ((192, AREA), F32),
            ((slabs, 4, AREA), F32),
        ],
        HEAD_SCRATCH,
        4 * 192 * 105 * 512,
        4000000,
        flags,
        z,
        stats,
        own,
        low,
        high,
        out_cots,
        skip_cots,
        labels,
        affine,
        head_weight,
        head_weight.T,
        smem=1,
    )
    sums = lax.all_to_all(sums_send, SLABS, 0, 0, tiled=True)
    share = shares[0]
    shares = [share] + [moved(shares[d], "y", d) for d in (1, 2, 3)]
    fwd_out, rim_low, rim_high = call(
        forward_out,
        [((384, AREA), BF16), ((2, 192, AREA), BF16), ((2, 192, AREA), BF16)],
        [((384, AREA), F32)],
        0,
        1000000,
        stats,
        z,
        own,
        affine,
        share,
    )
    rim_low = moved(rim_low, SLABS, 1)
    rim_high = moved(rim_high, SLABS, -1)
    sums, fwd_out = lax.optimization_barrier((sums, fwd_out))
    parts, shift_grad, gain_grad = call(
        kernel_grads,
        [((8, 248, AREA), BF16), ((1, 192), F32), ((1, 192), F32)],
        [
            ((1296, 1024), BF16),
            ((192, 1024), BF16),
            ((1296, AREA), F32),
            ((648, AREA), F32),
            ((48, AREA), F32),
            ((48, AREA), F32),
        ],
        0,
        1000,
        sums,
        *shares,
        scale,
    )
    parts, rim_low, rim_high = lax.optimization_barrier((parts, rim_low, rim_high))
    summed = lax.all_to_all(parts, "z", 0, 0, tiled=True)
    grad_joined, outgoing = call(
        input_grads,
        [((384, AREA), BF16)] * 2,
        [((5184, 256), BF16), ((192, 5184), BF16), ((384, AREA), F32)],
        2 * 5184 * 192 * 256,
        4000000,
        flags,
        kernel_mat,
        sums,
        share,
        upstream,
        rim_low,
        rim_high,
        scale,
        fwd_out,
        smem=1,
        hbm=1,
        limit=52,
    )
    prev_block = moved(grad_joined, "segment", -1)
    next_block = moved(fwd_out, "segment", 1)
    mirrored = lax.ppermute(outgoing, "segment", [(i, segments - 1 - i) for i in range(segments)])
    total_cells = float(2 * slabs * AREA)

    def by_channel(block):
        return block.reshape(1, 192, 2, AREA)

    blocks = call(
        hand_over,
        [((384, AREA), BF16)] * 3,
        [],
        0,
        600000,
        next_block,
        prev_block,
        mirrored,
    )
    handed = [by_channel(block) for block in blocks]
    (kernel_grad,) = call(
        functools.partial(sum_rows, total_cells ** (-0.5)),
        [((6, 1, 5184), F32)],
        [((8, 5184), F32)],
        0,
        1000000,
        summed,
    )
    return (
        *handed,
        jnp.swapaxes(kernel_grad, 0, 1),
        gain_grad,
        shift_grad,
    )


def solution(mesh):
    grid = Mesh(mesh.devices.reshape(mesh.devices.shape[0], 4, 8), ("segment", "y", "z"))
    field = P("segment", None, SLABS, None)
    in_specs = (field,) * 6 + (
        P("segment", None, None),
        P("segment", None),
        P("segment", None),
        P(),
        P(SLABS, None),
    )
    out_specs = (
        field,
        field,
        field,
        P("segment", SLABS, None),
        P("segment", None),
        P("segment", None),
    )
    return jax.shard_map(
        per_device, mesh=grid, in_specs=in_specs, out_specs=out_specs, check_vma=False
    )
```
